32 devices in a mesh: row: 8 (over z, y), col: 4 (over x, core).
Axes of the slice: x: 2, y: 2, z: 4, core: 2. Of those that a mesh axis runs over, the one named last changes fastest.
Arguments:
- right_side: float32 [8, 4, 1024, 256], P('row', 'col'), may hold values from -4 to 4
- local_operator: bfloat16 [8, 4, 1536, 1536], P('row', 'col'), may hold values from -1 to 4
- local_inverse: bfloat16 [8, 4, 1536, 1536], P('row', 'col'), may hold values from -1 to 1
- coarse_basis: bfloat16 [8, 4, 1536, 32], P('row', 'col'), may hold values from -1 to 1
- coarse_inverse: bfloat16 [8, 128, 1024], P(None, 'col', 'row'), may hold values from -1 to 1
- send_rows: int32 [8, 4, 4, 128], P('row', 'col'), may hold values from 0 to 1023, as said below
- send_count: int32 [8, 4, 4], P('row', 'col'), may hold values from 0 to 128, as said below
Outputs:
- solution: float32 [8, 4, 1024, 256], P('row', 'col')
The draws below stay inside these ranges and needn't reach their ends.
Inputs may be any that keep to these rules, and one draw needn't show every extreme that they name: `send_rows`: within one subdomain and direction the entries are distinct owned rows; entries at or past that direction's count are ignored. `send_count`: 0 exactly where the neighbour in that direction lies outside the grid of subdomains; otherwise from 128 // 4 to 128, and 128 is reached.
All inputs are finite; a program needn't handle non-finite values.
Results may differ from the reference program's by a relative error of at most 0.023.
Values may be sent and summed in bfloat16 or wider, within the bound.
No kernel may reach another device: no remote copies, remote signals or barrier semaphores. Data moves between devices by JAX's collectives and lax.ppermute only.
A program may use at most 64 MiB of HBM per device.

```python
import jax
import jax.numpy as jnp
from jax import lax

OWN = 1024
TILE = 128
COARSE = 32
RHS = 256
ITERS = 3
LOCAL = 1536
COARSE_ALL = 1024
N_ROW = 8
N_COL = 4


def draw_right_side(key, part):
    values = jnp.clip(jax.random.normal(key, (N_ROW, N_COL, OWN, RHS), jnp.float32), -4.0, 4.0)
    return values.astype(jnp.float32)


def dominant_matrix(key, low, high, spread):
    first, second = jax.random.split(jax.random.fold_in(key, 11))
    noise = jnp.clip(jax.random.normal(first, (N_ROW, N_COL, LOCAL, LOCAL), jnp.float32), -4.0, 4.0)
    diagonal = jnp.exp(jax.random.uniform(second, (N_ROW, N_COL, LOCAL), jnp.float32, jnp.log(low), jnp.log(high)))
    index_rows = lax.broadcasted_iota(jnp.int32, (LOCAL, LOCAL), 0)
    index_cols = lax.broadcasted_iota(jnp.int32, (LOCAL, LOCAL), 1)
    identity = (index_rows == index_cols).astype(jnp.float32)
    return noise * (spread / jnp.sqrt(1.0 * LOCAL)) + identity * diagonal[..., None]


def draw_local_operator(key, part):
    return dominant_matrix(key, 1.0, 3.0, 0.6).astype(jnp.bfloat16)


def draw_local_inverse(key, part):
    return dominant_matrix(jax.random.fold_in(key, 5), 0.3, 0.8, 0.3).astype(jnp.bfloat16)


def draw_coarse_basis(key, part):
    values = jnp.clip(jax.random.normal(jax.random.fold_in(key, 7), (N_ROW, N_COL, LOCAL, COARSE), jnp.float32), -4.0, 4.0)
    return (values * (1.0 * LOCAL * COARSE) ** (-0.25)).astype(jnp.bfloat16)


def draw_coarse_inverse(key, part):
    shape = (N_ROW, N_COL * COARSE, COARSE_ALL)
    noise = jnp.clip(jax.random.normal(jax.random.fold_in(key, 9), shape, jnp.float32), -4.0, 4.0)
    major = lax.broadcasted_iota(jnp.int32, shape, 0)
    minor = lax.broadcasted_iota(jnp.int32, shape, 1)
    column = lax.broadcasted_iota(jnp.int32, shape, 2)
    identity = (major * (N_COL * COARSE) + minor == column).astype(jnp.float32)
    return (noise / jnp.sqrt(1.0 * COARSE_ALL) + 0.3 * identity).astype(jnp.bfloat16)


def draw_send_rows(key, part):
    keys = jax.random.split(jax.random.fold_in(key, 13), N_ROW * N_COL * 4)
    chosen = jax.vmap(lambda single: jax.random.permutation(single, OWN)[:TILE])(keys)
    return chosen.reshape(N_ROW, N_COL, 4, TILE).astype(jnp.int32)


def draw_send_count(key, part):
    drawn = jax.random.randint(jax.random.fold_in(key, 17), (N_ROW, N_COL, 4), TILE // 4, TILE + 1).astype(jnp.int32)
    major = lax.broadcasted_iota(jnp.int32, (N_ROW, N_COL, 4), 0)
    minor = lax.broadcasted_iota(jnp.int32, (N_ROW, N_COL, 4), 1)
    direction = lax.broadcasted_iota(jnp.int32, (N_ROW, N_COL, 4), 2)
    outside = (direction == 0) & (major == 0) | (direction == 1) & (major == N_ROW - 1)
    outside = outside | (direction == 2) & (minor == 0) | (direction == 3) & (minor == N_COL - 1)
    forced = (direction == 1) & (major == 0) & (minor == 0)
    drawn = jnp.where(forced, TILE, drawn)
    return jnp.where(outside, 0, drawn).astype(jnp.int32)


def setup_inputs(seed: int = 0) -> dict:
    key_list = jax.random.split(jax.random.key(seed), 8)
    right_side = draw_right_side(jax.random.fold_in(key_list[7], 71), 0)
    local_operator = draw_local_operator(jax.random.fold_in(key_list[7], 71), 0)
    local_inverse = draw_local_inverse(jax.random.fold_in(key_list[7], 71), 0)
    coarse_basis = draw_coarse_basis(jax.random.fold_in(key_list[7], 71), 0)
    coarse_inverse = draw_coarse_inverse(jax.random.fold_in(key_list[7], 71), 0)
    send_rows = draw_send_rows(jax.random.fold_in(key_list[7], 71), 0)
    send_count = draw_send_count(jax.random.fold_in(key_list[7], 71), 0)
    return dict(right_side=right_side, local_operator=local_operator, local_inverse=local_inverse, coarse_basis=coarse_basis, coarse_inverse=coarse_inverse, send_rows=send_rows, send_count=send_count)


DAMPING = 0.5


def pack_tiles(values_half, send_rows, live_mask):
    picked = jax.vmap(jax.vmap(lambda rows_all, index_rows: rows_all[index_rows]))(values_half, send_rows)
    return picked * live_mask[..., None].astype(jnp.bfloat16)


def ghost_trade(buffer):
    zero_row = jnp.zeros_like(buffer[:1, :, 0])
    zero_col = jnp.zeros_like(buffer[:, :1, 0])
    from_lower_row = jnp.concatenate([zero_row, buffer[:-1, :, 1]], axis=0)
    from_upper_row = jnp.concatenate([buffer[1:, :, 0], zero_row], axis=0)
    from_lower_col = jnp.concatenate([zero_col, buffer[:, :-1, 3]], axis=1)
    from_upper_col = jnp.concatenate([buffer[:, 1:, 2], zero_col], axis=1)
    return jnp.stack([from_lower_row, from_upper_row, from_lower_col, from_upper_col], axis=2)


def with_ghosts(values_half, send_rows, live_mask):
    ghosts = ghost_trade(pack_tiles(values_half, send_rows, live_mask))
    dims = ghosts.shape
    flat_ghosts = ghosts.reshape(dims[0], dims[1], dims[2] * dims[3], dims[4])
    return jnp.concatenate([values_half, flat_ghosts], axis=2)


def scatter_one(terms, index_rows):
    width = terms.shape[-1]
    empty = jnp.zeros((OWN, width), jnp.float32)
    return empty.at[index_rows.reshape(-1)].add(terms.reshape(-1, width))


def owner_sum(local_terms, send_rows, live_mask):
    width = local_terms.shape[-1]
    rim_half = local_terms[:, :, OWN:].astype(jnp.bfloat16).reshape(N_ROW, N_COL, 4, TILE, width)
    returned = ghost_trade(rim_half)
    weighted = returned.astype(jnp.float32) * live_mask[..., None]
    summed = jax.vmap(jax.vmap(scatter_one))(weighted, send_rows)
    return local_terms[:, :, :OWN] + summed


def device_dot(left, right):
    flat_left = left.reshape((-1,) + left.shape[2:])
    flat_right = right.reshape((-1,) + right.shape[2:])
    products = lax.map(lambda pair: jnp.dot(pair[0], pair[1], preferred_element_type=jnp.float32), (flat_left, flat_right))
    return products.reshape(left.shape[:2] + products.shape[1:])


def reference(right_side, local_operator, local_inverse, coarse_basis, coarse_inverse, send_rows, send_count):
    positions = jnp.arange(TILE, dtype=jnp.int32)
    live_mask = (positions[None, None, None, :] < send_count[..., None]).astype(jnp.float32)
    inverse_whole = coarse_inverse.reshape(COARSE_ALL, COARSE_ALL)
    basis_turned = jnp.swapaxes(coarse_basis, 2, 3)
    solution = jnp.zeros(right_side.shape, jnp.float32)
    for sweep in range(ITERS):
        solution_half = solution.astype(jnp.bfloat16)
        image = owner_sum(device_dot(local_operator, with_ghosts(solution_half, send_rows, live_mask)), send_rows, live_mask)
        residual_half = (right_side - image).astype(jnp.bfloat16)
        residual_local = with_ghosts(residual_half, send_rows, live_mask)
        local_part = device_dot(local_inverse, residual_local)
        restricted = device_dot(basis_turned, residual_local).astype(jnp.bfloat16)
        coarse_level = jnp.dot(inverse_whole, restricted.reshape(COARSE_ALL, -1), preferred_element_type=jnp.float32).astype(jnp.bfloat16)
        coarse_level = coarse_level.reshape(N_ROW, N_COL, COARSE, -1)
        update = owner_sum(local_part + device_dot(coarse_basis, coarse_level), send_rows, live_mask)
        solution = solution + DAMPING * update
    return solution
```

```python
import jax
import jax.numpy as jnp
from jax import lax
from jax.experimental import pallas as pl
from jax.experimental.pallas import tpu as pltpu
from jax.sharding import PartitionSpec as P

ITERS = 3
DAMPING = 0.5
HALF = jnp.bfloat16
FULL = jnp.float32


def product(left, right):
    return jnp.dot(left, right, preferred_element_type=FULL)


def turned_product(left, right):
    return lax.dot_general(left, right, (((0,), (0,)), ((), ())), preferred_element_type=FULL)


def call(body, name, outs, *args, flops=0):
    here = pl.BlockSpec(memory_space=pltpu.VMEM)
    size = sum(a.size * a.dtype.itemsize for a in args)
    return pl.pallas_call(
        body,
        out_shape=tuple(pltpu.VMEM(shape, dtype) for shape, dtype in outs),
        in_specs=[here] * len(args),
        out_specs=tuple(here for _ in outs),
        compiler_params=pltpu.CompilerParams(vmem_limit_bytes=24 * 1024 * 1024),
        cost_estimate=pl.CostEstimate(flops=flops, bytes_accessed=size, transcendentals=0),
        name=name,
    )(*(pltpu.with_memory_space_constraint(a, pltpu.VMEM) for a in args))


def select_kernel(target, rows, counts, half, pick, spread, *tiles):
    own = target.shape[0]
    tile = rows.shape[1]
    half[...] = target[...].astype(HALF)
    for d in range(4):
        here = jnp.where(
            lax.broadcasted_iota(jnp.int32, (1, tile), 1) < counts[d : d + 1, :],
            rows[d : d + 1, :],
            -1,
        )
        wide = jnp.broadcast_to(here, (own, tile))
        spread[:, d * tile : (d + 1) * tile] = (
            lax.broadcasted_iota(jnp.int32, (own, tile), 0) == wide
        ).astype(FULL).astype(HALF)
        down = jnp.transpose(jnp.broadcast_to(here, (tile, tile)))[:, :1]
        pick[d * tile : (d + 1) * tile, :] = (
            lax.broadcasted_iota(jnp.int32, (tile, own), 1) == down
        ).astype(FULL).astype(HALF)
    for d in range(4):
        tiles[d][...] = product(pick[d * tile : (d + 1) * tile, :], half[...]).astype(HALF)


def own_columns_kernel(matrix, owned, out):
    own = owned.shape[0]
    out[...] = product(matrix[:, :own], owned[...])


def restrict_kernel(basis, owned, g0, g1, g2, g3, out):
    own, tile = owned.shape[0], g0.shape[0]
    total = turned_product(basis[:own, :], owned[...])
    for d, ghost in enumerate((g0, g1, g2, g3)):
        total += turned_product(basis[own + d * tile : own + (d + 1) * tile, :], ghost[...])
    out[...] = total.astype(HALF)


def stacked(g0, g1, g2, g3):
    return jnp.concatenate([g0[...], g1[...], g2[...], g3[...]], axis=0)


def margin_columns_kernel(matrix, partial, g0, g1, g2, g3, out):
    own = matrix.shape[1] - 4 * g0.shape[0]
    out[...] = partial[...] + product(matrix[:, own:], stacked(g0, g1, g2, g3))


def coarse_kernel(coarse_rows, gathered, basis, local, level, *tiles):
    tile = tiles[0].shape[0]
    own = local.shape[0] - 4 * tile
    level[...] = product(coarse_rows[...], gathered[...]).astype(HALF)
    for d in range(4):
        at = slice(own + d * tile, own + (d + 1) * tile)
        tiles[d][...] = (local[at, :] + product(basis[at, :], level[...])).astype(HALF)


def rim_kernel(matrix, partial, g0, g1, g2, g3, *tiles):
    tile = g0.shape[0]
    own = matrix.shape[1] - 4 * tile
    ghosts = stacked(g0, g1, g2, g3)
    for d in range(4):
        at = slice(own + d * tile, own + (d + 1) * tile)
        tiles[d][...] = (partial[at, :] + product(matrix[at, own:], ghosts)).astype(HALF)


def inner_kernel(matrix, partial, g0, g1, g2, g3, out):
    own = matrix.shape[1] - 4 * g0.shape[0]
    out[...] = partial[:own, :] + product(matrix[:own, own:], stacked(g0, g1, g2, g3))


def update_kernel(first, last):
    def body(*refs):
        refs = list(refs)
        before = None if first else refs.pop(0)
        local, level, basis, pick, spread, r0, r1, r2, r3, after, *rest = refs
        own = after.shape[0]
        update = (
            local[:own, :]
            + product(basis[:own, :], level[...])
            + product(spread[...], stacked(r0, r1, r2, r3))
        )
        after[...] = DAMPING * update if first else before[...] + DAMPING * update
        if last:
            return
        half, *tiles = rest
        tile = tiles[0].shape[0]
        half[...] = after[...].astype(HALF)
        for d in range(4):
            tiles[d][...] = product(pick[d * tile : (d + 1) * tile, :], half[...]).astype(HALF)

    return body


def residual_kernel(target, image, pick, spread, r0, r1, r2, r3, half, *tiles):
    tile = tiles[0].shape[0]
    half[...] = (
        target[...] - (image[...] + product(spread[...], stacked(r0, r1, r2, r3)))
    ).astype(HALF)
    for d in range(4):
        tiles[d][...] = product(pick[d * tile : (d + 1) * tile, :], half[...]).astype(HALF)


def passed_along(shard, axis, by):
    devices = lax.axis_size(axis)
    pairs = [(i, i + by) for i in range(devices) if 0 <= i + by < devices]
    return lax.ppermute(shard, axis, pairs)


def traded(tiles):
    return (
        passed_along(tiles[1], "row", 1),
        passed_along(tiles[0], "row", -1),
        passed_along(tiles[3], "col", 1),
        passed_along(tiles[2], "col", -1),
    )


def per_device(
    right_side, local_operator, local_inverse, coarse_basis, coarse_inverse, send_rows, send_count
):
    target = right_side[0, 0]
    operator = local_operator[0, 0]
    inverse = local_inverse[0, 0]
    basis = coarse_basis[0, 0]
    rows_list = send_rows[0, 0]
    own, columns = target.shape
    local = operator.shape[0]
    tile = rows_list.shape[1]
    margin = 4 * tile
    coarse = basis.shape[1]
    counts = jnp.broadcast_to(send_count[0, 0][:, None], rows_list.shape)
    coarse_rows = lax.all_to_all(coarse_inverse, "row", 0, 2, tiled=True)[0]

    four_tiles = [((tile, columns), HALF)] * 4
    owned_half = ((own, columns), HALF)
    residual, pick, spread, *tiles = call(
        select_kernel,
        "select",
        [owned_half, ((margin, own), HALF), ((own, margin), HALF)] + four_tiles,
        target,
        rows_list,
        counts,
        flops=2 * margin * own * columns,
    )
    solution = None
    for sweep in range(ITERS):
        if sweep:
            ghosts = traded(tiles)
            (partial,) = call(
                own_columns_kernel,
                "operator_own",
                [((local, columns), FULL)],
                operator,
                solution_half,
                flops=2 * local * own * columns,
            )
            tiles = call(
                rim_kernel,
                "operator_rim",
                four_tiles,
                operator,
                partial,
                *ghosts,
                flops=2 * margin * margin * columns,
            )
            returned = traded(tiles)
            (image,) = call(
                inner_kernel,
                "operator_inner",
                [((own, columns), FULL)],
                operator,
                partial,
                *ghosts,
                flops=2 * own * margin * columns,
            )
            residual, *tiles = call(
                residual_kernel,
                "residual",
                [owned_half] + four_tiles,
                target,
                image,
                pick,
                spread,
                *returned,
                flops=4 * margin * own * columns,
            )
        ghosts = traded(tiles)
        (partial,) = call(
            own_columns_kernel,
            "inverse_own",
            [((local, columns), FULL)],
            inverse,
            residual,
            flops=2 * local * own * columns,
        )
        (restricted,) = call(
            restrict_kernel,
            "restrict",
            [((coarse, columns), HALF)],
            basis,
            residual,
            *ghosts,
            flops=2 * local * coarse * columns,
        )
        gathered = lax.all_gather(restricted, ("row", "col"), axis=0, tiled=True)
        (correction,) = call(
            margin_columns_kernel,
            "inverse_margin",
            [((local, columns), FULL)],
            inverse,
            partial,
            *ghosts,
            flops=2 * local * margin * columns,
        )
        level, *tiles = call(
            coarse_kernel,
            "coarse",
            [((coarse, columns), HALF)] + four_tiles,
            coarse_rows,
            gathered,
            basis,
            correction,
            flops=2 * coarse * (coarse_rows.shape[1] + margin) * columns,
        )
        returned = traded(tiles)
        first, last = sweep == 0, sweep == ITERS - 1
        before = [] if first else [solution]
        outs = [((own, columns), FULL)] + ([] if last else [owned_half] + four_tiles)
        solution, *rest = call(
            update_kernel(first, last),
            "update",
            outs,
            *before,
            correction,
            level,
            basis,
            pick,
            spread,
            *returned,
            flops=4 * margin * own * columns,
        )
        if not last:
            solution_half, *tiles = rest
    return solution[None, None]


def solution(mesh):
    return jax.shard_map(
        per_device,
        mesh=mesh,
        in_specs=(
            P("row", "col", None, None),
            P("row", "col", None, None),
            P("row", "col", None, None),
            P("row", "col", None, None),
            P(None, "col", "row"),
            P("row", "col", None, None),
            P("row", "col", None),
        ),
        out_specs=P("row", "col", None, None),
        check_vma=False,
    )
```

```python
import jax
import jax.numpy as jnp
from jax import lax
from jax.experimental import pallas as pl
from jax.experimental.pallas import tpu as pltpu
from jax.sharding import PartitionSpec as P

ITERS = 3
DAMPING = 0.5
HALF = jnp.bfloat16
FULL = jnp.float32


def product(left, right):
    return jnp.dot(left, right, preferred_element_type=FULL)


def turned_product(left, right):
    return lax.dot_general(left, right, (((0,), (0,)), ((), ())), preferred_element_type=FULL)


def call(body, name, outs, *args, far=0, away=False, scratch=(), flops=0):
    here = pl.BlockSpec(memory_space=pltpu.VMEM)
    there = pl.BlockSpec(memory_space=pltpu.HBM)
    size = sum(a.size * a.dtype.itemsize for a in args)
    distant = [pltpu.with_memory_space_constraint(a, pltpu.HBM) for a in args[:far]]
    near = [pltpu.with_memory_space_constraint(a, pltpu.VMEM) for a in args[far:]]
    return pl.pallas_call(
        body,
        out_shape=tuple((pltpu.HBM if away else pltpu.VMEM)(*out) for out in outs),
        in_specs=[there] * far + [here] * len(near),
        out_specs=tuple(there if away else here for _ in outs),
        scratch_shapes=list(scratch),
        compiler_params=pltpu.CompilerParams(vmem_limit_bytes=24 * 1024 * 1024),
        cost_estimate=pl.CostEstimate(flops=flops, bytes_accessed=size, transcendentals=0),
        name=name,
    )(*distant, *near)


def select_kernel(far_target, far_rows, far_counts, target, half, pick, spread, *rest):
    *tiles, rows, counts, sems = rest
    own = target.shape[0]
    tile = rows.shape[1]
    loads = [
        pltpu.make_async_copy(far, near, sems.at[i])
        for i, (far, near) in enumerate(((far_rows, rows), (far_counts, counts), (far_target, target)))
    ]
    for load in loads:
        load.start()
    loads[0].wait()
    loads[1].wait()
    for d in range(4):
        here = jnp.where(
            lax.broadcasted_iota(jnp.int32, (1, tile), 1) < counts[0, d], rows[d : d + 1, :], -1
        )
        wide = jnp.broadcast_to(here, (own, tile))
        spread[:, d * tile : (d + 1) * tile] = (
            lax.broadcasted_iota(jnp.int32, (own, tile), 0) == wide
        ).astype(FULL).astype(HALF)
        down = jnp.transpose(jnp.broadcast_to(here, (tile, tile)))[:, :1]
        pick[d * tile : (d + 1) * tile, :] = (
            lax.broadcasted_iota(jnp.int32, (tile, own), 1) == down
        ).astype(FULL).astype(HALF)
    loads[2].wait()
    half[...] = target[...].astype(HALF)
    for d in range(4):
        tiles[d][...] = product(pick[d * tile : (d + 1) * tile, :], half[...]).astype(HALF)


def resident_kernel(far, owned, matrix, out, sems):
    own = owned.shape[0]
    pieces = sems.shape[0]
    height = far.shape[0] // pieces
    spans = [slice(i * height, (i + 1) * height) for i in range(pieces)]
    loads = [
        pltpu.make_async_copy(far.at[at], matrix.at[at], sems.at[i]) for i, at in enumerate(spans)
    ]
    for load in loads:
        load.start()
    for load, at in zip(loads, spans):
        load.wait()
        out[at, :] = product(matrix[at, :own], owned[...])


def own_columns_kernel(matrix, owned, out):
    own = owned.shape[0]
    out[...] = product(matrix[:, :own], owned[...])


def restrict_kernel(basis, owned, g0, g1, g2, g3, out):
    own, tile = owned.shape[0], g0.shape[0]
    total = product(basis[:, :own], owned[...])
    for d, ghost in enumerate((g0, g1, g2, g3)):
        total += product(basis[:, own + d * tile : own + (d + 1) * tile], ghost[...])
    out[...] = total.astype(HALF)


def stacked(g0, g1, g2, g3):
    return jnp.concatenate([g0[...], g1[...], g2[...], g3[...]], axis=0)


def margin_columns_kernel(matrix, partial, g0, g1, g2, g3, out):
    own = matrix.shape[1] - 4 * g0.shape[0]
    out[...] = partial[...] + product(matrix[:, own:], stacked(g0, g1, g2, g3))


def partial_kernel(inverse, gathered, out):
    for i in range(inverse.shape[0]):
        out[i, :, :] = product(inverse[i, :, :], gathered[...]).astype(HALF)


def coarse_kernel(parts, basis, local, level, *tiles):
    tile = tiles[0].shape[0]
    own = local.shape[0] - 4 * tile
    total = parts[0, :, :].astype(FULL)
    for i in range(1, parts.shape[0]):
        total += parts[i, :, :].astype(FULL)
    level[...] = total.astype(HALF)
    for d in range(4):
        at = slice(own + d * tile, own + (d + 1) * tile)
        tiles[d][...] = (local[at, :] + turned_product(basis[:, at], level[...])).astype(HALF)


def rim_kernel(matrix, partial, g0, g1, g2, g3, *tiles):
    tile = g0.shape[0]
    own = matrix.shape[1] - 4 * tile
    ghosts = stacked(g0, g1, g2, g3)
    for d in range(4):
        at = slice(own + d * tile, own + (d + 1) * tile)
        tiles[d][...] = (partial[at, :] + product(matrix[at, own:], ghosts)).astype(HALF)


def inner_kernel(matrix, partial, g0, g1, g2, g3, out):
    own = matrix.shape[1] - 4 * g0.shape[0]
    out[...] = partial[:own, :] + product(matrix[:own, own:], stacked(g0, g1, g2, g3))


def update_kernel(first):
    def body(*refs):
        refs = list(refs)
        before = None if first else refs.pop(0)
        local, level, basis, pick, spread, r0, r1, r2, r3, after, half, *tiles = refs
        own = after.shape[0]
        update = (
            local[:own, :]
            + turned_product(basis[:, :own], level[...])
            + product(spread[...], stacked(r0, r1, r2, r3))
        )
        after[...] = DAMPING * update if first else before[...] + DAMPING * update
        tile = tiles[0].shape[0]
        half[...] = after[...].astype(HALF)
        for d in range(4):
            tiles[d][...] = product(pick[d * tile : (d + 1) * tile, :], half[...]).astype(HALF)

    return body


def last_update_kernel(before, local, level, basis, spread, r0, r1, r2, r3, far, after, sems):
    pieces = sems.shape[0]
    height = after.shape[0] // pieces
    returned = stacked(r0, r1, r2, r3)
    stores = []
    for i in range(pieces):
        at = slice(i * height, (i + 1) * height)
        update = (
            local[at, :]
            + turned_product(basis[:, at], level[...])
            + product(spread[at, :], returned)
        )
        after[at, :] = before[at, :] + DAMPING * update
        stores.append(pltpu.make_async_copy(after.at[at], far.at[at], sems.at[i]))
        stores[-1].start()
    for store in stores:
        store.wait()


def residual_kernel(target, image, pick, spread, r0, r1, r2, r3, half, *tiles):
    tile = tiles[0].shape[0]
    half[...] = (
        target[...] - (image[...] + product(spread[...], stacked(r0, r1, r2, r3)))
    ).astype(HALF)
    for d in range(4):
        tiles[d][...] = product(pick[d * tile : (d + 1) * tile, :], half[...]).astype(HALF)


def own_product(matrix, owned, arriving, name):
    local = matrix.shape[0]
    out = ((local, owned.shape[1]), FULL)
    flops = 2 * local * owned.size
    if arriving:
        return call(
            resident_kernel,
            name,
            [(matrix.shape, HALF), out],
            matrix,
            owned,
            far=1,
            scratch=(pltpu.SemaphoreType.DMA((6,)),),
            flops=flops,
        )
    return matrix, call(own_columns_kernel, name, [out], matrix, owned, flops=flops)[0]


def passed_along(shard, axis, by):
    devices = lax.axis_size(axis)
    pairs = [(i, i + by) for i in range(devices) if 0 <= i + by < devices]
    return lax.ppermute(shard, axis, pairs)


def traded(tiles):
    return (
        passed_along(tiles[1], "row", 1),
        passed_along(tiles[0], "row", -1),
        passed_along(tiles[3], "col", 1),
        passed_along(tiles[2], "col", -1),
    )


def per_device(
    right_side, local_operator, local_inverse, coarse_basis, coarse_inverse, send_rows, send_count
):
    target = right_side[0, 0]
    operator = local_operator[0, 0]
    inverse = local_inverse[0, 0]
    basis = jnp.swapaxes(coarse_basis[0, 0], 0, 1)
    rows_list = send_rows[0, 0]
    own, columns = target.shape
    local = operator.shape[0]
    tile = rows_list.shape[1]
    margin = 4 * tile
    coarse = basis.shape[0]
    groups = coarse_inverse.shape[0]
    four_tiles = [((tile, columns), HALF)] * 4
    owned_half = ((own, columns), HALF)
    target, residual, pick, spread, *tiles = call(
        select_kernel,
        "select",
        [((own, columns), FULL), owned_half, ((margin, own), HALF), ((own, margin), HALF)]
        + four_tiles,
        target,
        rows_list,
        send_count[0],
        far=3,
        scratch=(
            pltpu.VMEM(rows_list.shape, jnp.int32),
            pltpu.SMEM((1, 4), jnp.int32),
            pltpu.SemaphoreType.DMA((3,)),
        ),
        flops=2 * margin * own * columns,
    )
    solution = None
    for sweep in range(ITERS):
        if sweep:
            ghosts = traded(tiles)
            operator, partial = own_product(operator, solution_half, sweep == 1, "operator_own")
            tiles = call(
                rim_kernel,
                "operator_rim",
                four_tiles,
                operator,
                partial,
                *ghosts,
                flops=2 * margin * margin * columns,
            )
            returned = traded(tiles)
            (image,) = call(
                inner_kernel,
                "operator_inner",
                [((own, columns), FULL)],
                operator,
                partial,
                *ghosts,
                flops=2 * own * margin * columns,
            )
            residual, *tiles = call(
                residual_kernel,
                "residual",
                [owned_half] + four_tiles,
                target,
                image,
                pick,
                spread,
                *returned,
                flops=4 * margin * own * columns,
            )
        ghosts = traded(tiles)
        inverse, partial = own_product(inverse, residual, sweep == 0, "inverse_own")
        (restricted,) = call(
            restrict_kernel,
            "restrict",
            [((coarse, columns), HALF)],
            basis,
            residual,
            *ghosts,
            flops=2 * local * coarse * columns,
        )
        gathered = lax.all_gather(restricted, "col", axis=0, tiled=True)
        (parts,) = call(
            partial_kernel,
            "coarse_part",
            [((groups, coarse, columns), HALF)],
            coarse_inverse,
            gathered,
            flops=2 * coarse_inverse.size * columns,
        )
        parts = lax.all_to_all(parts, "row", 0, 0, tiled=True)
        (correction,) = call(
            margin_columns_kernel,
            "inverse_margin",
            [((local, columns), FULL)],
            inverse,
            partial,
            *ghosts,
            flops=2 * local * margin * columns,
        )
        level, *tiles = call(
            coarse_kernel,
            "coarse",
            [((coarse, columns), HALF)] + four_tiles,
            parts,
            basis,
            correction,
            flops=2 * coarse * margin * columns,
        )
        returned = traded(tiles)
        if sweep == ITERS - 1:
            break
        before = [solution] if sweep else []
        solution, solution_half, *tiles = call(
            update_kernel(not sweep),
            "update",
            [((own, columns), FULL), owned_half] + four_tiles,
            *before,
            correction,
            level,
            basis,
            pick,
            spread,
            *returned,
            flops=4 * margin * own * columns,
        )
    (solution,) = call(
        last_update_kernel,
        "last_update",
        [((own, columns), FULL)],
        solution,
        correction,
        level,
        basis,
        spread,
        *returned,
        away=True,
        scratch=(pltpu.VMEM((own, columns), FULL), pltpu.SemaphoreType.DMA((4,))),
        flops=2 * margin * own * columns,
    )
    return solution[None, None]


def solution(mesh):
    return jax.shard_map(
        per_device,
        mesh=mesh,
        in_specs=(
            P("row", "col", None, None),
            P("row", "col", None, None),
            P("row", "col", None, None),
            P("row", "col", None, None),
            P(None, "col", "row"),
            P("row", "col", None, None),
            P("row", "col", None),
        ),
        out_specs=P("row", "col", None, None),
        check_vma=False,
    )
```

```python
import jax
import jax.numpy as jnp
from jax import lax
from jax.experimental import pallas as pl
from jax.experimental.pallas import tpu as pltpu
from jax.sharding import PartitionSpec as P

ITERS = 3
DAMPING = 0.5
HALF = jnp.bfloat16
FULL = jnp.float32


def product(left, right):
    return jnp.dot(left, right, preferred_element_type=FULL)


def turned_product(left, right):
    return lax.dot_general(left, right, (((0,), (0,)), ((), ())), preferred_element_type=FULL)


def call(body, name, outs, *args, far=0, away=False, scratch=(), flops=0):
    here = pl.BlockSpec(memory_space=pltpu.VMEM)
    there = pl.BlockSpec(memory_space=pltpu.HBM)
    size = sum(a.size * a.dtype.itemsize for a in args)
    distant = [pltpu.with_memory_space_constraint(a, pltpu.HBM) for a in args[:far]]
    near = [pltpu.with_memory_space_constraint(a, pltpu.VMEM) for a in args[far:]]
    return pl.pallas_call(
        body,
        out_shape=tuple((pltpu.HBM if away else pltpu.VMEM)(*out) for out in outs),
        in_specs=[there] * far + [here] * len(near),
        out_specs=tuple(there if away else here for _ in outs),
        scratch_shapes=list(scratch),
        compiler_params=pltpu.CompilerParams(vmem_limit_bytes=24 * 1024 * 1024),
        cost_estimate=pl.CostEstimate(flops=flops, bytes_accessed=size, transcendentals=0),
        name=name,
    )(*distant, *near)


def select_kernel(far_target, far_rows, far_counts, target, half, pick, spread, *rest):
    *tiles, rows, counts, sems = rest
    own = target.shape[0]
    tile = rows.shape[1]
    loads = [
        pltpu.make_async_copy(far, near, sems.at[i])
        for i, (far, near) in enumerate(((far_rows, rows), (far_counts, counts), (far_target, target)))
    ]
    for load in loads:
        load.start()
    loads[0].wait()
    loads[1].wait()
    for d in range(4):
        here = jnp.where(
            lax.broadcasted_iota(jnp.int32, (1, tile), 1) < counts[0, d], rows[d : d + 1, :], -1
        )
        wide = jnp.broadcast_to(here, (own, tile))
        spread[:, d * tile : (d + 1) * tile] = (
            lax.broadcasted_iota(jnp.int32, (own, tile), 0) == wide
        ).astype(FULL).astype(HALF)
        down = jnp.transpose(jnp.broadcast_to(here, (tile, tile)))[:, :1]
        pick[d * tile : (d + 1) * tile, :] = (
            lax.broadcasted_iota(jnp.int32, (tile, own), 1) == down
        ).astype(FULL).astype(HALF)
    loads[2].wait()
    half[...] = target[...].astype(HALF)
    for d in range(4):
        tiles[d][...] = product(pick[d * tile : (d + 1) * tile, :], half[...]).astype(HALF)


def resident_kernel(far, owned, matrix, out, sems):
    own = owned.shape[0]
    pieces = sems.shape[0]
    height = far.shape[0] // pieces
    spans = [slice(i * height, (i + 1) * height) for i in range(pieces)]
    loads = [
        pltpu.make_async_copy(far.at[at], matrix.at[at], sems.at[i]) for i, at in enumerate(spans)
    ]
    for load in loads:
        load.start()
    for load, at in zip(loads, spans):
        load.wait()
        out[at, :] = product(matrix[at, :own], owned[...])


def own_columns_kernel(matrix, owned, out):
    own = owned.shape[0]
    out[...] = product(matrix[:, :own], owned[...])


def restrict_kernel(basis, owned, g0, g1, g2, g3, out):
    own, tile = owned.shape[0], g0.shape[0]
    total = product(basis[:, :own], owned[...])
    for d, ghost in enumerate((g0, g1, g2, g3)):
        total += product(basis[:, own + d * tile : own + (d + 1) * tile], ghost[...])
    out[...] = total.astype(HALF)


def stacked(g0, g1, g2, g3):
    return jnp.concatenate([g0[...], g1[...], g2[...], g3[...]], axis=0)


def margin_columns_kernel(matrix, partial, g0, g1, g2, g3, out):
    own = matrix.shape[1] - 4 * g0.shape[0]
    out[...] = partial[...] + product(matrix[:, own:], stacked(g0, g1, g2, g3))


def coarse_kernel(coarse_rows, gathered, basis, local, level, *tiles):
    tile = tiles[0].shape[0]
    own = local.shape[0] - 4 * tile
    width = coarse_rows.shape[2]
    total = product(coarse_rows[0, :, :], gathered[:width, :])
    for i in range(1, coarse_rows.shape[0]):
        total += product(coarse_rows[i, :, :], gathered[i * width : (i + 1) * width, :])
    level[...] = total.astype(HALF)
    for d in range(4):
        at = slice(own + d * tile, own + (d + 1) * tile)
        tiles[d][...] = (local[at, :] + turned_product(basis[:, at], level[...])).astype(HALF)


def rim_kernel(matrix, partial, g0, g1, g2, g3, *tiles):
    tile = g0.shape[0]
    own = matrix.shape[1] - 4 * tile
    ghosts = stacked(g0, g1, g2, g3)
    for d in range(4):
        at = slice(own + d * tile, own + (d + 1) * tile)
        tiles[d][...] = (partial[at, :] + product(matrix[at, own:], ghosts)).astype(HALF)


def inner_kernel(matrix, partial, g0, g1, g2, g3, out):
    own = matrix.shape[1] - 4 * g0.shape[0]
    out[...] = partial[:own, :] + product(matrix[:own, own:], stacked(g0, g1, g2, g3))


def update_kernel(first):
    def body(*refs):
        refs = list(refs)
        before = None if first else refs.pop(0)
        local, level, basis, pick, spread, r0, r1, r2, r3, after, half, *tiles = refs
        own = after.shape[0]
        update = (
            local[:own, :]
            + turned_product(basis[:, :own], level[...])
            + product(spread[...], stacked(r0, r1, r2, r3))
        )
        after[...] = DAMPING * update if first else before[...] + DAMPING * update
        tile = tiles[0].shape[0]
        half[...] = after[...].astype(HALF)
        for d in range(4):
            tiles[d][...] = product(pick[d * tile : (d + 1) * tile, :], half[...]).astype(HALF)

    return body


def last_update_kernel(before, local, level, basis, spread, r0, r1, r2, r3, far, after, sems):
    pieces = sems.shape[0]
    height = after.shape[0] // pieces
    returned = stacked(r0, r1, r2, r3)
    stores = []
    for i in range(pieces):
        at = slice(i * height, (i + 1) * height)
        update = (
            local[at, :]
            + turned_product(basis[:, at], level[...])
            + product(spread[at, :], returned)
        )
        after[at, :] = before[at, :] + DAMPING * update
        stores.append(pltpu.make_async_copy(after.at[at], far.at[at], sems.at[i]))
        stores[-1].start()
    for store in stores:
        store.wait()


def residual_kernel(target, image, pick, spread, r0, r1, r2, r3, half, *tiles):
    tile = tiles[0].shape[0]
    half[...] = (
        target[...] - (image[...] + product(spread[...], stacked(r0, r1, r2, r3)))
    ).astype(HALF)
    for d in range(4):
        tiles[d][...] = product(pick[d * tile : (d + 1) * tile, :], half[...]).astype(HALF)


def own_product(matrix, owned, arriving, name):
    local = matrix.shape[0]
    out = ((local, owned.shape[1]), FULL)
    flops = 2 * local * owned.size
    if arriving:
        return call(
            resident_kernel,
            name,
            [(matrix.shape, HALF), out],
            matrix,
            owned,
            far=1,
            scratch=(pltpu.SemaphoreType.DMA((6,)),),
            flops=flops,
        )
    return matrix, call(own_columns_kernel, name, [out], matrix, owned, flops=flops)[0]


def passed_along(shard, axis, by):
    devices = lax.axis_size(axis)
    pairs = [(i, i + by) for i in range(devices) if 0 <= i + by < devices]
    return lax.ppermute(shard, axis, pairs)


def traded(tiles):
    return (
        passed_along(tiles[1], "row", 1),
        passed_along(tiles[0], "row", -1),
        passed_along(tiles[3], "col", 1),
        passed_along(tiles[2], "col", -1),
    )


def per_device(
    right_side, local_operator, local_inverse, coarse_basis, coarse_inverse, send_rows, send_count
):
    target = right_side[0, 0]
    operator = local_operator[0, 0]
    inverse = local_inverse[0, 0]
    basis = jnp.swapaxes(coarse_basis[0, 0], 0, 1)
    rows_list = send_rows[0, 0]
    own, columns = target.shape
    local = operator.shape[0]
    tile = rows_list.shape[1]
    margin = 4 * tile
    coarse = basis.shape[0]
    coarse_rows = lax.all_to_all(coarse_inverse, "row", 0, 0, tiled=True)
    coarse_rows, rows_list = lax.optimization_barrier((coarse_rows, rows_list))

    four_tiles = [((tile, columns), HALF)] * 4
    owned_half = ((own, columns), HALF)
    target, residual, pick, spread, *tiles = call(
        select_kernel,
        "select",
        [((own, columns), FULL), owned_half, ((margin, own), HALF), ((own, margin), HALF)]
        + four_tiles,
        target,
        rows_list,
        send_count[0],
        far=3,
        scratch=(
            pltpu.VMEM(rows_list.shape, jnp.int32),
            pltpu.SMEM((1, 4), jnp.int32),
            pltpu.SemaphoreType.DMA((3,)),
        ),
        flops=2 * margin * own * columns,
    )
    solution = None
    for sweep in range(ITERS):
        if sweep:
            ghosts = traded(tiles)
            operator, partial = own_product(operator, solution_half, sweep == 1, "operator_own")
            tiles = call(
                rim_kernel,
                "operator_rim",
                four_tiles,
                operator,
                partial,
                *ghosts,
                flops=2 * margin * margin * columns,
            )
            returned = traded(tiles)
            (image,) = call(
                inner_kernel,
                "operator_inner",
                [((own, columns), FULL)],
                operator,
                partial,
                *ghosts,
                flops=2 * own * margin * columns,
            )
            residual, *tiles = call(
                residual_kernel,
                "residual",
                [owned_half] + four_tiles,
                target,
                image,
                pick,
                spread,
                *returned,
                flops=4 * margin * own * columns,
            )
        ghosts = traded(tiles)
        inverse, partial = own_product(inverse, residual, sweep == 0, "inverse_own")
        (restricted,) = call(
            restrict_kernel,
            "restrict",
            [((coarse, columns), HALF)],
            basis,
            residual,
            *ghosts,
            flops=2 * local * coarse * columns,
        )
        gathered = lax.all_gather(restricted, "col", axis=0, tiled=True)
        gathered = lax.all_gather(gathered, "row", axis=0, tiled=True)
        (correction,) = call(
            margin_columns_kernel,
            "inverse_margin",
            [((local, columns), FULL)],
            inverse,
            partial,
            *ghosts,
            flops=2 * local * margin * columns,
        )
        level, *tiles = call(
            coarse_kernel,
            "coarse",
            [((coarse, columns), HALF)] + four_tiles,
            coarse_rows,
            gathered,
            basis,
            correction,
            flops=2 * (coarse_rows.size + coarse * margin) * columns,
        )
        returned = traded(tiles)
        if sweep == ITERS - 1:
            break
        before = [solution] if sweep else []
        solution, solution_half, *tiles = call(
            update_kernel(not sweep),
            "update",
            [((own, columns), FULL), owned_half] + four_tiles,
            *before,
            correction,
            level,
            basis,
            pick,
            spread,
            *returned,
            flops=4 * margin * own * columns,
        )
    (solution,) = call(
        last_update_kernel,
        "last_update",
        [((own, columns), FULL)],
        solution,
        correction,
        level,
        basis,
        spread,
        *returned,
        away=True,
        scratch=(pltpu.VMEM((own, columns), FULL), pltpu.SemaphoreType.DMA((4,))),
        flops=2 * margin * own * columns,
    )
    return solution[None, None]


def solution(mesh):
    return jax.shard_map(
        per_device,
        mesh=mesh,
        in_specs=(
            P("row", "col", None, None),
            P("row", "col", None, None),
            P("row", "col", None, None),
            P("row", "col", None, None),
            P(None, "col", "row"),
            P("row", "col", None, None),
            P("row", "col", None),
        ),
        out_specs=P("row", "col", None, None),
        check_vma=False,
    )
```

```python
import jax
import jax.numpy as jnp
from jax import lax
from jax.experimental import pallas as pl
from jax.experimental.pallas import tpu as pltpu
from jax.sharding import PartitionSpec as P

ITERS = 3
DAMPING = 0.5
HALF = jnp.bfloat16
FULL = jnp.float32


def product(left, right):
    return jnp.dot(left, right, preferred_element_type=FULL)


def turned_product(left, right):
    return lax.dot_general(left, right, (((0,), (0,)), ((), ())), preferred_element_type=FULL)


def call(body, name, outs, *args, far=0, away=False, scratch=(), flops=0):
    here = pl.BlockSpec(memory_space=pltpu.VMEM)
    there = pl.BlockSpec(memory_space=pltpu.HBM)
    size = sum(a.size * a.dtype.itemsize for a in args)
    distant = [pltpu.with_memory_space_constraint(a, pltpu.HBM) for a in args[:far]]
    near = [pltpu.with_memory_space_constraint(a, pltpu.VMEM) for a in args[far:]]
    return pl.pallas_call(
        body,
        out_shape=tuple((pltpu.HBM if away else pltpu.VMEM)(*out) for out in outs),
        in_specs=[there] * far + [here] * len(near),
        out_specs=tuple(there if away else here for _ in outs),
        scratch_shapes=list(scratch),
        compiler_params=pltpu.CompilerParams(vmem_limit_bytes=24 * 1024 * 1024),
        cost_estimate=pl.CostEstimate(flops=flops, bytes_accessed=size, transcendentals=0),
        name=name,
    )(*distant, *near)


def select_kernel(far_target, far_rows, far_counts, half, pick, spread, *rest):
    *tiles, target, rows, counts, sems = rest
    own = target.shape[0]
    tile = rows.shape[1]
    loads = [
        pltpu.make_async_copy(far, near, sems.at[i])
        for i, (far, near) in enumerate(((far_rows, rows), (far_counts, counts), (far_target, target)))
    ]
    for load in loads:
        load.start()
    loads[0].wait()
    loads[1].wait()
    for d in range(4):
        here = jnp.where(
            lax.broadcasted_iota(jnp.int32, (1, tile), 1) < counts[0, d], rows[d : d + 1, :], -1
        )
        wide = jnp.broadcast_to(here, (own, tile))
        spread[:, d * tile : (d + 1) * tile] = (
            lax.broadcasted_iota(jnp.int32, (own, tile), 0) == wide
        ).astype(FULL).astype(HALF)
        down = jnp.transpose(jnp.broadcast_to(here, (tile, tile)))[:, :1]
        pick[d * tile : (d + 1) * tile, :] = (
            lax.broadcasted_iota(jnp.int32, (tile, own), 1) == down
        ).astype(FULL).astype(HALF)
    loads[2].wait()
    half[...] = target[...].astype(HALF)
    for d in range(4):
        tiles[d][...] = product(pick[d * tile : (d + 1) * tile, :], half[...]).astype(HALF)


def resident_kernel(far, owned, matrix, out, sems):
    own = owned.shape[0]
    pieces = sems.shape[0]
    height = far.shape[0] // pieces
    spans = [slice(i * height, (i + 1) * height) for i in range(pieces)]
    loads = [
        pltpu.make_async_copy(far.at[at], matrix.at[at], sems.at[i]) for i, at in enumerate(spans)
    ]
    for load in loads:
        load.start()
    for load, at in zip(loads, spans):
        load.wait()
        out[at, :] = product(matrix[at, :own], owned[...])


def load_kernel(far, near, sems):
    pieces = sems.shape[0]
    height = far.shape[0] // pieces
    loads = []
    for i in range(pieces):
        at = slice(i * height, (i + 1) * height)
        loads.append(pltpu.make_async_copy(far.at[at], near.at[at], sems.at[i]))
        loads[-1].start()
    for load in loads:
        load.wait()


def own_columns_kernel(matrix, owned, out):
    own = owned.shape[0]
    out[...] = product(matrix[:, :own], owned[...])


def stacked(g0, g1, g2, g3):
    return jnp.concatenate([g0[...], g1[...], g2[...], g3[...]], axis=0)


def solve_kernel(matrix, partial, basis, owned, g0, g1, g2, g3, restricted, rim, inner):
    own = owned.shape[0]
    ghosts = stacked(g0, g1, g2, g3)
    total = product(basis[:, :own], owned[...]) + product(basis[:, own:], ghosts)
    for i in range(restricted.shape[0]):
        restricted[i, :, :] = total.astype(HALF)
    rim[...] = partial[own:, :] + product(matrix[own:, own:], ghosts)
    inner[...] = partial[:own, :] + product(matrix[:own, own:], ghosts)


def partial_kernel(inverse, gathered, out):
    for i in range(inverse.shape[0]):
        out[i, :, :] = product(inverse[i, :, :], gathered[...]).astype(HALF)


def coarse_kernel(parts, basis, rim, level, *tiles):
    tile = tiles[0].shape[0]
    own = basis.shape[1] - 4 * tile
    total = parts[0, :, :].astype(FULL)
    for i in range(1, parts.shape[0]):
        total += parts[i, :, :].astype(FULL)
    level[...] = total.astype(HALF)
    for d in range(4):
        here = slice(d * tile, (d + 1) * tile)
        there = slice(own + d * tile, own + (d + 1) * tile)
        tiles[d][...] = (rim[here, :] + turned_product(basis[:, there], level[...])).astype(HALF)


def rim_kernel(matrix, partial, g0, g1, g2, g3, *tiles):
    tile = g0.shape[0]
    own = matrix.shape[1] - 4 * tile
    ghosts = stacked(g0, g1, g2, g3)
    for d in range(4):
        at = slice(own + d * tile, own + (d + 1) * tile)
        tiles[d][...] = (partial[at, :] + product(matrix[at, own:], ghosts)).astype(HALF)


def inner_kernel(matrix, partial, g0, g1, g2, g3, out):
    own = matrix.shape[1] - 4 * g0.shape[0]
    out[...] = partial[:own, :] + product(matrix[:own, own:], stacked(g0, g1, g2, g3))


def update_kernel(first):
    def body(*refs):
        refs = list(refs)
        before = None if first else refs.pop(0)
        local, level, basis, pick, spread, r0, r1, r2, r3, after, half, *tiles = refs
        own = after.shape[0]
        update = (
            local[...]
            + turned_product(basis[:, :own], level[...])
            + product(spread[...], stacked(r0, r1, r2, r3))
        )
        after[...] = DAMPING * update if first else before[...] + DAMPING * update
        tile = tiles[0].shape[0]
        half[...] = after[...].astype(HALF)
        for d in range(4):
            tiles[d][...] = product(pick[d * tile : (d + 1) * tile, :], half[...]).astype(HALF)

    return body


def last_update_kernel(before, local, level, basis, spread, r0, r1, r2, r3, far, after, sems):
    pieces = sems.shape[0]
    height = after.shape[0] // pieces
    returned = stacked(r0, r1, r2, r3)
    stores = []
    for i in range(pieces):
        at = slice(i * height, (i + 1) * height)
        update = (
            local[at, :]
            + turned_product(basis[:, at], level[...])
            + product(spread[at, :], returned)
        )
        after[at, :] = before[at, :] + DAMPING * update
        stores.append(pltpu.make_async_copy(after.at[at], far.at[at], sems.at[i]))
        stores[-1].start()
    for store in stores:
        store.wait()


def residual_kernel(far, image, pick, spread, r0, r1, r2, r3, half, *rest):
    *tiles, target, sem = rest
    tile = tiles[0].shape[0]
    load = pltpu.make_async_copy(far, target, sem)
    load.start()
    image_sum = image[...] + product(spread[...], stacked(r0, r1, r2, r3))
    load.wait()
    half[...] = (target[...] - image_sum).astype(HALF)
    for d in range(4):
        tiles[d][...] = product(pick[d * tile : (d + 1) * tile, :], half[...]).astype(HALF)


def brought(matrix, tiles, name):
    matrix, tiles = lax.optimization_barrier((matrix, tuple(tiles)))
    (near,) = call(
        load_kernel,
        name,
        [(matrix.shape, HALF)],
        matrix,
        far=1,
        scratch=(pltpu.SemaphoreType.DMA((8,)),),
    )
    return near, tiles


def passed_along(shard, axis, by):
    devices = lax.axis_size(axis)
    pairs = [(i, i + by) for i in range(devices) if 0 <= i + by < devices]
    return lax.ppermute(shard, axis, pairs)


def traded(tiles):
    return (
        passed_along(tiles[1], "row", 1),
        passed_along(tiles[0], "row", -1),
        passed_along(tiles[3], "col", 1),
        passed_along(tiles[2], "col", -1),
    )


def per_device(
    right_side, local_operator, local_inverse, coarse_basis, coarse_inverse, send_rows, send_count
):
    target = right_side[0, 0]
    operator = local_operator[0, 0]
    inverse = local_inverse[0, 0]
    basis = jnp.swapaxes(coarse_basis[0, 0], 0, 1)
    rows_list = send_rows[0, 0]
    own, columns = target.shape
    local = operator.shape[0]
    tile = rows_list.shape[1]
    margin = 4 * tile
    coarse = basis.shape[0]
    groups = coarse_inverse.shape[0]
    across = lax.axis_size("col")

    four_tiles = [((tile, columns), HALF)] * 4
    owned_half = ((own, columns), HALF)
    owned_full = ((own, columns), FULL)
    local_full = ((local, columns), FULL)
    residual, pick, spread, *tiles = call(
        select_kernel,
        "select",
        [owned_half, ((margin, own), HALF), ((own, margin), HALF)] + four_tiles,
        target,
        rows_list,
        send_count[0],
        far=3,
        scratch=(
            pltpu.VMEM((own, columns), FULL),
            pltpu.VMEM(rows_list.shape, jnp.int32),
            pltpu.SMEM((1, 4), jnp.int32),
            pltpu.SemaphoreType.DMA((3,)),
        ),
        flops=2 * margin * own * columns,
    )
    solution = None
    for sweep in range(ITERS):
        if sweep:
            ghosts = traded(tiles)
            (partial,) = call(
                own_columns_kernel,
                "operator_own",
                [local_full],
                near_operator,
                solution_half,
                flops=2 * local * own * columns,
            )
            tiles = call(
                rim_kernel,
                "operator_rim",
                four_tiles,
                near_operator,
                partial,
                *ghosts,
                flops=2 * margin * margin * columns,
            )
            near_inverse, tiles = brought(inverse, tiles, "inverse_load")
            returned = traded(tiles)
            (image,) = call(
                inner_kernel,
                "operator_inner",
                [owned_full],
                near_operator,
                partial,
                *ghosts,
                flops=2 * own * margin * columns,
            )
            residual, *tiles = call(
                residual_kernel,
                "residual",
                [owned_half] + four_tiles,
                target,
                image,
                pick,
                spread,
                *returned,
                far=1,
                scratch=(pltpu.VMEM((own, columns), FULL), pltpu.SemaphoreType.DMA),
                flops=4 * margin * own * columns,
            )
            ghosts = traded(tiles)
            (partial,) = call(
                own_columns_kernel,
                "inverse_own",
                [local_full],
                near_inverse,
                residual,
                flops=2 * local * own * columns,
            )
        else:
            ghosts = traded(tiles)
            near_inverse, partial = call(
                resident_kernel,
                "inverse_own",
                [(inverse.shape, HALF), local_full],
                inverse,
                residual,
                far=1,
                scratch=(pltpu.SemaphoreType.DMA((6,)),),
                flops=2 * local * own * columns,
            )
        restricted, rim, inner = call(
            solve_kernel,
            "inverse_margin",
            [((across, coarse, columns), HALF), ((margin, columns), FULL), owned_full],
            near_inverse,
            partial,
            basis,
            residual,
            *ghosts,
            flops=2 * local * (margin + coarse) * columns,
        )
        gathered = lax.all_to_all(restricted, "col", 0, 0, tiled=True)
        (parts,) = call(
            partial_kernel,
            "coarse_part",
            [((groups, coarse, columns), HALF)],
            coarse_inverse,
            gathered.reshape(across * coarse, columns),
            flops=2 * coarse_inverse.size * columns,
        )
        parts = lax.all_to_all(parts, "row", 0, 0, tiled=True)
        level, *tiles = call(
            coarse_kernel,
            "coarse",
            [((coarse, columns), HALF)] + four_tiles,
            parts,
            basis,
            rim,
            flops=2 * coarse * margin * columns,
        )
        if sweep < ITERS - 1:
            near_operator, tiles = brought(operator, tiles, "operator_load")
        returned = traded(tiles)
        if sweep == ITERS - 1:
            break
        before = [solution] if sweep else []
        solution, solution_half, *tiles = call(
            update_kernel(not sweep),
            "update",
            [owned_full, owned_half] + four_tiles,
            *before,
            inner,
            level,
            basis,
            pick,
            spread,
            *returned,
            flops=4 * margin * own * columns,
        )
    (solution,) = call(
        last_update_kernel,
        "last_update",
        [owned_full],
        solution,
        inner,
        level,
        basis,
        spread,
        *returned,
        away=True,
        scratch=(pltpu.VMEM((own, columns), FULL), pltpu.SemaphoreType.DMA((4,))),
        flops=2 * margin * own * columns,
    )
    return solution[None, None]


def solution(mesh):
    return jax.shard_map(
        per_device,
        mesh=mesh,
        in_specs=(
            P("row", "col", None, None),
            P("row", "col", None, None),
            P("row", "col", None, None),
            P("row", "col", None, None),
            P(None, "col", "row"),
            P("row", "col", None, None),
            P("row", "col", None),
        ),
        out_specs=P("row", "col", None, None),
        check_vma=False,
    )
```

```python
import jax
import jax.numpy as jnp
from jax import lax
from jax.experimental import pallas as pl
from jax.experimental.pallas import tpu as pltpu
from jax.sharding import PartitionSpec as P

ITERS = 3
DAMPING = 0.5
HALF = jnp.bfloat16
FULL = jnp.float32


def product(left, right):
    return jnp.dot(left, right, preferred_element_type=FULL)


def turned_product(left, right):
    return lax.dot_general(left, right, (((0,), (0,)), ((), ())), preferred_element_type=FULL)


def call(body, name, outs, *args, far=0, away=False, scratch=(), flops=0):
    here = pl.BlockSpec(memory_space=pltpu.VMEM)
    there = pl.BlockSpec(memory_space=pltpu.HBM)
    size = sum(a.size * a.dtype.itemsize for a in args)
    distant = [pltpu.with_memory_space_constraint(a, pltpu.HBM) for a in args[:far]]
    near = [pltpu.with_memory_space_constraint(a, pltpu.VMEM) for a in args[far:]]
    return pl.pallas_call(
        body,
        out_shape=tuple((pltpu.HBM if away else pltpu.VMEM)(*out) for out in outs),
        in_specs=[there] * far + [here] * len(near),
        out_specs=tuple(there if away else here for _ in outs),
        scratch_shapes=list(scratch),
        compiler_params=pltpu.CompilerParams(vmem_limit_bytes=24 * 1024 * 1024),
        cost_estimate=pl.CostEstimate(flops=flops, bytes_accessed=size, transcendentals=0),
        name=name,
    )(*distant, *near)


def select_kernel(
    far_target, far_rows, far_counts, far_inverse, target, half, pick, masked, inverse, *rest
):
    *tiles, rows, counts, sems = rest
    own = target.shape[0]
    tile = rows.shape[1]
    pairs = [(far_rows, rows), (far_counts, counts), (far_target, target)]
    pieces = sems.shape[0] - len(pairs)
    height = inverse.shape[0] // pieces
    for i in range(pieces):
        at = slice(i * height, (i + 1) * height)
        pairs.append((far_inverse.at[at], inverse.at[at]))
    loads = [
        pltpu.make_async_copy(far, near, sems.at[i]) for i, (far, near) in enumerate(pairs)
    ]
    for load in loads:
        load.start()
    loads[0].wait()
    loads[1].wait()
    for d in range(4):
        here = jnp.where(
            lax.broadcasted_iota(jnp.int32, (1, tile), 1) < counts[0, d], rows[d : d + 1, :], -1
        )
        masked[d : d + 1, :] = here
        down = jnp.transpose(jnp.broadcast_to(here, (tile, tile)))[:, :1]
        pick[d * tile : (d + 1) * tile, :] = (
            lax.broadcasted_iota(jnp.int32, (tile, own), 1) == down
        ).astype(FULL).astype(HALF)
    loads[2].wait()
    half[...] = target[...].astype(HALF)
    picked(pick, half, tiles)
    for load in loads[3:]:
        load.wait()


def picked(pick, half, tiles):
    tile = tiles[0].shape[0]
    for d in range(4):
        tiles[d][...] = product(pick[d * tile : (d + 1) * tile, :], half[...]).astype(HALF)


def spread_kernel(masked, spread):
    own = spread.shape[0]
    tile = masked.shape[1]
    for d in range(4):
        wide = jnp.broadcast_to(masked[d : d + 1, :], (own, tile))
        spread[:, d * tile : (d + 1) * tile] = (
            lax.broadcasted_iota(jnp.int32, (own, tile), 0) == wide
        ).astype(FULL).astype(HALF)


def load_kernel(far, near, sems):
    pieces = sems.shape[0]
    height = far.shape[0] // pieces
    loads = []
    for i in range(pieces):
        at = slice(i * height, (i + 1) * height)
        loads.append(pltpu.make_async_copy(far.at[at], near.at[at], sems.at[i]))
        loads[-1].start()
    for load in loads:
        load.wait()


def stacked(*parts):
    return jnp.concatenate([part[...] for part in parts], axis=0)


def own_columns_kernel(matrix, owned, out):
    own = owned.shape[0]
    out[...] = product(matrix[:, :own], owned[...])


def near_columns_kernel(matrix, owned, g0, g1, out):
    own = owned.shape[0]
    split = own + 2 * g0.shape[0]
    out[...] = product(matrix[:, :own], owned[...]) + product(matrix[:, own:split], stacked(g0, g1))


def share_kernel(basis, owned, t2, t3, g0, g1, out):
    own, tile, coarse = owned.shape[0], t2.shape[0], basis.shape[0]
    split = own + 2 * tile
    out[:tile, :] = t2[...]
    out[tile : 2 * tile, :] = t3[...]
    out[2 * tile : 2 * tile + coarse, :] = (
        product(basis[:, :own], owned[...]) + product(basis[:, own:split], stacked(g0, g1))
    ).astype(HALF)
    if out.shape[0] > 2 * tile + coarse:
        out[2 * tile + coarse :, : 2 * tile] = basis[:, split:]


def solve_kernel(first, across):
    def body(*refs):
        refs = list(refs)
        rims = None if first else refs.pop(0)
        matrix, partial, gathered, inverse, g0, g1, parts, rim, inner, *rest = refs
        tile, coarse = g0.shape[0], inverse.shape[1]
        own = inner.shape[0]
        stride = gathered.shape[0] // across
        if first:
            (rims,) = rest
            for b in range(across):
                at = b * stride + 2 * tile + coarse
                rims[b * coarse : (b + 1) * coarse, :] = gathered[at : at + coarse, : 2 * tile]
        restricted = []
        for b in range(across):
            here = slice(b * coarse, (b + 1) * coarse)
            at = b * stride + 2 * tile
            total = gathered[at : at + coarse, :].astype(FULL)
            if b > 0:
                at = (b - 1) * stride + tile
                total += product(rims[here, :tile], gathered[at : at + tile, :])
            if b < across - 1:
                at = (b + 1) * stride
                total += product(rims[here, tile:], gathered[at : at + tile, :])
            restricted.append(total.astype(HALF))
        restricted = jnp.concatenate(restricted, axis=0)
        for i in range(parts.shape[0]):
            parts[i, :, :] = product(inverse[i, :, :], restricted).astype(HALF)
        me = lax.axis_index("col")
        at = pl.multiple_of(jnp.maximum(me - 1, 0) * stride + tile, 32)
        lower = gathered[pl.ds(at, tile), :]
        at = pl.multiple_of(jnp.minimum(me + 1, across - 1) * stride, 32)
        upper = gathered[pl.ds(at, tile), :]
        lower = jnp.where(me > 0, lower, jnp.zeros_like(lower))
        upper = jnp.where(me < across - 1, upper, jnp.zeros_like(upper))
        ghosts = jnp.concatenate([g0[...], g1[...], lower, upper], axis=0)
        rim[...] = partial[own:, :] + product(matrix[own:, own:], ghosts)
        inner[...] = partial[:own, :] + product(matrix[:own, own:], ghosts)

    return body


def coarse_kernel(parts, basis, rim, level, *tiles):
    tile = tiles[0].shape[0]
    own = basis.shape[1] - 4 * tile
    total = parts[0, :, :].astype(FULL)
    for i in range(1, parts.shape[0]):
        total += parts[i, :, :].astype(FULL)
    level[...] = total.astype(HALF)
    for d in range(4):
        here = slice(d * tile, (d + 1) * tile)
        there = slice(own + d * tile, own + (d + 1) * tile)
        tiles[d][...] = (rim[here, :] + turned_product(basis[:, there], level[...])).astype(HALF)


def base_kernel(first):
    def body(*refs):
        refs = list(refs)
        before = None if first else refs.pop(0)
        inner, level, basis, spread, r0, r1, out = refs
        own, tile = out.shape[0], r0.shape[0]
        update = (
            inner[...]
            + turned_product(basis[:, :own], level[...])
            + product(spread[:, : 2 * tile], stacked(r0, r1))
        )
        out[...] = DAMPING * update if first else before[...] + DAMPING * update

    return body


def update_kernel(base, pick, spread, r2, r3, after, half, *tiles):
    tile = r2.shape[0]
    after[...] = base[...] + DAMPING * product(spread[:, 2 * tile :], stacked(r2, r3))
    half[...] = after[...].astype(HALF)
    picked(pick, half, tiles)


def last_update_kernel(base, spread, r2, r3, far, after, sems):
    tile = r2.shape[0]
    pieces = sems.shape[0]
    height = after.shape[0] // pieces
    returned = stacked(r2, r3)
    stores = []
    for i in range(pieces):
        at = slice(i * height, (i + 1) * height)
        after[at, :] = base[at, :] + DAMPING * product(spread[at, 2 * tile :], returned)
        stores.append(pltpu.make_async_copy(after.at[at], far.at[at], sems.at[i]))
        stores[-1].start()
    for store in stores:
        store.wait()


def rim_kernel(matrix, partial, g2, g3, *tiles):
    tile = g2.shape[0]
    own = matrix.shape[1] - 4 * tile
    ghosts = stacked(g2, g3)
    for d in range(4):
        at = slice(own + d * tile, own + (d + 1) * tile)
        tiles[d][...] = (partial[at, :] + product(matrix[at, own + 2 * tile :], ghosts)).astype(HALF)


def remainder_kernel(target, matrix, partial, g2, g3, spread, r0, r1, out):
    own, tile = target.shape[0], g2.shape[0]
    image = (
        partial[:own, :]
        + product(matrix[:own, own + 2 * tile :], stacked(g2, g3))
        + product(spread[:, : 2 * tile], stacked(r0, r1))
    )
    out[...] = target[...] - image


def residual_kernel(remainder, pick, spread, r2, r3, half, *tiles):
    tile = r2.shape[0]
    half[...] = (remainder[...] - product(spread[:, 2 * tile :], stacked(r2, r3))).astype(HALF)
    picked(pick, half, tiles)


def brought(matrix, tiles, name):
    matrix, tiles = lax.optimization_barrier((matrix, tuple(tiles)))
    (near,) = call(
        load_kernel,
        name,
        [(matrix.shape, HALF)],
        matrix,
        far=1,
        scratch=(pltpu.SemaphoreType.DMA((8,)),),
    )
    return near, tiles


def passed_along(shard, axis, by):
    devices = lax.axis_size(axis)
    pairs = [(i, i + by) for i in range(devices) if 0 <= i + by < devices]
    return lax.ppermute(shard, axis, pairs)


def traded_over_row(tiles):
    return passed_along(tiles[1], "row", 1), passed_along(tiles[0], "row", -1)


def traded(tiles):
    return (
        *traded_over_row(tiles),
        passed_along(tiles[3], "col", 1),
        passed_along(tiles[2], "col", -1),
    )


def per_device(
    right_side, local_operator, local_inverse, coarse_basis, coarse_inverse, send_rows, send_count
):
    target = right_side[0, 0]
    operator = local_operator[0, 0]
    inverse = local_inverse[0, 0]
    basis = jnp.swapaxes(coarse_basis[0, 0], 0, 1)
    rows_list = send_rows[0, 0]
    own, columns = target.shape
    local = operator.shape[0]
    tile = rows_list.shape[1]
    margin = 4 * tile
    coarse = basis.shape[0]
    groups = coarse_inverse.shape[0]
    across = lax.axis_size("col")

    four_tiles = [((tile, columns), HALF)] * 4
    owned_half = ((own, columns), HALF)
    owned_full = ((own, columns), FULL)
    local_full = ((local, columns), FULL)
    target, residual, pick, masked, inverse, *tiles = call(
        select_kernel,
        "select",
        [
            owned_full,
            owned_half,
            ((margin, own), HALF),
            (rows_list.shape, jnp.int32),
            (inverse.shape, HALF),
        ]
        + four_tiles,
        target,
        rows_list,
        send_count[0],
        inverse,
        far=4,
        scratch=(
            pltpu.VMEM(rows_list.shape, jnp.int32),
            pltpu.SMEM((1, 4), jnp.int32),
            pltpu.SemaphoreType.DMA((3 + 8,)),
        ),
        flops=2 * margin * own * columns,
    )
    rims = spread = solution = None
    for sweep in range(ITERS):
        first, last = sweep == 0, sweep == ITERS - 1
        if sweep:
            g0, g1, g2, g3 = traded(tiles)
            (partial,) = call(
                near_columns_kernel,
                "operator_near",
                [local_full],
                operator,
                solution_half,
                g0,
                g1,
                flops=2 * local * (own + 2 * tile) * columns,
            )
            tiles = call(
                rim_kernel,
                "operator_rim",
                four_tiles,
                operator,
                partial,
                g2,
                g3,
                flops=4 * margin * tile * columns,
            )
            r0, r1, r2, r3 = traded(tiles)
            (remainder,) = call(
                remainder_kernel,
                "remainder",
                [owned_full],
                target,
                operator,
                partial,
                g2,
                g3,
                spread,
                r0,
                r1,
                flops=8 * own * tile * columns,
            )
            residual, *tiles = call(
                residual_kernel,
                "residual",
                [owned_half] + four_tiles,
                remainder,
                pick,
                spread,
                r2,
                r3,
                flops=(2 * margin + 4 * tile) * own * columns,
            )
        g0, g1 = traded_over_row(tiles)
        (partial,) = call(
            own_columns_kernel,
            "inverse_own",
            [local_full],
            inverse,
            residual,
            flops=2 * local * own * columns,
        )
        if first:
            (spread,) = call(spread_kernel, "spread", [((own, margin), HALF)], masked)
        (share,) = call(
            share_kernel,
            "share",
            [((2 * tile + coarse * (2 if first else 1), columns), HALF)],
            basis,
            residual,
            tiles[2],
            tiles[3],
            g0,
            g1,
            flops=2 * local * coarse * columns,
        )
        gathered = lax.all_gather(share, "col", axis=0, tiled=True)
        outs = [((groups, coarse, columns), HALF), ((margin, columns), FULL), owned_full]
        parts, rim, inner, *rest = call(
            solve_kernel(first, across),
            "inverse_margin",
            outs + ([((across * coarse, 2 * tile), HALF)] if first else []),
            *([] if first else [rims]),
            inverse,
            partial,
            gathered,
            coarse_inverse,
            g0,
            g1,
            flops=2 * (local * margin + coarse_inverse.size) * columns,
        )
        if first:
            (rims,) = rest
        parts = lax.all_to_all(parts, "row", 0, 0, tiled=True)
        level, *tiles = call(
            coarse_kernel,
            "coarse",
            [((coarse, columns), HALF)] + four_tiles,
            parts,
            basis,
            rim,
            flops=2 * coarse * margin * columns,
        )
        if first:
            operator, tiles = brought(operator, tiles, "operator_load")
        r0, r1, r2, r3 = traded(tiles)
        (base,) = call(
            base_kernel(first),
            "base",
            [owned_full],
            *([] if first else [solution]),
            inner,
            level,
            basis,
            spread,
            r0,
            r1,
            flops=2 * (2 * tile + coarse) * own * columns,
        )
        if last:
            break
        solution, solution_half, *tiles = call(
            update_kernel,
            "update",
            [owned_full, owned_half] + four_tiles,
            base,
            pick,
            spread,
            r2,
            r3,
            flops=(2 * margin + 4 * tile) * own * columns,
        )
    (solution,) = call(
        last_update_kernel,
        "last_update",
        [owned_full],
        base,
        spread,
        r2,
        r3,
        away=True,
        scratch=(pltpu.VMEM((own, columns), FULL), pltpu.SemaphoreType.DMA((4,))),
        flops=4 * tile * own * columns,
    )
    return solution[None, None]


def solution(mesh):
    return jax.shard_map(
        per_device,
        mesh=mesh,
        in_specs=(
            P("row", "col", None, None),
            P("row", "col", None, None),
            P("row", "col", None, None),
            P("row", "col", None, None),
            P(None, "col", "row"),
            P("row", "col", None, None),
            P("row", "col", None),
        ),
        out_specs=P("row", "col", None, None),
        check_vma=False,
    )
```

```python
import jax
import jax.numpy as jnp
from jax import lax
from jax.experimental import pallas as pl
from jax.experimental.pallas import tpu as pltpu
from jax.sharding import PartitionSpec as P

ITERS = 3
DAMPING = 0.5
HALF = jnp.bfloat16
FULL = jnp.float32


def product(left, right):
    return jnp.dot(left, right, preferred_element_type=FULL)


def turned_product(left, right):
    return lax.dot_general(left, right, (((0,), (0,)), ((), ())), preferred_element_type=FULL)


def call(body, name, outs, *args, far=0, away=False, scratch=(), flops=0):
    here = pl.BlockSpec(memory_space=pltpu.VMEM)
    there = pl.BlockSpec(memory_space=pltpu.HBM)
    size = sum(a.size * a.dtype.itemsize for a in args)
    distant = [pltpu.with_memory_space_constraint(a, pltpu.HBM) for a in args[:far]]
    near = [pltpu.with_memory_space_constraint(a, pltpu.VMEM) for a in args[far:]]
    return pl.pallas_call(
        body,
        out_shape=tuple((pltpu.HBM if away else pltpu.VMEM)(*out) for out in outs),
        in_specs=[there] * far + [here] * len(near),
        out_specs=tuple(there if away else here for _ in outs),
        scratch_shapes=list(scratch),
        compiler_params=pltpu.CompilerParams(vmem_limit_bytes=24 * 1024 * 1024),
        cost_estimate=pl.CostEstimate(flops=flops, bytes_accessed=size, transcendentals=0),
        name=name,
    )(*distant, *near)


def parities():
    return lax.rem(lax.axis_index("row"), 2), lax.rem(lax.axis_index("col"), 2)


def directions():
    row, col = parities()
    return 1 - row, row, 3 - col, 2 + col


def margin_spans(own, tile):
    return [
        (pl.ds(pl.multiple_of(own + d * tile, tile), tile), slice(own + i * tile, own + (i + 1) * tile))
        for i, d in enumerate(directions())
    ]


def matrix_pieces(far, near, own, tile):
    margins = margin_spans(own, tile)
    half = own // 2
    rows = [(slice(0, half), slice(0, half)), (slice(half, own), slice(half, own))] + margins
    columns = [(slice(0, own), slice(0, own))] + margins
    return [(far.at[fr, fc], near.at[nr, nc]) for fr, nr in rows for fc, nc in columns]


MATRIX_PIECES = 30


def started(pairs, sems):
    loads = [pltpu.make_async_copy(far, near, sems.at[i]) for i, (far, near) in enumerate(pairs)]
    for load in loads:
        load.start()
    return loads


def select_kernel(
    far_target, far_rows, far_counts, far_basis, far_inverse, target, half, pick, masked, basis, inverse, *rest
):
    *tiles, rows, counts, sems = rest
    own = target.shape[0]
    tile = rows.shape[1]
    pairs = [(far_rows, rows), (far_counts, counts), (far_target, target)]
    pairs += [
        (far_basis.at[:, far], basis.at[:, near])
        for far, near in [(slice(0, own), slice(0, own))] + margin_spans(own, tile)
    ]
    pairs += matrix_pieces(far_inverse, inverse, own, tile)
    loads = started(pairs, sems)
    loads[0].wait()
    loads[1].wait()
    listed = [
        jnp.where(
            lax.broadcasted_iota(jnp.int32, (1, tile), 1) < counts[0, d], rows[d : d + 1, :], -1
        )
        for d in range(4)
    ]
    row, col = parities()
    ordered = (
        jnp.where(row == 0, listed[1], listed[0]),
        jnp.where(row == 0, listed[0], listed[1]),
        jnp.where(col == 0, listed[3], listed[2]),
        jnp.where(col == 0, listed[2], listed[3]),
    )
    for i, here in enumerate(ordered):
        masked[i : i + 1, :] = here
        down = jnp.transpose(jnp.broadcast_to(here, (tile, tile)))[:, :1]
        pick[i * tile : (i + 1) * tile, :] = (
            lax.broadcasted_iota(jnp.int32, (tile, own), 1) == down
        ).astype(FULL).astype(HALF)
    loads[2].wait()
    half[...] = target[...].astype(HALF)
    picked(pick, half, tiles)
    for load in loads[3:]:
        load.wait()


def picked(pick, half, tiles):
    tile = tiles[0].shape[0]
    for d in range(4):
        tiles[d][...] = product(pick[d * tile : (d + 1) * tile, :], half[...]).astype(HALF)


def spread_kernel(far, masked, spread, matrix, sems):
    own = spread.shape[0]
    tile = masked.shape[1]
    loads = started(matrix_pieces(far, matrix, own, tile), sems)
    for d in range(4):
        wide = jnp.broadcast_to(masked[d : d + 1, :], (own, tile))
        spread[:, d * tile : (d + 1) * tile] = (
            lax.broadcasted_iota(jnp.int32, (own, tile), 0) == wide
        ).astype(FULL).astype(HALF)
    for load in loads:
        load.wait()


def stacked(*parts):
    return jnp.concatenate([part[...] for part in parts], axis=0)


def own_columns_kernel(matrix, owned, out):
    own = owned.shape[0]
    out[...] = product(matrix[:, :own], owned[...])


def near_columns_kernel(matrix, owned, g0, g1, out):
    own = owned.shape[0]
    split = own + 2 * g0.shape[0]
    out[...] = product(matrix[:, :own], owned[...]) + product(matrix[:, own:split], stacked(g0, g1))


def share_kernel(basis, owned, t2, t3, g0, g1, out):
    own, tile, coarse = owned.shape[0], t2.shape[0], basis.shape[0]
    split = own + 2 * tile
    out[:tile, :] = t2[...]
    out[tile : 2 * tile, :] = t3[...]
    out[2 * tile : 2 * tile + coarse, :] = (
        product(basis[:, :own], owned[...]) + product(basis[:, own:split], stacked(g0, g1))
    ).astype(HALF)
    if out.shape[0] > 2 * tile + coarse:
        out[2 * tile + coarse :, : 2 * tile] = basis[:, split:]


def solve_kernel(first, across):
    def body(*refs):
        refs = list(refs)
        rims = None if first else refs.pop(0)
        matrix, partial, gathered, inverse, g0, g1, parts, rim, inner, *rest = refs
        tile, coarse = g0.shape[0], inverse.shape[1]
        own = inner.shape[0]
        stride = gathered.shape[0] // across
        if first:
            (rims,) = rest
            for b in range(across):
                at = b * stride + 2 * tile + coarse
                rims[b * coarse : (b + 1) * coarse, :] = gathered[at : at + coarse, : 2 * tile]
        restricted = []
        for b in range(across):
            here = slice(b * coarse, (b + 1) * coarse)
            at = b * stride + 2 * tile
            total = gathered[at : at + coarse, :].astype(FULL)
            for i in range(2):
                other = partner(b, i)
                if 0 <= other < across:
                    at = other * stride + i * tile
                    total += product(
                        rims[here, i * tile : (i + 1) * tile], gathered[at : at + tile, :]
                    )
            restricted.append(total.astype(HALF))
        restricted = jnp.concatenate(restricted, axis=0)
        for i in range(parts.shape[0]):
            parts[i, :, :] = product(inverse[i, :, :], restricted).astype(HALF)
        ghosts = [g0[...], g1[...]]
        for i in range(2):
            other = partner(lax.axis_index("col"), i)
            there = (other >= 0) & (other < across)
            at = pl.multiple_of(jnp.where(there, other, 0) * stride + i * tile, 32)
            ghost = gathered[pl.ds(at, tile), :]
            ghosts.append(jnp.where(there, ghost, jnp.zeros_like(ghost)))
        ghosts = jnp.concatenate(ghosts, axis=0)
        rim[...] = partial[own:, :] + product(matrix[own:, own:], ghosts)
        inner[...] = partial[:own, :] + product(matrix[:own, own:], ghosts)

    return body


def coarse_kernel(parts, basis, rim, level, *tiles):
    tile = tiles[0].shape[0]
    own = basis.shape[1] - 4 * tile
    total = parts[0, :, :].astype(FULL)
    for i in range(1, parts.shape[0]):
        total += parts[i, :, :].astype(FULL)
    level[...] = total.astype(HALF)
    for d in range(4):
        here = slice(d * tile, (d + 1) * tile)
        there = slice(own + d * tile, own + (d + 1) * tile)
        tiles[d][...] = (rim[here, :] + turned_product(basis[:, there], level[...])).astype(HALF)


def base_kernel(first):
    def body(*refs):
        refs = list(refs)
        before = None if first else refs.pop(0)
        inner, level, basis, spread, r0, r1, out = refs
        own, tile = out.shape[0], r0.shape[0]
        update = (
            inner[...]
            + turned_product(basis[:, :own], level[...])
            + product(spread[:, : 2 * tile], stacked(r0, r1))
        )
        out[...] = DAMPING * update if first else before[...] + DAMPING * update

    return body


def update_kernel(base, pick, spread, r2, r3, after, half, *tiles):
    tile = r2.shape[0]
    after[...] = base[...] + DAMPING * product(spread[:, 2 * tile :], stacked(r2, r3))
    half[...] = after[...].astype(HALF)
    picked(pick, half, tiles)


def last_update_kernel(base, spread, r2, r3, far, after, sems):
    tile = r2.shape[0]
    pieces = sems.shape[0]
    height = after.shape[0] // pieces
    returned = stacked(r2, r3)
    stores = []
    for i in range(pieces):
        at = slice(i * height, (i + 1) * height)
        after[at, :] = base[at, :] + DAMPING * product(spread[at, 2 * tile :], returned)
        stores.append(pltpu.make_async_copy(after.at[at], far.at[at], sems.at[i]))
        stores[-1].start()
    for store in stores:
        store.wait()


def rim_kernel(matrix, partial, g2, g3, *tiles):
    tile = g2.shape[0]
    own = matrix.shape[1] - 4 * tile
    ghosts = stacked(g2, g3)
    for d in range(4):
        at = slice(own + d * tile, own + (d + 1) * tile)
        tiles[d][...] = (partial[at, :] + product(matrix[at, own + 2 * tile :], ghosts)).astype(HALF)


def remainder_kernel(target, matrix, partial, g2, g3, spread, r0, r1, out):
    own, tile = target.shape[0], g2.shape[0]
    image = (
        partial[:own, :]
        + product(matrix[:own, own + 2 * tile :], stacked(g2, g3))
        + product(spread[:, : 2 * tile], stacked(r0, r1))
    )
    out[...] = target[...] - image


def residual_kernel(remainder, pick, spread, r2, r3, half, *tiles):
    tile = r2.shape[0]
    half[...] = (remainder[...] - product(spread[:, 2 * tile :], stacked(r2, r3))).astype(HALF)
    picked(pick, half, tiles)


def partner(place, exchange):
    odd = place % 2 if isinstance(place, int) else lax.rem(place, 2)
    return place + 1 - 2 * odd if exchange == 0 else place - 1 + 2 * odd


def swapped(shard, axis, exchange):
    devices = lax.axis_size(axis)
    pairs = [(i, partner(i, exchange)) for i in range(devices)]
    return lax.ppermute(shard, axis, [(i, j) for i, j in pairs if 0 <= j < devices])


def traded_over_row(tiles):
    return tuple(swapped(tiles[i], "row", i) for i in range(2))


def traded(tiles):
    return traded_over_row(tiles) + tuple(swapped(tiles[2 + i], "col", i) for i in range(2))


def per_device(
    right_side, local_operator, local_inverse, coarse_basis, coarse_inverse, send_rows, send_count
):
    target = right_side[0, 0]
    operator = local_operator[0, 0]
    inverse = local_inverse[0, 0]
    basis = jnp.swapaxes(coarse_basis[0, 0], 0, 1)
    rows_list = send_rows[0, 0]
    own, columns = target.shape
    local = operator.shape[0]
    tile = rows_list.shape[1]
    margin = 4 * tile
    coarse = basis.shape[0]
    groups = coarse_inverse.shape[0]
    across = lax.axis_size("col")

    four_tiles = [((tile, columns), HALF)] * 4
    owned_half = ((own, columns), HALF)
    owned_full = ((own, columns), FULL)
    local_full = ((local, columns), FULL)
    target, residual, pick, masked, basis, inverse, *tiles = call(
        select_kernel,
        "select",
        [
            owned_full,
            owned_half,
            ((margin, own), HALF),
            (rows_list.shape, jnp.int32),
            (basis.shape, HALF),
            (inverse.shape, HALF),
        ]
        + four_tiles,
        target,
        rows_list,
        send_count[0],
        basis,
        inverse,
        far=5,
        scratch=(
            pltpu.VMEM(rows_list.shape, jnp.int32),
            pltpu.SMEM((1, 4), jnp.int32),
            pltpu.SemaphoreType.DMA((8 + MATRIX_PIECES,)),
        ),
        flops=2 * margin * own * columns,
    )
    rims = spread = solution = None
    for sweep in range(ITERS):
        first, last = sweep == 0, sweep == ITERS - 1
        if sweep:
            g0, g1, g2, g3 = traded(tiles)
            (partial,) = call(
                near_columns_kernel,
                "operator_near",
                [local_full],
                operator,
                solution_half,
                g0,
                g1,
                flops=2 * local * (own + 2 * tile) * columns,
            )
            tiles = call(
                rim_kernel,
                "operator_rim",
                four_tiles,
                operator,
                partial,
                g2,
                g3,
                flops=4 * margin * tile * columns,
            )
            r0, r1, r2, r3 = traded(tiles)
            (remainder,) = call(
                remainder_kernel,
                "remainder",
                [owned_full],
                target,
                operator,
                partial,
                g2,
                g3,
                spread,
                r0,
                r1,
                flops=8 * own * tile * columns,
            )
            residual, *tiles = call(
                residual_kernel,
                "residual",
                [owned_half] + four_tiles,
                remainder,
                pick,
                spread,
                r2,
                r3,
                flops=(2 * margin + 4 * tile) * own * columns,
            )
        g0, g1 = traded_over_row(tiles)
        (partial,) = call(
            own_columns_kernel,
            "inverse_own",
            [local_full],
            inverse,
            residual,
            flops=2 * local * own * columns,
        )
        (share,) = call(
            share_kernel,
            "share",
            [((2 * tile + coarse * (2 if first else 1), columns), HALF)],
            basis,
            residual,
            tiles[2],
            tiles[3],
            g0,
            g1,
            flops=2 * local * coarse * columns,
        )
        gathered = lax.all_gather(share, "col", axis=0, tiled=True)
        outs = [((groups, coarse, columns), HALF), ((margin, columns), FULL), owned_full]
        parts, rim, inner, *rest = call(
            solve_kernel(first, across),
            "inverse_margin",
            outs + ([((across * coarse, 2 * tile), HALF)] if first else []),
            *([] if first else [rims]),
            inverse,
            partial,
            gathered,
            coarse_inverse,
            g0,
            g1,
            flops=2 * (local * margin + coarse_inverse.size) * columns,
        )
        if first:
            (rims,) = rest
        parts = lax.all_to_all(parts, "row", 0, 0, tiled=True)
        level, *tiles = call(
            coarse_kernel,
            "coarse",
            [((coarse, columns), HALF)] + four_tiles,
            parts,
            basis,
            rim,
            flops=2 * coarse * margin * columns,
        )
        if first:
            masked, tiles = lax.optimization_barrier((masked, tuple(tiles)))
            spread, operator = call(
                spread_kernel,
                "spread",
                [((own, margin), HALF), (operator.shape, HALF)],
                operator,
                masked,
                far=1,
                scratch=(pltpu.SemaphoreType.DMA((MATRIX_PIECES,)),),
            )
        r0, r1, r2, r3 = traded(tiles)
        (base,) = call(
            base_kernel(first),
            "base",
            [owned_full],
            *([] if first else [solution]),
            inner,
            level,
            basis,
            spread,
            r0,
            r1,
            flops=2 * (2 * tile + coarse) * own * columns,
        )
        if last:
            break
        solution, solution_half, *tiles = call(
            update_kernel,
            "update",
            [owned_full, owned_half] + four_tiles,
            base,
            pick,
            spread,
            r2,
            r3,
            flops=(2 * margin + 4 * tile) * own * columns,
        )
    (solution,) = call(
        last_update_kernel,
        "last_update",
        [owned_full],
        base,
        spread,
        r2,
        r3,
        away=True,
        scratch=(pltpu.VMEM((own, columns), FULL), pltpu.SemaphoreType.DMA((4,))),
        flops=4 * tile * own * columns,
    )
    return solution[None, None]


def solution(mesh):
    return jax.shard_map(
        per_device,
        mesh=mesh,
        in_specs=(
            P("row", "col", None, None),
            P("row", "col", None, None),
            P("row", "col", None, None),
            P("row", "col", None, None),
            P(None, "col", "row"),
            P("row", "col", None, None),
            P("row", "col", None),
        ),
        out_specs=P("row", "col", None, None),
        check_vma=False,
    )
```

```python
import jax
import jax.numpy as jnp
from jax import lax
from jax.experimental import pallas as pl
from jax.experimental.pallas import tpu as pltpu
from jax.sharding import PartitionSpec as P

ITERS = 3
DAMPING = 0.5
HALF = jnp.bfloat16
FULL = jnp.float32


def product(left, right):
    return jnp.dot(left, right, preferred_element_type=FULL)


def turned_product(left, right):
    return lax.dot_general(left, right, (((0,), (0,)), ((), ())), preferred_element_type=FULL)


def call(body, name, outs, *args, far=0, away=False, scratch=(), flops=0):
    here = pl.BlockSpec(memory_space=pltpu.VMEM)
    there = pl.BlockSpec(memory_space=pltpu.HBM)
    size = sum(a.size * a.dtype.itemsize for a in args)
    distant = [pltpu.with_memory_space_constraint(a, pltpu.HBM) for a in args[:far]]
    near = [pltpu.with_memory_space_constraint(a, pltpu.VMEM) for a in args[far:]]
    return pl.pallas_call(
        body,
        out_shape=tuple((pltpu.HBM if away else pltpu.VMEM)(*out) for out in outs),
        in_specs=[there] * far + [here] * len(near),
        out_specs=tuple(there if away else here for _ in outs),
        scratch_shapes=list(scratch),
        compiler_params=pltpu.CompilerParams(vmem_limit_bytes=24 * 1024 * 1024),
        cost_estimate=pl.CostEstimate(flops=flops, bytes_accessed=size, transcendentals=0),
        name=name,
    )(*distant, *near)


def parities():
    return lax.rem(lax.axis_index("row"), 2), lax.rem(lax.axis_index("col"), 2)


def directions():
    row, col = parities()
    return 1 - row, row, 3 - col, 2 + col


def margin_spans(own, tile):
    return [
        (pl.ds(pl.multiple_of(own + d * tile, tile), tile), slice(own + i * tile, own + (i + 1) * tile))
        for i, d in enumerate(directions())
    ]


def matrix_pieces(far, near, own, tile):
    margins = margin_spans(own, tile)
    half = own // 2
    rows = [(slice(0, half), slice(0, half)), (slice(half, own), slice(half, own))] + margins
    columns = [(slice(0, own), slice(0, own))] + margins
    return [(far.at[fr, fc], near.at[nr, nc]) for fr, nr in rows for fc, nc in columns]


MATRIX_PIECES = 30


def started(pairs, sems):
    loads = [pltpu.make_async_copy(far, near, sems.at[i]) for i, (far, near) in enumerate(pairs)]
    for load in loads:
        load.start()
    return loads


def select_kernel(
    far_target, far_rows, far_counts, far_basis, far_inverse, target, half, pick, masked, basis, inverse, *rest
):
    *tiles, rows, counts, sems = rest
    own = target.shape[0]
    tile = rows.shape[1]
    pairs = [(far_rows, rows), (far_counts, counts), (far_target, target)]
    pairs += [
        (far_basis.at[:, far], basis.at[:, near])
        for far, near in [(slice(0, own), slice(0, own))] + margin_spans(own, tile)
    ]
    pairs += matrix_pieces(far_inverse, inverse, own, tile)
    loads = started(pairs, sems)
    loads[0].wait()
    loads[1].wait()
    listed = [
        jnp.where(
            lax.broadcasted_iota(jnp.int32, (1, tile), 1) < counts[0, d], rows[d : d + 1, :], -1
        )
        for d in range(4)
    ]
    row, col = parities()
    ordered = (
        jnp.where(row == 0, listed[1], listed[0]),
        jnp.where(row == 0, listed[0], listed[1]),
        jnp.where(col == 0, listed[3], listed[2]),
        jnp.where(col == 0, listed[2], listed[3]),
    )
    for i, here in enumerate(ordered):
        masked[i : i + 1, :] = here
        down = jnp.transpose(jnp.broadcast_to(here, (tile, tile)))[:, :1]
        pick[i * tile : (i + 1) * tile, :] = (
            lax.broadcasted_iota(jnp.int32, (tile, own), 1) == down
        ).astype(FULL).astype(HALF)
    loads[2].wait()
    half[...] = target[...].astype(HALF)
    picked(pick, half, tiles)
    for load in loads[3:]:
        load.wait()


def picked(pick, half, tiles):
    tile = tiles[0].shape[0]
    for d in range(4):
        tiles[d][...] = product(pick[d * tile : (d + 1) * tile, :], half[...]).astype(HALF)


def spread_kernel(far, masked, spread, matrix, sems):
    own = spread.shape[0]
    tile = masked.shape[1]
    loads = started(matrix_pieces(far, matrix, own, tile), sems)
    for d in range(4):
        wide = jnp.broadcast_to(masked[d : d + 1, :], (own, tile))
        spread[:, d * tile : (d + 1) * tile] = (
            lax.broadcasted_iota(jnp.int32, (own, tile), 0) == wide
        ).astype(FULL).astype(HALF)
    for load in loads:
        load.wait()


def stacked(*parts):
    return jnp.concatenate([part[...] for part in parts], axis=0)


def own_columns_kernel(matrix, owned, out):
    own = owned.shape[0]
    out[...] = product(matrix[:, :own], owned[...])


def near_columns_kernel(matrix, owned, g0, g1, out):
    own = owned.shape[0]
    split = own + 2 * g0.shape[0]
    out[...] = product(matrix[:, :own], owned[...]) + product(matrix[:, own:split], stacked(g0, g1))


def share_kernel(basis, owned, t2, t3, g0, g1, out):
    own, tile, coarse = owned.shape[0], t2.shape[0], basis.shape[0]
    split = own + 2 * tile
    out[:tile, :] = t2[...]
    out[tile : 2 * tile, :] = t3[...]
    out[2 * tile : 2 * tile + coarse, :] = (
        product(basis[:, :own], owned[...]) + product(basis[:, own:split], stacked(g0, g1))
    ).astype(HALF)
    if out.shape[0] > 2 * tile + coarse:
        out[2 * tile + coarse :, : 2 * tile] = basis[:, split:]


def solve_kernel(first, across):
    def body(*refs):
        refs = list(refs)
        rims = None if first else refs.pop(0)
        matrix, partial, gathered, inverse, g0, g1, parts, rim, inner, *rest = refs
        tile, coarse = g0.shape[0], inverse.shape[1]
        own = inner.shape[0]
        stride = gathered.shape[0] // across
        if first:
            (rims,) = rest
            for b in range(across):
                at = b * stride + 2 * tile + coarse
                rims[b * coarse : (b + 1) * coarse, :] = gathered[at : at + coarse, : 2 * tile]
        restricted = []
        for b in range(across):
            here = slice(b * coarse, (b + 1) * coarse)
            at = b * stride + 2 * tile
            total = gathered[at : at + coarse, :].astype(FULL)
            for i in range(2):
                other = partner(b, i)
                if 0 <= other < across:
                    at = other * stride + i * tile
                    total += product(
                        rims[here, i * tile : (i + 1) * tile], gathered[at : at + tile, :]
                    )
            restricted.append(total.astype(HALF))
        restricted = jnp.concatenate(restricted, axis=0)
        for i in range(parts.shape[0]):
            parts[i, :, :] = product(inverse[i, :, :], restricted).astype(HALF)
        ghosts = [g0[...], g1[...]]
        for i in range(2):
            other = partner(lax.axis_index("col"), i)
            there = (other >= 0) & (other < across)
            at = pl.multiple_of(jnp.where(there, other, 0) * stride + i * tile, 32)
            ghost = gathered[pl.ds(at, tile), :]
            ghosts.append(jnp.where(there, ghost, jnp.zeros_like(ghost)))
        ghosts = jnp.concatenate(ghosts, axis=0)
        rim[...] = partial[own:, :] + product(matrix[own:, own:], ghosts)
        inner[...] = partial[:own, :] + product(matrix[:own, own:], ghosts)

    return body


def coarse_kernel(parts, basis, rim, level, *tiles):
    tile = tiles[0].shape[0]
    own = basis.shape[1] - 4 * tile
    total = parts[0, :, :].astype(FULL)
    for i in range(1, parts.shape[0]):
        total += parts[i, :, :].astype(FULL)
    level[...] = total.astype(HALF)
    for d in range(4):
        here = slice(d * tile, (d + 1) * tile)
        there = slice(own + d * tile, own + (d + 1) * tile)
        tiles[d][...] = (rim[here, :] + turned_product(basis[:, there], level[...])).astype(HALF)


def base_kernel(first):
    def body(*refs):
        refs = list(refs)
        before = None if first else refs.pop(0)
        inner, level, basis, spread, r0, r1, out = refs
        own, tile = out.shape[0], r0.shape[0]
        update = (
            inner[...]
            + turned_product(basis[:, :own], level[...])
            + product(spread[:, : 2 * tile], stacked(r0, r1))
        )
        out[...] = DAMPING * update if first else before[...] + DAMPING * update

    return body


def update_kernel(base, pick, spread, r2, r3, after, half, *tiles):
    tile = r2.shape[0]
    after[...] = base[...] + DAMPING * product(spread[:, 2 * tile :], stacked(r2, r3))
    half[...] = after[...].astype(HALF)
    picked(pick, half, tiles)


def last_update_kernel(base, spread, r2, r3, far, after, sems):
    tile = r2.shape[0]
    pieces = sems.shape[0]
    height = after.shape[0] // pieces
    returned = stacked(r2, r3)
    stores = []
    for i in range(pieces):
        at = slice(i * height, (i + 1) * height)
        after[at, :] = base[at, :] + DAMPING * product(spread[at, 2 * tile :], returned)
        stores.append(pltpu.make_async_copy(after.at[at], far.at[at], sems.at[i]))
        stores[-1].start()
    for store in stores:
        store.wait()


def rim_kernel(matrix, partial, g2, g3, *tiles):
    tile = g2.shape[0]
    own = matrix.shape[1] - 4 * tile
    ghosts = stacked(g2, g3)
    for d in range(4):
        at = slice(own + d * tile, own + (d + 1) * tile)
        tiles[d][...] = (partial[at, :] + product(matrix[at, own + 2 * tile :], ghosts)).astype(HALF)


def remainder_kernel(target, matrix, partial, g2, g3, spread, r0, r1, out):
    own, tile = target.shape[0], g2.shape[0]
    image = (
        partial[:own, :]
        + product(matrix[:own, own + 2 * tile :], stacked(g2, g3))
        + product(spread[:, : 2 * tile], stacked(r0, r1))
    )
    out[...] = target[...] - image


def residual_kernel(remainder, pick, spread, r2, r3, half, *tiles):
    tile = r2.shape[0]
    half[...] = (remainder[...] - product(spread[:, 2 * tile :], stacked(r2, r3))).astype(HALF)
    picked(pick, half, tiles)


def partner(place, exchange):
    odd = place % 2 if isinstance(place, int) else lax.rem(place, 2)
    return place + 1 - 2 * odd if exchange == 0 else place - 1 + 2 * odd


def swapped(shard, axis, exchange):
    devices = lax.axis_size(axis)
    pairs = [(i, partner(i, exchange)) for i in range(devices)]
    return lax.ppermute(shard, axis, [(i, j if 0 <= j < devices else i) for i, j in pairs])


def traded_over_row(tiles):
    return tuple(swapped(tiles[i], "row", i) for i in range(2))


def traded(tiles):
    return traded_over_row(tiles) + tuple(swapped(tiles[2 + i], "col", i) for i in range(2))


def per_device(
    right_side, local_operator, local_inverse, coarse_basis, coarse_inverse, send_rows, send_count
):
    target = right_side[0, 0]
    operator = local_operator[0, 0]
    inverse = local_inverse[0, 0]
    basis = jnp.swapaxes(coarse_basis[0, 0], 0, 1)
    rows_list = send_rows[0, 0]
    own, columns = target.shape
    local = operator.shape[0]
    tile = rows_list.shape[1]
    margin = 4 * tile
    coarse = basis.shape[0]
    groups = coarse_inverse.shape[0]
    across = lax.axis_size("col")

    four_tiles = [((tile, columns), HALF)] * 4
    owned_half = ((own, columns), HALF)
    owned_full = ((own, columns), FULL)
    local_full = ((local, columns), FULL)
    target, residual, pick, masked, basis, inverse, *tiles = call(
        select_kernel,
        "select",
        [
            owned_full,
            owned_half,
            ((margin, own), HALF),
            (rows_list.shape, jnp.int32),
            (basis.shape, HALF),
            (inverse.shape, HALF),
        ]
        + four_tiles,
        target,
        rows_list,
        send_count[0],
        basis,
        inverse,
        far=5,
        scratch=(
            pltpu.VMEM(rows_list.shape, jnp.int32),
            pltpu.SMEM((1, 4), jnp.int32),
            pltpu.SemaphoreType.DMA((8 + MATRIX_PIECES,)),
        ),
        flops=2 * margin * own * columns,
    )
    rims = spread = solution = None
    for sweep in range(ITERS):
        first, last = sweep == 0, sweep == ITERS - 1
        if sweep:
            g0, g1, g2, g3 = traded(tiles)
            (partial,) = call(
                near_columns_kernel,
                "operator_near",
                [local_full],
                operator,
                solution_half,
                g0,
                g1,
                flops=2 * local * (own + 2 * tile) * columns,
            )
            tiles = call(
                rim_kernel,
                "operator_rim",
                four_tiles,
                operator,
                partial,
                g2,
                g3,
                flops=4 * margin * tile * columns,
            )
            r0, r1, r2, r3 = traded(tiles)
            (remainder,) = call(
                remainder_kernel,
                "remainder",
                [owned_full],
                target,
                operator,
                partial,
                g2,
                g3,
                spread,
                r0,
                r1,
                flops=8 * own * tile * columns,
            )
            residual, *tiles = call(
                residual_kernel,
                "residual",
                [owned_half] + four_tiles,
                remainder,
                pick,
                spread,
                r2,
                r3,
                flops=(2 * margin + 4 * tile) * own * columns,
            )
        g0, g1 = traded_over_row(tiles)
        (partial,) = call(
            own_columns_kernel,
            "inverse_own",
            [local_full],
            inverse,
            residual,
            flops=2 * local * own * columns,
        )
        (share,) = call(
            share_kernel,
            "share",
            [((2 * tile + coarse * (2 if first else 1), columns), HALF)],
            basis,
            residual,
            tiles[2],
            tiles[3],
            g0,
            g1,
            flops=2 * local * coarse * columns,
        )
        gathered = lax.all_gather(share, "col", axis=0, tiled=True)
        outs = [((groups, coarse, columns), HALF), ((margin, columns), FULL), owned_full]
        parts, rim, inner, *rest = call(
            solve_kernel(first, across),
            "inverse_margin",
            outs + ([((across * coarse, 2 * tile), HALF)] if first else []),
            *([] if first else [rims]),
            inverse,
            partial,
            gathered,
            coarse_inverse,
            g0,
            g1,
            flops=2 * (local * margin + coarse_inverse.size) * columns,
        )
        if first:
            (rims,) = rest
        parts = lax.all_to_all(parts, "row", 0, 0, tiled=True)
        level, *tiles = call(
            coarse_kernel,
            "coarse",
            [((coarse, columns), HALF)] + four_tiles,
            parts,
            basis,
            rim,
            flops=2 * coarse * margin * columns,
        )
        if first:
            masked, tiles = lax.optimization_barrier((masked, tuple(tiles)))
            spread, operator = call(
                spread_kernel,
                "spread",
                [((own, margin), HALF), (operator.shape, HALF)],
                operator,
                masked,
                far=1,
                scratch=(pltpu.SemaphoreType.DMA((MATRIX_PIECES,)),),
            )
        r0, r1, r2, r3 = traded(tiles)
        (base,) = call(
            base_kernel(first),
            "base",
            [owned_full],
            *([] if first else [solution]),
            inner,
            level,
            basis,
            spread,
            r0,
            r1,
            flops=2 * (2 * tile + coarse) * own * columns,
        )
        if last:
            break
        solution, solution_half, *tiles = call(
            update_kernel,
            "update",
            [owned_full, owned_half] + four_tiles,
            base,
            pick,
            spread,
            r2,
            r3,
            flops=(2 * margin + 4 * tile) * own * columns,
        )
    (solution,) = call(
        last_update_kernel,
        "last_update",
        [owned_full],
        base,
        spread,
        r2,
        r3,
        away=True,
        scratch=(pltpu.VMEM((own, columns), FULL), pltpu.SemaphoreType.DMA((4,))),
        flops=4 * tile * own * columns,
    )
    return solution[None, None]


def solution(mesh):
    return jax.shard_map(
        per_device,
        mesh=mesh,
        in_specs=(
            P("row", "col", None, None),
            P("row", "col", None, None),
            P("row", "col", None, None),
            P("row", "col", None, None),
            P(None, "col", "row"),
            P("row", "col", None, None),
            P("row", "col", None),
        ),
        out_specs=P("row", "col", None, None),
        check_vma=False,
    )
```

```python
import jax
import jax.numpy as jnp
from jax import lax
from jax.experimental import pallas as pl
from jax.experimental.pallas import tpu as pltpu
from jax.sharding import PartitionSpec as P

ITERS = 3
DAMPING = 0.5
HALF = jnp.bfloat16
FULL = jnp.float32


def product(left, right):
    return jnp.dot(left, right, preferred_element_type=FULL)


def turned_product(left, right):
    return lax.dot_general(left, right, (((0,), (0,)), ((), ())), preferred_element_type=FULL)


def call(body, name, outs, *args, far=0, away=False, scratch=(), flops=0):
    here = pl.BlockSpec(memory_space=pltpu.VMEM)
    there = pl.BlockSpec(memory_space=pltpu.HBM)
    size = sum(a.size * a.dtype.itemsize for a in args)
    distant = [pltpu.with_memory_space_constraint(a, pltpu.HBM) for a in args[:far]]
    near = [pltpu.with_memory_space_constraint(a, pltpu.VMEM) for a in args[far:]]
    return pl.pallas_call(
        body,
        out_shape=tuple((pltpu.HBM if away else pltpu.VMEM)(*out) for out in outs),
        in_specs=[there] * far + [here] * len(near),
        out_specs=tuple(there if away else here for _ in outs),
        scratch_shapes=list(scratch),
        compiler_params=pltpu.CompilerParams(vmem_limit_bytes=24 * 1024 * 1024),
        cost_estimate=pl.CostEstimate(flops=flops, bytes_accessed=size, transcendentals=0),
        name=name,
    )(*distant, *near)


def parities():
    return lax.rem(lax.axis_index("row"), 2), lax.rem(lax.axis_index("col"), 2)


def directions():
    row, col = parities()
    return 1 - row, row, 3 - col, 2 + col


def margin_spans(own, tile):
    return [
        (pl.ds(pl.multiple_of(own + d * tile, tile), tile), slice(own + i * tile, own + (i + 1) * tile))
        for i, d in enumerate(directions())
    ]


def matrix_pieces(far, near, own, tile):
    margins = margin_spans(own, tile)
    half = own // 2
    rows = [(slice(0, half), slice(0, half)), (slice(half, own), slice(half, own))] + margins
    columns = [(slice(0, own), slice(0, own))] + margins
    return [(far.at[fr, fc], near.at[nr, nc]) for fr, nr in rows for fc, nc in columns]


MATRIX_PIECES = 30


def started(pairs, sems):
    loads = [pltpu.make_async_copy(far, near, sems.at[i]) for i, (far, near) in enumerate(pairs)]
    for load in loads:
        load.start()
    return loads


def select_kernel(
    far_target, far_rows, far_counts, far_basis, far_inverse, target, half, pick, masked, basis, inverse, *rest
):
    *tiles, rows, counts, sems = rest
    own = target.shape[0]
    tile = rows.shape[1]
    pairs = [(far_rows, rows), (far_counts, counts), (far_target, target)]
    pairs += [
        (far_basis.at[:, far], basis.at[:, near])
        for far, near in [(slice(0, own), slice(0, own))] + margin_spans(own, tile)
    ]
    pairs += matrix_pieces(far_inverse, inverse, own, tile)
    loads = started(pairs, sems)
    loads[0].wait()
    loads[1].wait()
    listed = [
        jnp.where(
            lax.broadcasted_iota(jnp.int32, (1, tile), 1) < counts[0, d], rows[d : d + 1, :], -1
        )
        for d in range(4)
    ]
    row, col = parities()
    ordered = (
        jnp.where(row == 0, listed[1], listed[0]),
        jnp.where(row == 0, listed[0], listed[1]),
        jnp.where(col == 0, listed[3], listed[2]),
        jnp.where(col == 0, listed[2], listed[3]),
    )
    for i, here in enumerate(ordered):
        masked[i : i + 1, :] = here
        down = jnp.transpose(jnp.broadcast_to(here, (tile, tile)))[:, :1]
        pick[i * tile : (i + 1) * tile, :] = (
            lax.broadcasted_iota(jnp.int32, (tile, own), 1) == down
        ).astype(FULL).astype(HALF)
    loads[2].wait()
    half[...] = target[...].astype(HALF)
    picked(pick, half, tiles)
    for load in loads[3:]:
        load.wait()


def picked(pick, half, tiles):
    tile = tiles[0].shape[0]
    for d in range(4):
        tiles[d][...] = product(pick[d * tile : (d + 1) * tile, :], half[...]).astype(HALF)


def spread_kernel(far, masked, spread, matrix, sems):
    own = spread.shape[0]
    tile = masked.shape[1]
    loads = started(matrix_pieces(far, matrix, own, tile), sems)
    for d in range(4):
        wide = jnp.broadcast_to(masked[d : d + 1, :], (own, tile))
        spread[:, d * tile : (d + 1) * tile] = (
            lax.broadcasted_iota(jnp.int32, (own, tile), 0) == wide
        ).astype(FULL).astype(HALF)
    for load in loads:
        load.wait()


def stacked(*parts):
    return jnp.concatenate([part[...] for part in parts], axis=0)


def own_columns_kernel(matrix, owned, out):
    own = owned.shape[0]
    out[...] = product(matrix[:, :own], owned[...])


def near_columns_kernel(matrix, owned, g0, g1, out):
    own = owned.shape[0]
    split = own + 2 * g0.shape[0]
    out[...] = product(matrix[:, :own], owned[...]) + product(matrix[:, own:split], stacked(g0, g1))


def share_kernel(basis, owned, t2, t3, g0, g1, out):
    own, tile, coarse = owned.shape[0], t2.shape[0], basis.shape[0]
    split = own + 2 * tile
    out[:tile, :] = t2[...]
    out[tile : 2 * tile, :] = t3[...]
    out[2 * tile : 2 * tile + coarse, :] = (
        product(basis[:, :own], owned[...]) + product(basis[:, own:split], stacked(g0, g1))
    ).astype(HALF)
    if out.shape[0] > 2 * tile + coarse:
        out[2 * tile + coarse :, : 2 * tile] = basis[:, split:]


def solve_kernel(first, across):
    def body(*refs):
        refs = list(refs)
        rims = None if first else refs.pop(0)
        matrix, partial, gathered, inverse, g0, g1, parts, rim, inner, *rest = refs
        tile, coarse = g0.shape[0], inverse.shape[1]
        own = inner.shape[0]
        stride = gathered.shape[0] // across
        if first:
            (rims,) = rest
            for b in range(across):
                at = b * stride + 2 * tile + coarse
                rims[b * coarse : (b + 1) * coarse, :] = gathered[at : at + coarse, : 2 * tile]
        restricted = []
        for b in range(across):
            here = slice(b * coarse, (b + 1) * coarse)
            at = b * stride + 2 * tile
            total = gathered[at : at + coarse, :].astype(FULL)
            for i in range(2):
                other = partner(b, i)
                if 0 <= other < across:
                    at = other * stride + i * tile
                    total += product(
                        rims[here, i * tile : (i + 1) * tile], gathered[at : at + tile, :]
                    )
            restricted.append(total.astype(HALF))
        restricted = jnp.concatenate(restricted, axis=0)
        for i in range(parts.shape[0]):
            parts[i, :, :] = product(inverse[i, :, :], restricted).astype(HALF)
        ghosts = [g0[...], g1[...]]
        for i in range(2):
            other = partner(lax.axis_index("col"), i)
            there = (other >= 0) & (other < across)
            at = pl.multiple_of(jnp.where(there, other, 0) * stride + i * tile, 32)
            ghost = gathered[pl.ds(at, tile), :]
            ghosts.append(jnp.where(there, ghost, jnp.zeros_like(ghost)))
        ghosts = jnp.concatenate(ghosts, axis=0)
        rim[...] = partial[own:, :] + product(matrix[own:, own:], ghosts)
        inner[...] = partial[:own, :] + product(matrix[:own, own:], ghosts)

    return body


def coarse_kernel(parts, basis, rim, level, *tiles):
    tile = tiles[0].shape[0]
    own = basis.shape[1] - 4 * tile
    total = parts[0, :, :].astype(FULL)
    for i in range(1, parts.shape[0]):
        total += parts[i, :, :].astype(FULL)
    level[...] = total.astype(HALF)
    for d in range(4):
        here = slice(d * tile, (d + 1) * tile)
        there = slice(own + d * tile, own + (d + 1) * tile)
        tiles[d][...] = (rim[here, :] + turned_product(basis[:, there], level[...])).astype(HALF)


def base_kernel(first):
    def body(*refs):
        refs = list(refs)
        before = None if first else refs.pop(0)
        inner, level, basis, spread, r0, r1, out = refs
        own, tile = out.shape[0], r0.shape[0]
        update = (
            inner[...]
            + turned_product(basis[:, :own], level[...])
            + product(spread[:, : 2 * tile], stacked(r0, r1))
        )
        out[...] = DAMPING * update if first else before[...] + DAMPING * update

    return body


def update_kernel(base, pick, spread, r2, r3, after, half, *tiles):
    tile = r2.shape[0]
    after[...] = base[...] + DAMPING * product(spread[:, 2 * tile :], stacked(r2, r3))
    half[...] = after[...].astype(HALF)
    picked(pick, half, tiles)


def last_update_kernel(base, spread, r2, r3, far, after, sems):
    tile = r2.shape[0]
    pieces = sems.shape[0]
    height = after.shape[0] // pieces
    returned = stacked(r2, r3)
    stores = []
    for i in range(pieces):
        at = slice(i * height, (i + 1) * height)
        after[at, :] = base[at, :] + DAMPING * product(spread[at, 2 * tile :], returned)
        stores.append(pltpu.make_async_copy(after.at[at], far.at[at], sems.at[i]))
        stores[-1].start()
    for store in stores:
        store.wait()


def rim_kernel(matrix, partial, g2, g3, *tiles):
    tile = g2.shape[0]
    own = matrix.shape[1] - 4 * tile
    ghosts = stacked(g2, g3)
    for d in range(4):
        at = slice(own + d * tile, own + (d + 1) * tile)
        tiles[d][...] = (partial[at, :] + product(matrix[at, own + 2 * tile :], ghosts)).astype(HALF)


def remainder_kernel(target, matrix, partial, g2, g3, spread, r0, r1, out):
    own, tile = target.shape[0], g2.shape[0]
    image = (
        partial[:own, :]
        + product(matrix[:own, own + 2 * tile :], stacked(g2, g3))
        + product(spread[:, : 2 * tile], stacked(r0, r1))
    )
    out[...] = target[...] - image


def residual_kernel(remainder, pick, spread, r2, r3, half, *tiles):
    tile = r2.shape[0]
    half[...] = (remainder[...] - product(spread[:, 2 * tile :], stacked(r2, r3))).astype(HALF)
    picked(pick, half, tiles)


def partner(place, exchange):
    odd = place % 2 if isinstance(place, int) else lax.rem(place, 2)
    return place + 1 - 2 * odd if exchange == 0 else place - 1 + 2 * odd


def swapped(shard, axis, exchange):
    devices = lax.axis_size(axis)
    pairs = [(i, partner(i, exchange)) for i in range(devices)]
    if devices % 2 == 0:
        pairs = [(i, j % devices) for i, j in pairs]
    return lax.ppermute(shard, axis, [(i, j) for i, j in pairs if 0 <= j < devices])


def traded_over_row(tiles):
    return tuple(swapped(tiles[i], "row", i) for i in range(2))


def traded(tiles):
    return traded_over_row(tiles) + tuple(swapped(tiles[2 + i], "col", i) for i in range(2))


def per_device(
    right_side, local_operator, local_inverse, coarse_basis, coarse_inverse, send_rows, send_count
):
    target = right_side[0, 0]
    operator = local_operator[0, 0]
    inverse = local_inverse[0, 0]
    basis = jnp.swapaxes(coarse_basis[0, 0], 0, 1)
    rows_list = send_rows[0, 0]
    own, columns = target.shape
    local = operator.shape[0]
    tile = rows_list.shape[1]
    margin = 4 * tile
    coarse = basis.shape[0]
    groups = coarse_inverse.shape[0]
    across = lax.axis_size("col")

    four_tiles = [((tile, columns), HALF)] * 4
    owned_half = ((own, columns), HALF)
    owned_full = ((own, columns), FULL)
    local_full = ((local, columns), FULL)
    target, residual, pick, masked, basis, inverse, *tiles = call(
        select_kernel,
        "select",
        [
            owned_full,
            owned_half,
            ((margin, own), HALF),
            (rows_list.shape, jnp.int32),
            (basis.shape, HALF),
            (inverse.shape, HALF),
        ]
        + four_tiles,
        target,
        rows_list,
        send_count[0],
        basis,
        inverse,
        far=5,
        scratch=(
            pltpu.VMEM(rows_list.shape, jnp.int32),
            pltpu.SMEM((1, 4), jnp.int32),
            pltpu.SemaphoreType.DMA((8 + MATRIX_PIECES,)),
        ),
        flops=2 * margin * own * columns,
    )
    rims = spread = solution = None
    for sweep in range(ITERS):
        first, last = sweep == 0, sweep == ITERS - 1
        if sweep:
            g0, g1, g2, g3 = traded(tiles)
            (partial,) = call(
                near_columns_kernel,
                "operator_near",
                [local_full],
                operator,
                solution_half,
                g0,
                g1,
                flops=2 * local * (own + 2 * tile) * columns,
            )
            tiles = call(
                rim_kernel,
                "operator_rim",
                four_tiles,
                operator,
                partial,
                g2,
                g3,
                flops=4 * margin * tile * columns,
            )
            r0, r1, r2, r3 = traded(tiles)
            (remainder,) = call(
                remainder_kernel,
                "remainder",
                [owned_full],
                target,
                operator,
                partial,
                g2,
                g3,
                spread,
                r0,
                r1,
                flops=8 * own * tile * columns,
            )
            residual, *tiles = call(
                residual_kernel,
                "residual",
                [owned_half] + four_tiles,
                remainder,
                pick,
                spread,
                r2,
                r3,
                flops=(2 * margin + 4 * tile) * own * columns,
            )
        g0, g1 = traded_over_row(tiles)
        (partial,) = call(
            own_columns_kernel,
            "inverse_own",
            [local_full],
            inverse,
            residual,
            flops=2 * local * own * columns,
        )
        (share,) = call(
            share_kernel,
            "share",
            [((2 * tile + coarse * (2 if first else 1), columns), HALF)],
            basis,
            residual,
            tiles[2],
            tiles[3],
            g0,
            g1,
            flops=2 * local * coarse * columns,
        )
        gathered = lax.all_gather(share, "col", axis=0, tiled=True)
        outs = [((groups, coarse, columns), HALF), ((margin, columns), FULL), owned_full]
        parts, rim, inner, *rest = call(
            solve_kernel(first, across),
            "inverse_margin",
            outs + ([((across * coarse, 2 * tile), HALF)] if first else []),
            *([] if first else [rims]),
            inverse,
            partial,
            gathered,
            coarse_inverse,
            g0,
            g1,
            flops=2 * (local * margin + coarse_inverse.size) * columns,
        )
        if first:
            (rims,) = rest
        parts = lax.all_to_all(parts, "row", 0, 0, tiled=True)
        level, *tiles = call(
            coarse_kernel,
            "coarse",
            [((coarse, columns), HALF)] + four_tiles,
            parts,
            basis,
            rim,
            flops=2 * coarse * margin * columns,
        )
        if first:
            masked, tiles = lax.optimization_barrier((masked, tuple(tiles)))
            spread, operator = call(
                spread_kernel,
                "spread",
                [((own, margin), HALF), (operator.shape, HALF)],
                operator,
                masked,
                far=1,
                scratch=(pltpu.SemaphoreType.DMA((MATRIX_PIECES,)),),
            )
        r0, r1, r2, r3 = traded(tiles)
        (base,) = call(
            base_kernel(first),
            "base",
            [owned_full],
            *([] if first else [solution]),
            inner,
            level,
            basis,
            spread,
            r0,
            r1,
            flops=2 * (2 * tile + coarse) * own * columns,
        )
        if last:
            break
        solution, solution_half, *tiles = call(
            update_kernel,
            "update",
            [owned_full, owned_half] + four_tiles,
            base,
            pick,
            spread,
            r2,
            r3,
            flops=(2 * margin + 4 * tile) * own * columns,
        )
    (solution,) = call(
        last_update_kernel,
        "last_update",
        [owned_full],
        base,
        spread,
        r2,
        r3,
        away=True,
        scratch=(pltpu.VMEM((own, columns), FULL), pltpu.SemaphoreType.DMA((4,))),
        flops=4 * tile * own * columns,
    )
    return solution[None, None]


def solution(mesh):
    return jax.shard_map(
        per_device,
        mesh=mesh,
        in_specs=(
            P("row", "col", None, None),
            P("row", "col", None, None),
            P("row", "col", None, None),
            P("row", "col", None, None),
            P(None, "col", "row"),
            P("row", "col", None, None),
            P("row", "col", None),
        ),
        out_specs=P("row", "col", None, None),
        check_vma=False,
    )
```

```python
import jax
import jax.numpy as jnp
from jax import lax
from jax.experimental import pallas as pl
from jax.experimental.pallas import tpu as pltpu
from jax.sharding import PartitionSpec as P

ITERS = 3
DAMPING = 0.5
HALF = jnp.bfloat16
FULL = jnp.float32


def product(left, right):
    return jnp.dot(left, right, preferred_element_type=FULL)


def turned_product(left, right):
    return lax.dot_general(left, right, (((0,), (0,)), ((), ())), preferred_element_type=FULL)


def call(body, name, outs, *args, far=0, away=False, scratch=(), flops=0):
    here = pl.BlockSpec(memory_space=pltpu.VMEM)
    there = pl.BlockSpec(memory_space=pltpu.HBM)
    size = sum(a.size * a.dtype.itemsize for a in args)
    distant = [pltpu.with_memory_space_constraint(a, pltpu.HBM) for a in args[:far]]
    near = [pltpu.with_memory_space_constraint(a, pltpu.VMEM) for a in args[far:]]
    return pl.pallas_call(
        body,
        out_shape=tuple((pltpu.HBM if away else pltpu.VMEM)(*out) for out in outs),
        in_specs=[there] * far + [here] * len(near),
        out_specs=tuple(there if away else here for _ in outs),
        scratch_shapes=list(scratch),
        compiler_params=pltpu.CompilerParams(vmem_limit_bytes=24 * 1024 * 1024),
        cost_estimate=pl.CostEstimate(flops=flops, bytes_accessed=size, transcendentals=0),
        name=name,
    )(*distant, *near)


def parities():
    return lax.rem(lax.axis_index("row"), 2), lax.rem(lax.axis_index("col"), 2)


def directions():
    row, col = parities()
    return 1 - row, row, 3 - col, 2 + col


def margin_spans(own, tile):
    return [
        (pl.ds(pl.multiple_of(own + d * tile, tile), tile), slice(own + i * tile, own + (i + 1) * tile))
        for i, d in enumerate(directions())
    ]


def matrix_pieces(far, near, own, tile):
    margins = margin_spans(own, tile)
    half = own // 2
    rows = [(slice(0, half), slice(0, half)), (slice(half, own), slice(half, own))] + margins
    columns = [(slice(0, own), slice(0, own))] + margins
    return [(far.at[fr, fc], near.at[nr, nc]) for fr, nr in rows for fc, nc in columns]


MATRIX_PIECES = 30


def started(pairs, sems):
    loads = [pltpu.make_async_copy(far, near, sems.at[i]) for i, (far, near) in enumerate(pairs)]
    for load in loads:
        load.start()
    return loads


def select_kernel(
    far_target, far_rows, far_counts, far_basis, target, half, pick, masked, basis, *rest
):
    *tiles, rows, counts, sems = rest
    own = target.shape[0]
    tile = rows.shape[1]
    pairs = [(far_rows, rows), (far_counts, counts), (far_target, target)]
    pairs += [
        (far_basis.at[:, far], basis.at[:, near])
        for far, near in [(slice(0, own), slice(0, own))] + margin_spans(own, tile)
    ]
    loads = started(pairs, sems)
    loads[0].wait()
    loads[1].wait()
    listed = [
        jnp.where(
            lax.broadcasted_iota(jnp.int32, (1, tile), 1) < counts[0, d], rows[d : d + 1, :], -1
        )
        for d in range(4)
    ]
    row, col = parities()
    ordered = (
        jnp.where(row == 0, listed[1], listed[0]),
        jnp.where(row == 0, listed[0], listed[1]),
        jnp.where(col == 0, listed[3], listed[2]),
        jnp.where(col == 0, listed[2], listed[3]),
    )
    for i, here in enumerate(ordered):
        masked[i : i + 1, :] = here
        down = jnp.transpose(jnp.broadcast_to(here, (tile, tile)))[:, :1]
        pick[i * tile : (i + 1) * tile, :] = (
            lax.broadcasted_iota(jnp.int32, (tile, own), 1) == down
        ).astype(FULL).astype(HALF)
    loads[2].wait()
    half[...] = target[...].astype(HALF)
    picked(pick, half, tiles)
    for load in loads[3:]:
        load.wait()


def picked(pick, half, tiles):
    tile = tiles[0].shape[0]
    for d in range(4):
        tiles[d][...] = product(pick[d * tile : (d + 1) * tile, :], half[...]).astype(HALF)


def spread_kernel(far, masked, spread, matrix, sems):
    own = spread.shape[0]
    tile = masked.shape[1]
    loads = started(matrix_pieces(far, matrix, own, tile), sems)
    for d in range(4):
        wide = jnp.broadcast_to(masked[d : d + 1, :], (own, tile))
        spread[:, d * tile : (d + 1) * tile] = (
            lax.broadcasted_iota(jnp.int32, (own, tile), 0) == wide
        ).astype(FULL).astype(HALF)
    for load in loads:
        load.wait()


def stacked(*parts):
    return jnp.concatenate([part[...] for part in parts], axis=0)


def load_kernel(far, owned, matrix, sems):
    own = owned.shape[0]
    tile = (matrix.shape[0] - own) // 4
    for load in started(matrix_pieces(far, matrix, own, tile), sems):
        load.wait()


def near_columns_kernel(matrix, owned, g0, g1, out):
    own = owned.shape[0]
    split = own + 2 * g0.shape[0]
    out[...] = product(matrix[:, :own], owned[...]) + product(matrix[:, own:split], stacked(g0, g1))


def near_solve_kernel(matrix, basis, owned, g0, g1, out, restricted):
    own = owned.shape[0]
    split = own + 2 * g0.shape[0]
    ghosts = stacked(g0, g1)
    out[...] = product(matrix[:, :own], owned[...]) + product(matrix[:, own:split], ghosts)
    restricted[...] = product(basis[:, :own], owned[...]) + product(basis[:, own:split], ghosts)


def restrict_kernel(basis, near, g2, g3, out):
    split = basis.shape[1] - 2 * g2.shape[0]
    out[...] = (near[...] + product(basis[:, split:], stacked(g2, g3))).astype(HALF)


def solve_kernel(matrix, partial, g2, g3, rim, inner):
    own = inner.shape[0]
    ghosts = stacked(g2, g3)
    split = matrix.shape[1] - ghosts.shape[0]
    rim[...] = partial[own:, :] + product(matrix[own:, split:], ghosts)
    inner[...] = partial[:own, :] + product(matrix[:own, split:], ghosts)


def met(place, turn, devices):
    if devices & (devices - 1) == 0:
        return place ^ turn
    return (turn + devices - place) % devices


def meeting(shard, axis, turn):
    devices = lax.axis_size(axis)
    pairs = [(i, met(i, turn, devices)) for i in range(devices)]
    return shard if all(i == j for i, j in pairs) else lax.ppermute(shard, axis, pairs)


def parts_kernel(groups, across):
    def body(inverse, *refs):
        restricted, parts, gathered = refs[:across], refs[across:-1], refs[-1]
        coarse = inverse.shape[1]
        for turn, piece in enumerate(restricted):
            at = pl.multiple_of(met(lax.axis_index("col"), turn, across) * coarse, coarse)
            gathered[pl.ds(at, coarse), :] = piece[...]
        for turn, part in enumerate(parts):
            other = met(lax.axis_index("row"), turn, groups)
            part[...] = product(inverse[other], gathered[...]).astype(HALF)

    return body


def coarse_kernel(groups):
    def body(*refs):
        parts, (basis, rim, level, *tiles) = refs[:groups], refs[groups:]
        tile = tiles[0].shape[0]
        own = basis.shape[1] - 4 * tile
        total = parts[0][...].astype(FULL)
        for part in parts[1:]:
            total += part[...].astype(FULL)
        level[...] = total.astype(HALF)
        for d in range(4):
            here = slice(d * tile, (d + 1) * tile)
            there = slice(own + d * tile, own + (d + 1) * tile)
            tiles[d][...] = (
                rim[here, :] + turned_product(basis[:, there], level[...])
            ).astype(HALF)

    return body


def base_kernel(first):
    def body(*refs):
        refs = list(refs)
        before = None if first else refs.pop(0)
        inner, level, basis, spread, r0, r1, out = refs
        own, tile = out.shape[0], r0.shape[0]
        update = (
            inner[...]
            + turned_product(basis[:, :own], level[...])
            + product(spread[:, : 2 * tile], stacked(r0, r1))
        )
        out[...] = DAMPING * update if first else before[...] + DAMPING * update

    return body


def update_kernel(base, pick, spread, r2, r3, after, half, *tiles):
    tile = r2.shape[0]
    after[...] = base[...] + DAMPING * product(spread[:, 2 * tile :], stacked(r2, r3))
    half[...] = after[...].astype(HALF)
    picked(pick, half, tiles)


def last_update_kernel(base, spread, r2, r3, far, after, sems):
    tile = r2.shape[0]
    pieces = sems.shape[0]
    height = after.shape[0] // pieces
    returned = stacked(r2, r3)
    stores = []
    for i in range(pieces):
        at = slice(i * height, (i + 1) * height)
        after[at, :] = base[at, :] + DAMPING * product(spread[at, 2 * tile :], returned)
        stores.append(pltpu.make_async_copy(after.at[at], far.at[at], sems.at[i]))
        stores[-1].start()
    for store in stores:
        store.wait()


def rim_kernel(matrix, partial, g2, g3, *tiles):
    tile = g2.shape[0]
    own = matrix.shape[1] - 4 * tile
    ghosts = stacked(g2, g3)
    for d in range(4):
        at = slice(own + d * tile, own + (d + 1) * tile)
        tiles[d][...] = (partial[at, :] + product(matrix[at, own + 2 * tile :], ghosts)).astype(HALF)


def remainder_kernel(target, matrix, partial, g2, g3, spread, r0, r1, out):
    own, tile = target.shape[0], g2.shape[0]
    image = (
        partial[:own, :]
        + product(matrix[:own, own + 2 * tile :], stacked(g2, g3))
        + product(spread[:, : 2 * tile], stacked(r0, r1))
    )
    out[...] = target[...] - image


def residual_kernel(remainder, pick, spread, r2, r3, half, *tiles):
    tile = r2.shape[0]
    half[...] = (remainder[...] - product(spread[:, 2 * tile :], stacked(r2, r3))).astype(HALF)
    picked(pick, half, tiles)


def partner(place, exchange):
    odd = place % 2 if isinstance(place, int) else lax.rem(place, 2)
    return place + 1 - 2 * odd if exchange == 0 else place - 1 + 2 * odd


def swapped(shard, axis, exchange):
    devices = lax.axis_size(axis)
    pairs = [(i, partner(i, exchange)) for i in range(devices)]
    if devices % 2 == 0:
        pairs = [(i, j % devices) for i, j in pairs]
    return lax.ppermute(shard, axis, [(i, j) for i, j in pairs if 0 <= j < devices])


def traded(tiles):
    return tuple(swapped(tiles[i], "row" if i < 2 else "col", i % 2) for i in range(4))


def per_device(
    right_side, local_operator, local_inverse, coarse_basis, coarse_inverse, send_rows, send_count
):
    target = right_side[0, 0]
    operator = local_operator[0, 0]
    inverse = local_inverse[0, 0]
    basis = jnp.swapaxes(coarse_basis[0, 0], 0, 1)
    rows_list = send_rows[0, 0]
    own, columns = target.shape
    local = operator.shape[0]
    tile = rows_list.shape[1]
    margin = 4 * tile
    coarse = basis.shape[0]
    groups = coarse_inverse.shape[0]
    across = lax.axis_size("col")

    four_tiles = [((tile, columns), HALF)] * 4
    owned_half = ((own, columns), HALF)
    owned_full = ((own, columns), FULL)
    local_full = ((local, columns), FULL)
    target, residual, pick, masked, basis, *tiles = call(
        select_kernel,
        "select",
        [
            owned_full,
            owned_half,
            ((margin, own), HALF),
            (rows_list.shape, jnp.int32),
            (basis.shape, HALF),
        ]
        + four_tiles,
        target,
        rows_list,
        send_count[0],
        basis,
        far=4,
        scratch=(
            pltpu.VMEM(rows_list.shape, jnp.int32),
            pltpu.SMEM((1, 4), jnp.int32),
            pltpu.SemaphoreType.DMA((8,)),
        ),
        flops=2 * margin * own * columns,
    )
    spread = solution = None
    for sweep in range(ITERS):
        first, last = sweep == 0, sweep == ITERS - 1
        if sweep:
            g0, g1, g2, g3 = traded(tiles)
            (partial,) = call(
                near_columns_kernel,
                "operator_near",
                [local_full],
                operator,
                solution_half,
                g0,
                g1,
                flops=2 * local * (own + 2 * tile) * columns,
            )
            tiles = call(
                rim_kernel,
                "operator_rim",
                four_tiles,
                operator,
                partial,
                g2,
                g3,
                flops=4 * margin * tile * columns,
            )
            r0, r1, r2, r3 = traded(tiles)
            (remainder,) = call(
                remainder_kernel,
                "remainder",
                [owned_full],
                target,
                operator,
                partial,
                g2,
                g3,
                spread,
                r0,
                r1,
                flops=8 * own * tile * columns,
            )
            residual, *tiles = call(
                residual_kernel,
                "residual",
                [owned_half] + four_tiles,
                remainder,
                pick,
                spread,
                r2,
                r3,
                flops=(2 * margin + 4 * tile) * own * columns,
            )
        if first:
            residual, tiles = lax.optimization_barrier((residual, tuple(tiles)))
            (inverse,) = call(
                load_kernel,
                "load",
                [(inverse.shape, HALF)],
                inverse,
                residual,
                far=1,
                scratch=(pltpu.SemaphoreType.DMA((MATRIX_PIECES,)),),
            )
        g0, g1, g2, g3 = traded(tiles)
        partial, near = call(
            near_solve_kernel,
            "inverse_near",
            [local_full, ((coarse, columns), FULL)],
            inverse,
            basis,
            residual,
            g0,
            g1,
            flops=2 * (local + coarse) * (own + 2 * tile) * columns,
        )
        (restricted,) = call(
            restrict_kernel,
            "restrict",
            [((coarse, columns), HALF)],
            basis,
            near,
            g2,
            g3,
            flops=4 * coarse * tile * columns,
        )
        restricted = [meeting(restricted, "col", turn) for turn in reversed(range(across))][::-1]
        rim, inner = call(
            solve_kernel,
            "inverse_margin",
            [((margin, columns), FULL), owned_full],
            inverse,
            partial,
            g2,
            g3,
            flops=4 * local * tile * columns,
        )
        parts = call(
            parts_kernel(groups, across),
            "coarse_part",
            [((coarse, columns), HALF)] * groups,
            coarse_inverse,
            *restricted,
            scratch=(pltpu.VMEM((across * coarse, columns), HALF),),
            flops=2 * coarse_inverse.size * columns,
        )
        parts = [meeting(parts[turn], "row", turn) for turn in reversed(range(groups))]
        level, *tiles = call(
            coarse_kernel(groups),
            "coarse",
            [((coarse, columns), HALF)] + four_tiles,
            *parts,
            basis,
            rim,
            flops=2 * coarse * margin * columns,
        )
        if first:
            masked, tiles = lax.optimization_barrier((masked, tuple(tiles)))
            spread, operator = call(
                spread_kernel,
                "spread",
                [((own, margin), HALF), (operator.shape, HALF)],
                operator,
                masked,
                far=1,
                scratch=(pltpu.SemaphoreType.DMA((MATRIX_PIECES,)),),
            )
        r0, r1, r2, r3 = traded(tiles)
        (base,) = call(
            base_kernel(first),
            "base",
            [owned_full],
            *([] if first else [solution]),
            inner,
            level,
            basis,
            spread,
            r0,
            r1,
            flops=2 * (2 * tile + coarse) * own * columns,
        )
        if last:
            break
        solution, solution_half, *tiles = call(
            update_kernel,
            "update",
            [owned_full, owned_half] + four_tiles,
            base,
            pick,
            spread,
            r2,
            r3,
            flops=(2 * margin + 4 * tile) * own * columns,
        )
    (solution,) = call(
        last_update_kernel,
        "last_update",
        [owned_full],
        base,
        spread,
        r2,
        r3,
        away=True,
        scratch=(pltpu.VMEM((own, columns), FULL), pltpu.SemaphoreType.DMA((4,))),
        flops=4 * tile * own * columns,
    )
    return solution[None, None]


def solution(mesh):
    return jax.shard_map(
        per_device,
        mesh=mesh,
        in_specs=(
            P("row", "col", None, None),
            P("row", "col", None, None),
            P("row", "col", None, None),
            P("row", "col", None, None),
            P(None, "col", "row"),
            P("row", "col", None, None),
            P("row", "col", None),
        ),
        out_specs=P("row", "col", None, None),
        check_vma=False,
    )
```

```python
import jax
import jax.numpy as jnp
from jax import lax
from jax.experimental import pallas as pl
from jax.experimental.pallas import tpu as pltpu
from jax.sharding import PartitionSpec as P

ITERS = 3
DAMPING = 0.5
HALF = jnp.bfloat16
FULL = jnp.float32


def product(left, right):
    return jnp.dot(left, right, preferred_element_type=FULL)


def turned_product(left, right):
    return lax.dot_general(left, right, (((0,), (0,)), ((), ())), preferred_element_type=FULL)


def call(body, name, outs, *args, far=0, away=False, scratch=(), flops=0):
    here = pl.BlockSpec(memory_space=pltpu.VMEM)
    there = pl.BlockSpec(memory_space=pltpu.HBM)
    size = sum(a.size * a.dtype.itemsize for a in args)
    distant = [pltpu.with_memory_space_constraint(a, pltpu.HBM) for a in args[:far]]
    near = [pltpu.with_memory_space_constraint(a, pltpu.VMEM) for a in args[far:]]
    return pl.pallas_call(
        body,
        out_shape=tuple((pltpu.HBM if away else pltpu.VMEM)(*out) for out in outs),
        in_specs=[there] * far + [here] * len(near),
        out_specs=tuple(there if away else here for _ in outs),
        scratch_shapes=list(scratch),
        compiler_params=pltpu.CompilerParams(vmem_limit_bytes=24 * 1024 * 1024),
        cost_estimate=pl.CostEstimate(flops=flops, bytes_accessed=size, transcendentals=0),
        name=name,
    )(*distant, *near)


def parities():
    return lax.rem(lax.axis_index("row"), 2), lax.rem(lax.axis_index("col"), 2)


def directions():
    row, col = parities()
    return 1 - row, row, 3 - col, 2 + col


def margin_spans(own, tile):
    return [
        (pl.ds(pl.multiple_of(own + d * tile, tile), tile), slice(own + i * tile, own + (i + 1) * tile))
        for i, d in enumerate(directions())
    ]


def matrix_pieces(far, near, own, tile):
    margins = margin_spans(own, tile)
    half = own // 2
    rows = [(slice(0, half), slice(0, half)), (slice(half, own), slice(half, own))] + margins
    columns = [(slice(0, own), slice(0, own))] + margins
    return [(far.at[fr, fc], near.at[nr, nc]) for fr, nr in rows for fc, nc in columns]


MATRIX_PIECES = 30


def started(pairs, sems):
    loads = [pltpu.make_async_copy(far, near, sems.at[i]) for i, (far, near) in enumerate(pairs)]
    for load in loads:
        load.start()
    return loads


def select_kernel(
    far_target, far_rows, far_counts, far_basis, target, half, pick, masked, basis, *rest
):
    *tiles, rows, counts, sems = rest
    own = target.shape[0]
    tile = rows.shape[1]
    pairs = [(far_rows, rows), (far_counts, counts), (far_target, target)]
    pairs += [
        (far_basis.at[:, far], basis.at[:, near])
        for far, near in [(slice(0, own), slice(0, own))] + margin_spans(own, tile)
    ]
    loads = started(pairs, sems)
    loads[0].wait()
    loads[1].wait()
    listed = [
        jnp.where(
            lax.broadcasted_iota(jnp.int32, (1, tile), 1) < counts[0, d], rows[d : d + 1, :], -1
        )
        for d in range(4)
    ]
    row, col = parities()
    ordered = (
        jnp.where(row == 0, listed[1], listed[0]),
        jnp.where(row == 0, listed[0], listed[1]),
        jnp.where(col == 0, listed[3], listed[2]),
        jnp.where(col == 0, listed[2], listed[3]),
    )
    for i, here in enumerate(ordered):
        masked[i : i + 1, :] = here
        down = jnp.transpose(jnp.broadcast_to(here, (tile, tile)))[:, :1]
        pick[i * tile : (i + 1) * tile, :] = (
            lax.broadcasted_iota(jnp.int32, (tile, own), 1) == down
        ).astype(FULL).astype(HALF)
    loads[2].wait()
    half[...] = target[...].astype(HALF)
    picked(pick, half, tiles)
    for load in loads[3:]:
        load.wait()


def picked(pick, half, tiles):
    tile = tiles[0].shape[0]
    for d in range(4):
        tiles[d][...] = product(pick[d * tile : (d + 1) * tile, :], half[...]).astype(HALF)


def spread_kernel(far, masked, spread, matrix, sems):
    own = spread.shape[0]
    tile = masked.shape[1]
    loads = started(matrix_pieces(far, matrix, own, tile), sems)
    for d in range(4):
        wide = jnp.broadcast_to(masked[d : d + 1, :], (own, tile))
        spread[:, d * tile : (d + 1) * tile] = (
            lax.broadcasted_iota(jnp.int32, (own, tile), 0) == wide
        ).astype(FULL).astype(HALF)
    for load in loads:
        load.wait()


def stacked(*parts):
    return jnp.concatenate([part[...] for part in parts], axis=0)


def load_kernel(far, owned, matrix, out, sems):
    own = owned.shape[0]
    tile = (matrix.shape[0] - own) // 4
    for load in started(matrix_pieces(far, matrix, own, tile), sems):
        load.wait()
    out[...] = product(matrix[:, :own], owned[...])


def own_columns_kernel(matrix, owned, out):
    own = owned.shape[0]
    out[...] = product(matrix[:, :own], owned[...])


def restrict_kernel(basis, owned, g0, g1, g2, g3, out):
    own = owned.shape[0]
    out[...] = (
        product(basis[:, :own], owned[...]) + product(basis[:, own:], stacked(g0, g1, g2, g3))
    ).astype(HALF)


def solve_kernel(matrix, partial, g0, g1, g2, g3, rim, inner):
    own = inner.shape[0]
    ghosts = stacked(g0, g1, g2, g3)
    rim[...] = partial[own:, :] + product(matrix[own:, own:], ghosts)
    inner[...] = partial[:own, :] + product(matrix[:own, own:], ghosts)


def met(place, turn, devices):
    if devices & (devices - 1) == 0:
        return place ^ turn
    return (turn + devices - place) % devices


def meeting(shard, axis, turn, block=1):
    devices = lax.axis_size(axis)
    pairs = [
        (i, met(i // block, turn, devices // block) * block + i % block) for i in range(devices)
    ]
    return shard if all(i == j for i, j in pairs) else lax.ppermute(shard, axis, pairs)


def parts_kernel(groups, across):
    def body(inverse, *refs):
        restricted, parts, gathered = refs[:across], refs[across:-1], refs[-1]
        coarse = inverse.shape[1]
        for turn, piece in enumerate(restricted):
            at = pl.multiple_of(met(lax.axis_index("col"), turn, across) * coarse, coarse)
            gathered[pl.ds(at, coarse), :] = piece[...]
        pair = lax.axis_index("row") // 2
        for turn, part in enumerate(parts):
            other = 2 * met(pair, turn, groups // 2)
            for i in range(2):
                part[i * coarse : (i + 1) * coarse, :] = product(
                    inverse[other + i], gathered[...]
                ).astype(HALF)

    return body


def pair_kernel(*refs):
    *parts, mine, others = refs
    coarse = mine.shape[0]
    total = parts[0][...].astype(FULL)
    for part in parts[1:]:
        total += part[...].astype(FULL)
    odd = lax.rem(lax.axis_index("row"), 2) == 1
    low, high = total[:coarse, :], total[coarse:, :]
    mine[...] = jnp.where(odd, high, low)
    others[...] = jnp.where(odd, low, high).astype(HALF)


def coarse_kernel(mine, theirs, basis, rim, level, *tiles):
    tile = tiles[0].shape[0]
    own = basis.shape[1] - 4 * tile
    level[...] = (mine[...] + theirs[...].astype(FULL)).astype(HALF)
    for d in range(4):
        here = slice(d * tile, (d + 1) * tile)
        there = slice(own + d * tile, own + (d + 1) * tile)
        tiles[d][...] = (rim[here, :] + turned_product(basis[:, there], level[...])).astype(HALF)


def base_kernel(first):
    def body(*refs):
        refs = list(refs)
        before = None if first else refs.pop(0)
        inner, level, basis, out = refs
        own = out.shape[0]
        update = inner[...] + turned_product(basis[:, :own], level[...])
        out[...] = DAMPING * update if first else before[...] + DAMPING * update

    return body


def update_kernel(base, pick, spread, r0, r1, r2, r3, after, half, *tiles):
    after[...] = base[...] + DAMPING * product(spread[...], stacked(r0, r1, r2, r3))
    half[...] = after[...].astype(HALF)
    picked(pick, half, tiles)


def last_update_kernel(base, spread, r0, r1, r2, r3, far, after, sems):
    pieces = sems.shape[0]
    height = after.shape[0] // pieces
    returned = stacked(r0, r1, r2, r3)
    stores = []
    for i in range(pieces):
        at = slice(i * height, (i + 1) * height)
        after[at, :] = base[at, :] + DAMPING * product(spread[at, :], returned)
        stores.append(pltpu.make_async_copy(after.at[at], far.at[at], sems.at[i]))
        stores[-1].start()
    for store in stores:
        store.wait()


def rim_kernel(matrix, partial, g0, g1, g2, g3, *tiles):
    tile = g0.shape[0]
    own = matrix.shape[1] - 4 * tile
    ghosts = stacked(g0, g1, g2, g3)
    for d in range(4):
        at = slice(own + d * tile, own + (d + 1) * tile)
        tiles[d][...] = (partial[at, :] + product(matrix[at, own:], ghosts)).astype(HALF)


def remainder_kernel(target, matrix, partial, g0, g1, g2, g3, out):
    own = target.shape[0]
    out[...] = target[...] - (
        partial[:own, :] + product(matrix[:own, own:], stacked(g0, g1, g2, g3))
    )


def residual_kernel(remainder, pick, spread, r0, r1, r2, r3, half, *tiles):
    half[...] = (remainder[...] - product(spread[...], stacked(r0, r1, r2, r3))).astype(HALF)
    picked(pick, half, tiles)


def partner(place, exchange):
    odd = place % 2 if isinstance(place, int) else lax.rem(place, 2)
    return place + 1 - 2 * odd if exchange == 0 else place - 1 + 2 * odd


def swapped(shard, axis, exchange):
    devices = lax.axis_size(axis)
    pairs = [(i, partner(i, exchange)) for i in range(devices)]
    if devices % 2 == 0:
        pairs = [(i, j % devices) for i, j in pairs]
    return lax.ppermute(shard, axis, [(i, j) for i, j in pairs if 0 <= j < devices])


def traded(tiles):
    return tuple(swapped(tiles[i], "row" if i < 2 else "col", i % 2) for i in range(4))


def per_device(
    right_side, local_operator, local_inverse, coarse_basis, coarse_inverse, send_rows, send_count
):
    target = right_side[0, 0]
    operator = local_operator[0, 0]
    inverse = local_inverse[0, 0]
    basis = jnp.swapaxes(coarse_basis[0, 0], 0, 1)
    rows_list = send_rows[0, 0]
    own, columns = target.shape
    local = operator.shape[0]
    tile = rows_list.shape[1]
    margin = 4 * tile
    coarse = basis.shape[0]
    groups = coarse_inverse.shape[0]
    across = lax.axis_size("col")

    four_tiles = [((tile, columns), HALF)] * 4
    owned_half = ((own, columns), HALF)
    owned_full = ((own, columns), FULL)
    local_full = ((local, columns), FULL)
    target, residual, pick, masked, basis, *tiles = call(
        select_kernel,
        "select",
        [
            owned_full,
            owned_half,
            ((margin, own), HALF),
            (rows_list.shape, jnp.int32),
            (basis.shape, HALF),
        ]
        + four_tiles,
        target,
        rows_list,
        send_count[0],
        basis,
        far=4,
        scratch=(
            pltpu.VMEM(rows_list.shape, jnp.int32),
            pltpu.SMEM((1, 4), jnp.int32),
            pltpu.SemaphoreType.DMA((8,)),
        ),
        flops=2 * margin * own * columns,
    )
    spread = solution = None
    for sweep in range(ITERS):
        first, last = sweep == 0, sweep == ITERS - 1
        if sweep:
            ghosts = traded(tiles)
            (partial,) = call(
                own_columns_kernel,
                "operator_own",
                [local_full],
                operator,
                solution_half,
                flops=2 * local * own * columns,
            )
            tiles = call(
                rim_kernel,
                "operator_rim",
                four_tiles,
                operator,
                partial,
                *ghosts,
                flops=2 * margin * margin * columns,
            )
            returned = traded(tiles)
            (remainder,) = call(
                remainder_kernel,
                "remainder",
                [owned_full],
                target,
                operator,
                partial,
                *ghosts,
                flops=2 * own * margin * columns,
            )
            residual, *tiles = call(
                residual_kernel,
                "residual",
                [owned_half] + four_tiles,
                remainder,
                pick,
                spread,
                *returned,
                flops=4 * margin * own * columns,
            )
        ghosts = traded(tiles)
        if first:
            inverse, partial = call(
                load_kernel,
                "inverse_own",
                [(inverse.shape, HALF), local_full],
                inverse,
                residual,
                far=1,
                scratch=(pltpu.SemaphoreType.DMA((MATRIX_PIECES,)),),
                flops=2 * local * own * columns,
            )
        else:
            (partial,) = call(
                own_columns_kernel,
                "inverse_own",
                [local_full],
                inverse,
                residual,
                flops=2 * local * own * columns,
            )
        (restricted,) = call(
            restrict_kernel,
            "restrict",
            [((coarse, columns), HALF)],
            basis,
            residual,
            *ghosts,
            flops=2 * local * coarse * columns,
        )
        restricted = [meeting(restricted, "col", turn) for turn in reversed(range(across))][::-1]
        rim, inner = call(
            solve_kernel,
            "inverse_margin",
            [((margin, columns), FULL), owned_full],
            inverse,
            partial,
            *ghosts,
            flops=2 * local * margin * columns,
        )
        parts = call(
            parts_kernel(groups, across),
            "coarse_part",
            [((2 * coarse, columns), HALF)] * (groups // 2),
            coarse_inverse,
            *restricted,
            scratch=(pltpu.VMEM((across * coarse, columns), HALF),),
            flops=2 * coarse_inverse.size * columns,
        )
        parts = [meeting(parts[turn], "row", turn, 2) for turn in reversed(range(groups // 2))]
        mine, others = call(
            pair_kernel,
            "coarse_pair",
            [((coarse, columns), FULL), ((coarse, columns), HALF)],
            *parts,
        )
        level, *tiles = call(
            coarse_kernel,
            "coarse",
            [((coarse, columns), HALF)] + four_tiles,
            mine,
            swapped(others, "row", 0),
            basis,
            rim,
            flops=2 * coarse * margin * columns,
        )
        if first:
            masked, tiles = lax.optimization_barrier((masked, tuple(tiles)))
            spread, operator = call(
                spread_kernel,
                "spread",
                [((own, margin), HALF), (operator.shape, HALF)],
                operator,
                masked,
                far=1,
                scratch=(pltpu.SemaphoreType.DMA((MATRIX_PIECES,)),),
            )
        returned = traded(tiles)
        (base,) = call(
            base_kernel(first),
            "base",
            [owned_full],
            *([] if first else [solution]),
            inner,
            level,
            basis,
            flops=2 * coarse * own * columns,
        )
        if last:
            break
        solution, solution_half, *tiles = call(
            update_kernel,
            "update",
            [owned_full, owned_half] + four_tiles,
            base,
            pick,
            spread,
            *returned,
            flops=4 * margin * own * columns,
        )
    (solution,) = call(
        last_update_kernel,
        "last_update",
        [owned_full],
        base,
        spread,
        *returned,
        away=True,
        scratch=(pltpu.VMEM((own, columns), FULL), pltpu.SemaphoreType.DMA((4,))),
        flops=2 * margin * own * columns,
    )
    return solution[None, None]


def solution(mesh):
    return jax.shard_map(
        per_device,
        mesh=mesh,
        in_specs=(
            P("row", "col", None, None),
            P("row", "col", None, None),
            P("row", "col", None, None),
            P("row", "col", None, None),
            P(None, "col", "row"),
            P("row", "col", None, None),
            P("row", "col", None),
        ),
        out_specs=P("row", "col", None, None),
        check_vma=False,
    )
```

```python
import jax
import jax.numpy as jnp
from jax import lax
from jax.experimental import pallas as pl
from jax.experimental.pallas import tpu as pltpu
from jax.sharding import PartitionSpec as P

ITERS = 3
DAMPING = 0.5
HALF = jnp.bfloat16
FULL = jnp.float32


def product(left, right):
    return jnp.dot(left, right, preferred_element_type=FULL)


def turned_product(left, right):
    return lax.dot_general(left, right, (((0,), (0,)), ((), ())), preferred_element_type=FULL)


def call(body, name, outs, *args, far=0, away=False, scratch=(), flops=0):
    here = pl.BlockSpec(memory_space=pltpu.VMEM)
    there = pl.BlockSpec(memory_space=pltpu.HBM)
    size = sum(a.size * a.dtype.itemsize for a in args)
    distant = [pltpu.with_memory_space_constraint(a, pltpu.HBM) for a in args[:far]]
    near = [pltpu.with_memory_space_constraint(a, pltpu.VMEM) for a in args[far:]]
    return pl.pallas_call(
        body,
        out_shape=tuple((pltpu.HBM if away else pltpu.VMEM)(*out) for out in outs),
        in_specs=[there] * far + [here] * len(near),
        out_specs=tuple(there if away else here for _ in outs),
        scratch_shapes=list(scratch),
        compiler_params=pltpu.CompilerParams(vmem_limit_bytes=24 * 1024 * 1024),
        cost_estimate=pl.CostEstimate(flops=flops, bytes_accessed=size, transcendentals=0),
        name=name,
    )(*distant, *near)


def parities():
    return lax.rem(lax.axis_index("row"), 2), lax.rem(lax.axis_index("col"), 2)


def directions():
    row, col = parities()
    return 1 - row, row, 3 - col, 2 + col


def margin_spans(own, tile):
    return [
        (pl.ds(pl.multiple_of(own + d * tile, tile), tile), slice(own + i * tile, own + (i + 1) * tile))
        for i, d in enumerate(directions())
    ]


def matrix_pieces(far, near, own, tile):
    margins = margin_spans(own, tile)
    half = own // 2
    rows = [(slice(0, half), slice(0, half)), (slice(half, own), slice(half, own))] + margins
    columns = [(slice(0, own), slice(0, own))] + margins
    return [(far.at[fr, fc], near.at[nr, nc]) for fr, nr in rows for fc, nc in columns]


MATRIX_PIECES = 30


def started(pairs, sems):
    loads = [pltpu.make_async_copy(far, near, sems.at[i]) for i, (far, near) in enumerate(pairs)]
    for load in loads:
        load.start()
    return loads


def select_kernel(
    far_target, far_rows, far_counts, far_basis, target, half, pick, masked, basis, *rest
):
    *tiles, rows, counts, sems = rest
    own = target.shape[0]
    tile = rows.shape[1]
    pairs = [(far_rows, rows), (far_counts, counts), (far_target, target)]
    pairs += [
        (far_basis.at[:, far], basis.at[:, near])
        for far, near in [(slice(0, own), slice(0, own))] + margin_spans(own, tile)
    ]
    loads = started(pairs, sems)
    loads[0].wait()
    loads[1].wait()
    listed = [
        jnp.where(
            lax.broadcasted_iota(jnp.int32, (1, tile), 1) < counts[0, d], rows[d : d + 1, :], -1
        )
        for d in range(4)
    ]
    row, col = parities()
    ordered = (
        jnp.where(row == 0, listed[1], listed[0]),
        jnp.where(row == 0, listed[0], listed[1]),
        jnp.where(col == 0, listed[3], listed[2]),
        jnp.where(col == 0, listed[2], listed[3]),
    )
    for i, here in enumerate(ordered):
        masked[i : i + 1, :] = here
        down = jnp.transpose(jnp.broadcast_to(here, (tile, tile)))[:, :1]
        pick[i * tile : (i + 1) * tile, :] = (
            lax.broadcasted_iota(jnp.int32, (tile, own), 1) == down
        ).astype(FULL).astype(HALF)
    loads[2].wait()
    half[...] = target[...].astype(HALF)
    picked(pick, half, tiles)
    for load in loads[3:]:
        load.wait()


def picked(pick, half, tiles):
    tile = tiles[0].shape[0]
    for d in range(4):
        tiles[d][...] = product(pick[d * tile : (d + 1) * tile, :], half[...]).astype(HALF)


def spread_kernel(far, masked, spread, matrix, sems):
    own = spread.shape[0]
    tile = masked.shape[1]
    loads = started(matrix_pieces(far, matrix, own, tile), sems)
    for d in range(4):
        wide = jnp.broadcast_to(masked[d : d + 1, :], (own, tile))
        spread[:, d * tile : (d + 1) * tile] = (
            lax.broadcasted_iota(jnp.int32, (own, tile), 0) == wide
        ).astype(FULL).astype(HALF)
    for load in loads:
        load.wait()


def stacked(*parts):
    return jnp.concatenate([part[...] for part in parts], axis=0)


def load_kernel(far, owned, matrix, out, sems):
    own = owned.shape[0]
    tile = (matrix.shape[0] - own) // 4
    for load in started(matrix_pieces(far, matrix, own, tile), sems):
        load.wait()
    out[...] = product(matrix[:, :own], owned[...])


def own_columns_kernel(matrix, owned, out):
    own = owned.shape[0]
    out[...] = product(matrix[:, :own], owned[...])


def restrict_kernel(basis, owned, g0, g1, g2, g3, out):
    own = owned.shape[0]
    out[...] = (
        product(basis[:, :own], owned[...]) + product(basis[:, own:], stacked(g0, g1, g2, g3))
    ).astype(HALF)


def solve_kernel(matrix, partial, g0, g1, g2, g3, rim, inner):
    own = inner.shape[0]
    ghosts = stacked(g0, g1, g2, g3)
    rim[...] = partial[own:, :] + product(matrix[own:, own:], ghosts)
    inner[...] = partial[:own, :] + product(matrix[:own, own:], ghosts)


def met(place, turn, devices):
    if devices & (devices - 1) == 0:
        return place ^ turn
    return (turn + devices - place) % devices


def meeting(shard, axis, turn, block=1):
    devices = lax.axis_size(axis)
    pairs = [
        (i, met(i // block, turn, devices // block) * block + i % block) for i in range(devices)
    ]
    return shard if all(i == j for i, j in pairs) else lax.ppermute(shard, axis, pairs)


def parts_kernel(groups, across):
    def body(inverse, *refs):
        restricted, parts, gathered = refs[:across], refs[across:-1], refs[-1]
        coarse = inverse.shape[1]
        for turn, piece in enumerate(restricted):
            at = pl.multiple_of(met(lax.axis_index("col"), turn, across) * coarse, coarse)
            gathered[pl.ds(at, coarse), :] = piece[...]
        pair = lax.axis_index("row") // 2
        for turn, part in enumerate(parts):
            other = 2 * met(pair, turn, groups // 2)
            for i in range(2):
                part[i * coarse : (i + 1) * coarse, :] = product(
                    inverse[other + i], gathered[...]
                ).astype(HALF)

    return body


def pair_kernel(*refs):
    *parts, mine, others = refs
    coarse = mine.shape[0]
    total = parts[0][...].astype(FULL)
    for part in parts[1:]:
        total += part[...].astype(FULL)
    odd = lax.rem(lax.axis_index("row"), 2) == 1
    low, high = total[:coarse, :], total[coarse:, :]
    mine[...] = jnp.where(odd, high, low)
    others[...] = jnp.where(odd, low, high).astype(HALF)


def coarse_kernel(mine, theirs, basis, rim, level, *tiles):
    tile = tiles[0].shape[0]
    own = basis.shape[1] - 4 * tile
    level[...] = (mine[...] + theirs[...].astype(FULL)).astype(HALF)
    for d in range(4):
        here = slice(d * tile, (d + 1) * tile)
        there = slice(own + d * tile, own + (d + 1) * tile)
        tiles[d][...] = (rim[here, :] + turned_product(basis[:, there], level[...])).astype(HALF)


def base_kernel(first):
    def body(*refs):
        refs = list(refs)
        before = None if first else refs.pop(0)
        inner, level, basis, spread, r0, r1, out = refs
        own, tile = out.shape[0], r0.shape[0]
        update = (
            inner[...]
            + turned_product(basis[:, :own], level[...])
            + product(spread[:, : 2 * tile], stacked(r0, r1))
        )
        out[...] = DAMPING * update if first else before[...] + DAMPING * update

    return body


def update_kernel(base, pick, spread, r2, r3, after, half, *tiles):
    tile = r2.shape[0]
    after[...] = base[...] + DAMPING * product(spread[:, 2 * tile :], stacked(r2, r3))
    half[...] = after[...].astype(HALF)
    picked(pick, half, tiles)


def last_update_kernel(base, spread, r2, r3, far, after, sems):
    tile = r2.shape[0]
    pieces = sems.shape[0]
    height = after.shape[0] // pieces
    returned = stacked(r2, r3)
    stores = []
    for i in range(pieces):
        at = slice(i * height, (i + 1) * height)
        after[at, :] = base[at, :] + DAMPING * product(spread[at, 2 * tile :], returned)
        stores.append(pltpu.make_async_copy(after.at[at], far.at[at], sems.at[i]))
        stores[-1].start()
    for store in stores:
        store.wait()


def rim_kernel(matrix, partial, g0, g1, g2, g3, *tiles):
    tile = g0.shape[0]
    own = matrix.shape[1] - 4 * tile
    ghosts = stacked(g0, g1, g2, g3)
    for d in range(4):
        at = slice(own + d * tile, own + (d + 1) * tile)
        tiles[d][...] = (partial[at, :] + product(matrix[at, own:], ghosts)).astype(HALF)


def remainder_kernel(target, matrix, partial, g0, g1, g2, g3, spread, r0, r1, out):
    own, tile = target.shape[0], r0.shape[0]
    image = (
        partial[:own, :]
        + product(matrix[:own, own:], stacked(g0, g1, g2, g3))
        + product(spread[:, : 2 * tile], stacked(r0, r1))
    )
    out[...] = target[...] - image


def residual_kernel(remainder, pick, spread, r2, r3, half, *tiles):
    tile = r2.shape[0]
    half[...] = (remainder[...] - product(spread[:, 2 * tile :], stacked(r2, r3))).astype(HALF)
    picked(pick, half, tiles)


def partner(place, exchange):
    odd = place % 2 if isinstance(place, int) else lax.rem(place, 2)
    return place + 1 - 2 * odd if exchange == 0 else place - 1 + 2 * odd


def swapped(shard, axis, exchange):
    rows, columns = lax.axis_size("row"), lax.axis_size("col")

    def other(row, col):
        if axis == "row":
            there = partner(row, exchange), col
            beside = row, partner(col, 0)
        else:
            there = row, partner(col, exchange)
            beside = partner(row, 0), col
        for at in (there, beside):
            if 0 <= at[0] < rows and 0 <= at[1] < columns:
                return at
        return row, col

    places = [(row, col) for row in range(rows) for col in range(columns)]
    ends = [(at, other(*at)) for at in places]
    pairs = [(i * columns + j, k * columns + l) for (i, j), (k, l) in ends]
    return lax.ppermute(shard, ("row", "col"), pairs)


def traded(tiles):
    return tuple(swapped(tiles[i], "row" if i < 2 else "col", i % 2) for i in range(4))


def per_device(
    right_side, local_operator, local_inverse, coarse_basis, coarse_inverse, send_rows, send_count
):
    target = right_side[0, 0]
    operator = local_operator[0, 0]
    inverse = local_inverse[0, 0]
    basis = jnp.swapaxes(coarse_basis[0, 0], 0, 1)
    rows_list = send_rows[0, 0]
    own, columns = target.shape
    local = operator.shape[0]
    tile = rows_list.shape[1]
    margin = 4 * tile
    coarse = basis.shape[0]
    groups = coarse_inverse.shape[0]
    across = lax.axis_size("col")

    four_tiles = [((tile, columns), HALF)] * 4
    owned_half = ((own, columns), HALF)
    owned_full = ((own, columns), FULL)
    local_full = ((local, columns), FULL)
    target, residual, pick, masked, basis, *tiles = call(
        select_kernel,
        "select",
        [
            owned_full,
            owned_half,
            ((margin, own), HALF),
            (rows_list.shape, jnp.int32),
            (basis.shape, HALF),
        ]
        + four_tiles,
        target,
        rows_list,
        send_count[0],
        basis,
        far=4,
        scratch=(
            pltpu.VMEM(rows_list.shape, jnp.int32),
            pltpu.SMEM((1, 4), jnp.int32),
            pltpu.SemaphoreType.DMA((8,)),
        ),
        flops=2 * margin * own * columns,
    )
    spread = solution = None
    for sweep in range(ITERS):
        first, last = sweep == 0, sweep == ITERS - 1
        if sweep:
            ghosts = traded(tiles)
            (partial,) = call(
                own_columns_kernel,
                "operator_own",
                [local_full],
                operator,
                solution_half,
                flops=2 * local * own * columns,
            )
            tiles = call(
                rim_kernel,
                "operator_rim",
                four_tiles,
                operator,
                partial,
                *ghosts,
                flops=2 * margin * margin * columns,
            )
            returned = traded(tiles)
            (remainder,) = call(
                remainder_kernel,
                "remainder",
                [owned_full],
                target,
                operator,
                partial,
                *ghosts,
                spread,
                *returned[:2],
                flops=2 * own * (margin + 2 * tile) * columns,
            )
            residual, *tiles = call(
                residual_kernel,
                "residual",
                [owned_half] + four_tiles,
                remainder,
                pick,
                spread,
                *returned[2:],
                flops=2 * (margin + 2 * tile) * own * columns,
            )
        ghosts = traded(tiles)
        if first:
            inverse, partial = call(
                load_kernel,
                "inverse_own",
                [(inverse.shape, HALF), local_full],
                inverse,
                residual,
                far=1,
                scratch=(pltpu.SemaphoreType.DMA((MATRIX_PIECES,)),),
                flops=2 * local * own * columns,
            )
        else:
            (partial,) = call(
                own_columns_kernel,
                "inverse_own",
                [local_full],
                inverse,
                residual,
                flops=2 * local * own * columns,
            )
        (restricted,) = call(
            restrict_kernel,
            "restrict",
            [((coarse, columns), HALF)],
            basis,
            residual,
            *ghosts,
            flops=2 * local * coarse * columns,
        )
        restricted = [meeting(restricted, "col", turn) for turn in reversed(range(across))][::-1]
        rim, inner = call(
            solve_kernel,
            "inverse_margin",
            [((margin, columns), FULL), owned_full],
            inverse,
            partial,
            *ghosts,
            flops=2 * local * margin * columns,
        )
        parts = call(
            parts_kernel(groups, across),
            "coarse_part",
            [((2 * coarse, columns), HALF)] * (groups // 2),
            coarse_inverse,
            *restricted,
            scratch=(pltpu.VMEM((across * coarse, columns), HALF),),
            flops=2 * coarse_inverse.size * columns,
        )
        parts = [meeting(parts[turn], "row", turn, 2) for turn in reversed(range(groups // 2))]
        mine, others = call(
            pair_kernel,
            "coarse_pair",
            [((coarse, columns), FULL), ((coarse, columns), HALF)],
            *parts,
        )
        level, *tiles = call(
            coarse_kernel,
            "coarse",
            [((coarse, columns), HALF)] + four_tiles,
            mine,
            swapped(others, "row", 0),
            basis,
            rim,
            flops=2 * coarse * margin * columns,
        )
        if first:
            masked, tiles = lax.optimization_barrier((masked, tuple(tiles)))
            spread, operator = call(
                spread_kernel,
                "spread",
                [((own, margin), HALF), (operator.shape, HALF)],
                operator,
                masked,
                far=1,
                scratch=(pltpu.SemaphoreType.DMA((MATRIX_PIECES,)),),
            )
        returned = traded(tiles)
        (base,) = call(
            base_kernel(first),
            "base",
            [owned_full],
            *([] if first else [solution]),
            inner,
            level,
            basis,
            spread,
            *returned[:2],
            flops=2 * (coarse + 2 * tile) * own * columns,
        )
        if last:
            break
        solution, solution_half, *tiles = call(
            update_kernel,
            "update",
            [owned_full, owned_half] + four_tiles,
            base,
            pick,
            spread,
            *returned[2:],
            flops=2 * (margin + 2 * tile) * own * columns,
        )
    (solution,) = call(
        last_update_kernel,
        "last_update",
        [owned_full],
        base,
        spread,
        *returned[2:],
        away=True,
        scratch=(pltpu.VMEM((own, columns), FULL), pltpu.SemaphoreType.DMA((4,))),
        flops=2 * margin * own * columns,
    )
    return solution[None, None]


def solution(mesh):
    return jax.shard_map(
        per_device,
        mesh=mesh,
        in_specs=(
            P("row", "col", None, None),
            P("row", "col", None, None),
            P("row", "col", None, None),
            P("row", "col", None, None),
            P(None, "col", "row"),
            P("row", "col", None, None),
            P("row", "col", None),
        ),
        out_specs=P("row", "col", None, None),
        check_vma=False,
    )
```

```python
import jax
import jax.numpy as jnp
from jax import lax
from jax.experimental import pallas as pl
from jax.experimental.pallas import tpu as pltpu
from jax.sharding import PartitionSpec as P

ITERS = 3
DAMPING = 0.5
HALF = jnp.bfloat16
FULL = jnp.float32


def product(left, right):
    return jnp.dot(left, right, preferred_element_type=FULL)


def turned_product(left, right):
    return lax.dot_general(left, right, (((0,), (0,)), ((), ())), preferred_element_type=FULL)


def call(body, name, outs, *args, far=0, away=False, scratch=(), flops=0):
    here = pl.BlockSpec(memory_space=pltpu.VMEM)
    there = pl.BlockSpec(memory_space=pltpu.HBM)
    size = sum(a.size * a.dtype.itemsize for a in args)
    distant = [pltpu.with_memory_space_constraint(a, pltpu.HBM) for a in args[:far]]
    near = [pltpu.with_memory_space_constraint(a, pltpu.VMEM) for a in args[far:]]
    return pl.pallas_call(
        body,
        out_shape=tuple((pltpu.HBM if away else pltpu.VMEM)(*out) for out in outs),
        in_specs=[there] * far + [here] * len(near),
        out_specs=tuple(there if away else here for _ in outs),
        scratch_shapes=list(scratch),
        compiler_params=pltpu.CompilerParams(vmem_limit_bytes=24 * 1024 * 1024),
        cost_estimate=pl.CostEstimate(flops=flops, bytes_accessed=size, transcendentals=0),
        name=name,
    )(*distant, *near)


def parities():
    return lax.rem(lax.axis_index("row"), 2), lax.rem(lax.axis_index("col"), 2)


def directions():
    row, col = parities()
    return 1 - row, row, 3 - col, 2 + col


def margin_spans(own, tile):
    return [
        (pl.ds(pl.multiple_of(own + d * tile, tile), tile), slice(own + i * tile, own + (i + 1) * tile))
        for i, d in enumerate(directions())
    ]


def matrix_pieces(far, near, own, tile):
    margins = margin_spans(own, tile)
    half = own // 2
    rows = [(slice(0, half), slice(0, half)), (slice(half, own), slice(half, own))] + margins
    columns = [(slice(0, own), slice(0, own))] + margins
    return [(far.at[fr, fc], near.at[nr, nc]) for fr, nr in rows for fc, nc in columns]


MATRIX_PIECES = 30


def started(pairs, sems):
    loads = [pltpu.make_async_copy(far, near, sems.at[i]) for i, (far, near) in enumerate(pairs)]
    for load in loads:
        load.start()
    return loads


def select_kernel(
    far_target, far_rows, far_counts, far_basis, target, half, pick, masked, basis, *rest
):
    *tiles, rows, counts, sems = rest
    own = target.shape[0]
    tile = rows.shape[1]
    pairs = [(far_rows, rows), (far_counts, counts), (far_target, target)]
    pairs += [
        (far_basis.at[:, far], basis.at[:, near])
        for far, near in [(slice(0, own), slice(0, own))] + margin_spans(own, tile)
    ]
    loads = started(pairs, sems)
    loads[0].wait()
    loads[1].wait()
    listed = [
        jnp.where(
            lax.broadcasted_iota(jnp.int32, (1, tile), 1) < counts[0, d], rows[d : d + 1, :], -1
        )
        for d in range(4)
    ]
    row, col = parities()
    ordered = (
        jnp.where(row == 0, listed[1], listed[0]),
        jnp.where(row == 0, listed[0], listed[1]),
        jnp.where(col == 0, listed[3], listed[2]),
        jnp.where(col == 0, listed[2], listed[3]),
    )
    for i, here in enumerate(ordered):
        masked[i : i + 1, :] = here
        down = jnp.transpose(jnp.broadcast_to(here, (tile, tile)))[:, :1]
        pick[i * tile : (i + 1) * tile, :] = (
            lax.broadcasted_iota(jnp.int32, (tile, own), 1) == down
        ).astype(FULL).astype(HALF)
    loads[2].wait()
    half[...] = target[...].astype(HALF)
    picked(pick, half, tiles)
    for load in loads[3:]:
        load.wait()


def picked(pick, half, tiles):
    tile = tiles[0].shape[0]
    for d in range(4):
        tiles[d][...] = product(pick[d * tile : (d + 1) * tile, :], half[...]).astype(HALF)


def spread_kernel(far, masked, spread, matrix, sems):
    own = spread.shape[0]
    tile = masked.shape[1]
    loads = started(matrix_pieces(far, matrix, own, tile), sems)
    for d in range(4):
        wide = jnp.broadcast_to(masked[d : d + 1, :], (own, tile))
        spread[:, d * tile : (d + 1) * tile] = (
            lax.broadcasted_iota(jnp.int32, (own, tile), 0) == wide
        ).astype(FULL).astype(HALF)
    for load in loads:
        load.wait()


def stacked(*parts):
    return jnp.concatenate([part[...] for part in parts], axis=0)


def load_kernel(far, owned, matrix, out, sems):
    own = owned.shape[0]
    tile = (matrix.shape[0] - own) // 4
    for load in started(matrix_pieces(far, matrix, own, tile), sems):
        load.wait()
    out[...] = product(matrix[:, :own], owned[...])


def own_columns_kernel(matrix, owned, out):
    own = owned.shape[0]
    out[...] = product(matrix[:, :own], owned[...])


def restrict_kernel(basis, owned, g0, g1, g2, g3, out):
    own = owned.shape[0]
    out[...] = (
        product(basis[:, :own], owned[...]) + product(basis[:, own:], stacked(g0, g1, g2, g3))
    ).astype(HALF)


def solve_kernel(matrix, partial, g0, g1, g2, g3, rim, inner):
    own = inner.shape[0]
    ghosts = stacked(g0, g1, g2, g3)
    rim[...] = partial[own:, :] + product(matrix[own:, own:], ghosts)
    inner[...] = partial[:own, :] + product(matrix[:own, own:], ghosts)


def met(place, turn, devices):
    if devices & (devices - 1) == 0:
        return place ^ turn
    return (turn + devices - place) % devices


def meeting(shard, axis, turn, block=1):
    devices = lax.axis_size(axis)
    pairs = [
        (i, met(i // block, turn, devices // block) * block + i % block) for i in range(devices)
    ]
    return shard if all(i == j for i, j in pairs) else lax.ppermute(shard, axis, pairs)


def parts_kernel(groups, across):
    def body(inverse, *refs):
        restricted, parts, gathered = refs[:across], refs[across:-1], refs[-1]
        coarse = inverse.shape[1]
        for turn, piece in enumerate(restricted):
            at = pl.multiple_of(met(lax.axis_index("col"), turn, across) * coarse, coarse)
            gathered[pl.ds(at, coarse), :] = piece[...]
        pair = lax.axis_index("row") // 2
        for turn, part in enumerate(parts):
            other = 2 * met(pair, turn, groups // 2)
            for i in range(2):
                part[i * coarse : (i + 1) * coarse, :] = product(
                    inverse[other + i], gathered[...]
                ).astype(HALF)

    return body


def pair_kernel(*refs):
    *parts, mine, others = refs
    coarse = mine.shape[0]
    total = parts[0][...].astype(FULL)
    for part in parts[1:]:
        total += part[...].astype(FULL)
    odd = lax.rem(lax.axis_index("row"), 2) == 1
    low, high = total[:coarse, :], total[coarse:, :]
    mine[...] = jnp.where(odd, high, low)
    others[...] = jnp.where(odd, low, high).astype(HALF)


def coarse_kernel(mine, theirs, basis, rim, level, *tiles):
    tile = tiles[0].shape[0]
    own = basis.shape[1] - 4 * tile
    level[...] = (mine[...] + theirs[...].astype(FULL)).astype(HALF)
    for d in range(4):
        here = slice(d * tile, (d + 1) * tile)
        there = slice(own + d * tile, own + (d + 1) * tile)
        tiles[d][...] = (rim[here, :] + turned_product(basis[:, there], level[...])).astype(HALF)


def base_kernel(first):
    def body(*refs):
        refs = list(refs)
        before = None if first else refs.pop(0)
        inner, level, basis, spread, r0, r1, out = refs
        own, tile = out.shape[0], r0.shape[0]
        update = (
            inner[...]
            + turned_product(basis[:, :own], level[...])
            + product(spread[:, : 2 * tile], stacked(r0, r1))
        )
        out[...] = DAMPING * update if first else before[...] + DAMPING * update

    return body


def update_kernel(base, pick, spread, r2, r3, after, half, *tiles):
    tile = r2.shape[0]
    after[...] = base[...] + DAMPING * product(spread[:, 2 * tile :], stacked(r2, r3))
    half[...] = after[...].astype(HALF)
    picked(pick, half, tiles)


def last_update_kernel(base, spread, r2, r3, far, after, sems):
    tile = r2.shape[0]
    pieces = sems.shape[0]
    height = after.shape[0] // pieces
    returned = stacked(r2, r3)
    stores = []
    for i in range(pieces):
        at = slice(i * height, (i + 1) * height)
        after[at, :] = base[at, :] + DAMPING * product(spread[at, 2 * tile :], returned)
        stores.append(pltpu.make_async_copy(after.at[at], far.at[at], sems.at[i]))
        stores[-1].start()
    for store in stores:
        store.wait()


def rim_kernel(matrix, partial, g0, g1, g2, g3, *tiles):
    tile = g0.shape[0]
    own = matrix.shape[1] - 4 * tile
    ghosts = stacked(g0, g1, g2, g3)
    for d in range(4):
        at = slice(own + d * tile, own + (d + 1) * tile)
        tiles[d][...] = (partial[at, :] + product(matrix[at, own:], ghosts)).astype(HALF)


def remainder_kernel(target, matrix, partial, g0, g1, g2, g3, spread, r0, r1, out):
    own, tile = target.shape[0], r0.shape[0]
    image = (
        partial[:own, :]
        + product(matrix[:own, own:], stacked(g0, g1, g2, g3))
        + product(spread[:, : 2 * tile], stacked(r0, r1))
    )
    out[...] = target[...] - image


def residual_kernel(remainder, pick, spread, r2, r3, half, *tiles):
    tile = r2.shape[0]
    half[...] = (remainder[...] - product(spread[:, 2 * tile :], stacked(r2, r3))).astype(HALF)
    picked(pick, half, tiles)


def partner(place, exchange):
    odd = place % 2 if isinstance(place, int) else lax.rem(place, 2)
    return place + 1 - 2 * odd if exchange == 0 else place - 1 + 2 * odd


def swapped(shard, axis, exchange):
    rows, columns = lax.axis_size("row"), lax.axis_size("col")

    def other(row, col):
        if axis == "row":
            there = partner(row, exchange), col
            beside = row, partner(col, 0)
        else:
            there = row, partner(col, exchange)
            beside = partner(row, 0), col
        for at in (there, beside):
            if 0 <= at[0] < rows and 0 <= at[1] < columns:
                return at
        return row, col

    places = [(row, col) for row in range(rows) for col in range(columns)]
    ends = [(at, other(*at)) for at in places]
    pairs = [(i * columns + j, k * columns + l) for (i, j), (k, l) in ends]
    return lax.ppermute(shard, ("row", "col"), pairs)


def traded(tiles):
    arrived = {i: swapped(tiles[i], "row" if i < 2 else "col", i % 2) for i in (1, 3, 0, 2)}
    return [arrived[i] for i in range(4)]


def per_device(
    right_side, local_operator, local_inverse, coarse_basis, coarse_inverse, send_rows, send_count
):
    target = right_side[0, 0]
    operator = local_operator[0, 0]
    inverse = local_inverse[0, 0]
    basis = jnp.swapaxes(coarse_basis[0, 0], 0, 1)
    rows_list = send_rows[0, 0]
    own, columns = target.shape
    local = operator.shape[0]
    tile = rows_list.shape[1]
    margin = 4 * tile
    coarse = basis.shape[0]
    groups = coarse_inverse.shape[0]
    across = lax.axis_size("col")

    four_tiles = [((tile, columns), HALF)] * 4
    owned_half = ((own, columns), HALF)
    owned_full = ((own, columns), FULL)
    local_full = ((local, columns), FULL)
    target, residual, pick, masked, basis, *tiles = call(
        select_kernel,
        "select",
        [
            owned_full,
            owned_half,
            ((margin, own), HALF),
            (rows_list.shape, jnp.int32),
            (basis.shape, HALF),
        ]
        + four_tiles,
        target,
        rows_list,
        send_count[0],
        basis,
        far=4,
        scratch=(
            pltpu.VMEM(rows_list.shape, jnp.int32),
            pltpu.SMEM((1, 4), jnp.int32),
            pltpu.SemaphoreType.DMA((8,)),
        ),
        flops=2 * margin * own * columns,
    )
    spread = solution = None
    for sweep in range(ITERS):
        first, last = sweep == 0, sweep == ITERS - 1
        if sweep:
            ghosts = traded(tiles)
            (partial,) = call(
                own_columns_kernel,
                "operator_own",
                [local_full],
                operator,
                solution_half,
                flops=2 * local * own * columns,
            )
            tiles = call(
                rim_kernel,
                "operator_rim",
                four_tiles,
                operator,
                partial,
                *ghosts,
                flops=2 * margin * margin * columns,
            )
            returned = traded(tiles)
            (remainder,) = call(
                remainder_kernel,
                "remainder",
                [owned_full],
                target,
                operator,
                partial,
                *ghosts,
                spread,
                *returned[:2],
                flops=2 * own * (margin + 2 * tile) * columns,
            )
            residual, *tiles = call(
                residual_kernel,
                "residual",
                [owned_half] + four_tiles,
                remainder,
                pick,
                spread,
                *returned[2:],
                flops=2 * (margin + 2 * tile) * own * columns,
            )
        ghosts = traded(tiles)
        if first:
            inverse, partial = call(
                load_kernel,
                "inverse_own",
                [(inverse.shape, HALF), local_full],
                inverse,
                residual,
                far=1,
                scratch=(pltpu.SemaphoreType.DMA((MATRIX_PIECES,)),),
                flops=2 * local * own * columns,
            )
        else:
            (partial,) = call(
                own_columns_kernel,
                "inverse_own",
                [local_full],
                inverse,
                residual,
                flops=2 * local * own * columns,
            )
        (restricted,) = call(
            restrict_kernel,
            "restrict",
            [((coarse, columns), HALF)],
            basis,
            residual,
            *ghosts,
            flops=2 * local * coarse * columns,
        )
        restricted = [meeting(restricted, "col", turn) for turn in reversed(range(across))][::-1]
        rim, inner = call(
            solve_kernel,
            "inverse_margin",
            [((margin, columns), FULL), owned_full],
            inverse,
            partial,
            *ghosts,
            flops=2 * local * margin * columns,
        )
        parts = call(
            parts_kernel(groups, across),
            "coarse_part",
            [((2 * coarse, columns), HALF)] * (groups // 2),
            coarse_inverse,
            *restricted,
            scratch=(pltpu.VMEM((across * coarse, columns), HALF),),
            flops=2 * coarse_inverse.size * columns,
        )
        parts = [meeting(parts[turn], "row", turn, 2) for turn in reversed(range(groups // 2))]
        mine, others = call(
            pair_kernel,
            "coarse_pair",
            [((coarse, columns), FULL), ((coarse, columns), HALF)],
            *parts,
        )
        level, *tiles = call(
            coarse_kernel,
            "coarse",
            [((coarse, columns), HALF)] + four_tiles,
            mine,
            swapped(others, "row", 0),
            basis,
            rim,
            flops=2 * coarse * margin * columns,
        )
        if first:
            masked, tiles = lax.optimization_barrier((masked, tuple(tiles)))
            spread, operator = call(
                spread_kernel,
                "spread",
                [((own, margin), HALF), (operator.shape, HALF)],
                operator,
                masked,
                far=1,
                scratch=(pltpu.SemaphoreType.DMA((MATRIX_PIECES,)),),
            )
        returned = traded(tiles)
        (base,) = call(
            base_kernel(first),
            "base",
            [owned_full],
            *([] if first else [solution]),
            inner,
            level,
            basis,
            spread,
            *returned[:2],
            flops=2 * (coarse + 2 * tile) * own * columns,
        )
        if last:
            break
        solution, solution_half, *tiles = call(
            update_kernel,
            "update",
            [owned_full, owned_half] + four_tiles,
            base,
            pick,
            spread,
            *returned[2:],
            flops=2 * (margin + 2 * tile) * own * columns,
        )
    (solution,) = call(
        last_update_kernel,
        "last_update",
        [owned_full],
        base,
        spread,
        *returned[2:],
        away=True,
        scratch=(pltpu.VMEM((own, columns), FULL), pltpu.SemaphoreType.DMA((4,))),
        flops=2 * margin * own * columns,
    )
    return solution[None, None]


def solution(mesh):
    return jax.shard_map(
        per_device,
        mesh=mesh,
        in_specs=(
            P("row", "col", None, None),
            P("row", "col", None, None),
            P("row", "col", None, None),
            P("row", "col", None, None),
            P(None, "col", "row"),
            P("row", "col", None, None),
            P("row", "col", None),
        ),
        out_specs=P("row", "col", None, None),
        check_vma=False,
    )
```

```python
import jax
import jax.numpy as jnp
from jax import lax
from jax.experimental import pallas as pl
from jax.experimental.pallas import tpu as pltpu
from jax.sharding import PartitionSpec as P

ITERS = 3
DAMPING = 0.5
HALF = jnp.bfloat16
FULL = jnp.float32


def product(left, right):
    return jnp.dot(left, right, preferred_element_type=FULL)


def turned_product(left, right):
    return lax.dot_general(left, right, (((0,), (0,)), ((), ())), preferred_element_type=FULL)


def call(body, name, outs, *args, far=0, away=False, scratch=(), flops=0):
    here = pl.BlockSpec(memory_space=pltpu.VMEM)
    there = pl.BlockSpec(memory_space=pltpu.HBM)
    size = sum(a.size * a.dtype.itemsize for a in args)
    distant = [pltpu.with_memory_space_constraint(a, pltpu.HBM) for a in args[:far]]
    near = [pltpu.with_memory_space_constraint(a, pltpu.VMEM) for a in args[far:]]
    return pl.pallas_call(
        body,
        out_shape=tuple((pltpu.HBM if away else pltpu.VMEM)(*out) for out in outs),
        in_specs=[there] * far + [here] * len(near),
        out_specs=tuple(there if away else here for _ in outs),
        scratch_shapes=list(scratch),
        compiler_params=pltpu.CompilerParams(vmem_limit_bytes=24 * 1024 * 1024),
        cost_estimate=pl.CostEstimate(flops=flops, bytes_accessed=size, transcendentals=0),
        name=name,
    )(*distant, *near)


def parities():
    return lax.rem(lax.axis_index("row"), 2), lax.rem(lax.axis_index("col"), 2)


def directions():
    row, col = parities()
    return row, 1 - row, 2 + col, 3 - col


def margin_spans(own, tile):
    return [
        (pl.ds(pl.multiple_of(own + d * tile, tile), tile), slice(own + i * tile, own + (i + 1) * tile))
        for i, d in enumerate(directions())
    ]


def matrix_pieces(far, near, own, tile):
    margins = margin_spans(own, tile)
    half = own // 2
    rows = [(slice(0, half), slice(0, half)), (slice(half, own), slice(half, own))] + margins
    columns = [(slice(0, own), slice(0, own))] + margins
    return [(far.at[fr, fc], near.at[nr, nc]) for fr, nr in rows for fc, nc in columns]


MATRIX_PIECES = 30


def started(pairs, sems):
    loads = [pltpu.make_async_copy(far, near, sems.at[i]) for i, (far, near) in enumerate(pairs)]
    for load in loads:
        load.start()
    return loads


def select_kernel(
    far_target, far_rows, far_counts, far_basis, target, half, pick, masked, basis, *rest
):
    *tiles, rows, counts, sems = rest
    own = target.shape[0]
    tile = rows.shape[1]
    pairs = [(far_rows, rows), (far_counts, counts), (far_target, target)]
    pairs += [
        (far_basis.at[:, far], basis.at[:, near])
        for far, near in [(slice(0, own), slice(0, own))] + margin_spans(own, tile)
    ]
    loads = started(pairs, sems)
    loads[0].wait()
    loads[1].wait()
    listed = [
        jnp.where(
            lax.broadcasted_iota(jnp.int32, (1, tile), 1) < counts[0, d], rows[d : d + 1, :], -1
        )
        for d in range(4)
    ]
    row, col = parities()
    ordered = (
        jnp.where(row == 0, listed[0], listed[1]),
        jnp.where(row == 0, listed[1], listed[0]),
        jnp.where(col == 0, listed[2], listed[3]),
        jnp.where(col == 0, listed[3], listed[2]),
    )
    for i, here in enumerate(ordered):
        masked[i : i + 1, :] = here
        down = jnp.transpose(jnp.broadcast_to(here, (tile, tile)))[:, :1]
        pick[i * tile : (i + 1) * tile, :] = (
            lax.broadcasted_iota(jnp.int32, (tile, own), 1) == down
        ).astype(FULL).astype(HALF)
    loads[2].wait()
    half[...] = target[...].astype(HALF)
    picked(pick, half, tiles)
    for load in loads[3:]:
        load.wait()


def picked(pick, half, tiles):
    tile = tiles[0].shape[0]
    for d in range(4):
        tiles[d][...] = product(pick[d * tile : (d + 1) * tile, :], half[...]).astype(HALF)


def spread_kernel(far, masked, spread, matrix, sems):
    own = spread.shape[0]
    tile = masked.shape[1]
    loads = started(matrix_pieces(far, matrix, own, tile), sems)
    for d in range(4):
        wide = jnp.broadcast_to(masked[d : d + 1, :], (own, tile))
        spread[:, d * tile : (d + 1) * tile] = (
            lax.broadcasted_iota(jnp.int32, (own, tile), 0) == wide
        ).astype(FULL).astype(HALF)
    for load in loads:
        load.wait()


def stacked(*parts):
    return jnp.concatenate([part[...] for part in parts], axis=0)


def load_kernel(far, owned, matrix, out, sems):
    own = owned.shape[0]
    tile = (matrix.shape[0] - own) // 4
    for load in started(matrix_pieces(far, matrix, own, tile), sems):
        load.wait()
    out[...] = product(matrix[:, :own], owned[...])


def own_columns_kernel(matrix, owned, out):
    own = owned.shape[0]
    out[...] = product(matrix[:, :own], owned[...])


def restrict_kernel(basis, owned, g0, g1, g2, g3, out):
    own = owned.shape[0]
    out[...] = (
        product(basis[:, :own], owned[...]) + product(basis[:, own:], stacked(g0, g1, g2, g3))
    ).astype(HALF)


def solve_kernel(matrix, partial, g0, g1, g2, g3, rim, inner):
    own = inner.shape[0]
    ghosts = stacked(g0, g1, g2, g3)
    rim[...] = partial[own:, :] + product(matrix[own:, own:], ghosts)
    inner[...] = partial[:own, :] + product(matrix[:own, own:], ghosts)


def met(place, turn, devices):
    if devices & (devices - 1) == 0:
        return place ^ turn
    return (turn + devices - place) % devices


def meeting(shard, axis, turn, block=1):
    devices = lax.axis_size(axis)
    pairs = [
        (i, met(i // block, turn, devices // block) * block + i % block) for i in range(devices)
    ]
    return shard if all(i == j for i, j in pairs) else lax.ppermute(shard, axis, pairs)


def parts_kernel(groups, across):
    def body(inverse, *refs):
        restricted, parts, gathered = refs[:across], refs[across:-1], refs[-1]
        coarse = inverse.shape[1]
        for turn, piece in enumerate(restricted):
            at = pl.multiple_of(met(lax.axis_index("col"), turn, across) * coarse, coarse)
            gathered[pl.ds(at, coarse), :] = piece[...]
        pair = lax.axis_index("row") // 2
        for turn, part in enumerate(parts):
            other = 2 * met(pair, turn, groups // 2)
            for i in range(2):
                part[i * coarse : (i + 1) * coarse, :] = product(
                    inverse[other + i], gathered[...]
                ).astype(HALF)

    return body


def pair_kernel(*refs):
    *parts, mine, others = refs
    coarse = mine.shape[0]
    total = parts[0][...].astype(FULL)
    for part in parts[1:]:
        total += part[...].astype(FULL)
    odd = lax.rem(lax.axis_index("row"), 2) == 1
    low, high = total[:coarse, :], total[coarse:, :]
    mine[...] = jnp.where(odd, high, low)
    others[...] = jnp.where(odd, low, high).astype(HALF)


def coarse_kernel(mine, theirs, basis, rim, level, *tiles):
    tile = tiles[0].shape[0]
    own = basis.shape[1] - 4 * tile
    level[...] = (mine[...] + theirs[...].astype(FULL)).astype(HALF)
    for d in range(4):
        here = slice(d * tile, (d + 1) * tile)
        there = slice(own + d * tile, own + (d + 1) * tile)
        tiles[d][...] = (rim[here, :] + turned_product(basis[:, there], level[...])).astype(HALF)


def base_kernel(first):
    def body(*refs):
        refs = list(refs)
        before = None if first else refs.pop(0)
        inner, level, basis, spread, r0, r1, out = refs
        own, tile = out.shape[0], r0.shape[0]
        update = (
            inner[...]
            + turned_product(basis[:, :own], level[...])
            + product(spread[:, : 2 * tile], stacked(r0, r1))
        )
        out[...] = DAMPING * update if first else before[...] + DAMPING * update

    return body


def update_kernel(base, pick, spread, r2, r3, after, half, *tiles):
    tile = r2.shape[0]
    after[...] = base[...] + DAMPING * product(spread[:, 2 * tile :], stacked(r2, r3))
    half[...] = after[...].astype(HALF)
    picked(pick, half, tiles)


def last_update_kernel(base, spread, r2, r3, far, after, sems):
    tile = r2.shape[0]
    pieces = sems.shape[0]
    height = after.shape[0] // pieces
    returned = stacked(r2, r3)
    stores = []
    for i in range(pieces):
        at = slice(i * height, (i + 1) * height)
        after[at, :] = base[at, :] + DAMPING * product(spread[at, 2 * tile :], returned)
        stores.append(pltpu.make_async_copy(after.at[at], far.at[at], sems.at[i]))
        stores[-1].start()
    for store in stores:
        store.wait()


def rim_kernel(matrix, partial, g0, g1, g2, g3, *tiles):
    tile = g0.shape[0]
    own = matrix.shape[1] - 4 * tile
    ghosts = stacked(g0, g1, g2, g3)
    for d in range(4):
        at = slice(own + d * tile, own + (d + 1) * tile)
        tiles[d][...] = (partial[at, :] + product(matrix[at, own:], ghosts)).astype(HALF)


def remainder_kernel(target, matrix, partial, g0, g1, g2, g3, spread, r0, r1, out):
    own, tile = target.shape[0], r0.shape[0]
    image = (
        partial[:own, :]
        + product(matrix[:own, own:], stacked(g0, g1, g2, g3))
        + product(spread[:, : 2 * tile], stacked(r0, r1))
    )
    out[...] = target[...] - image


def residual_kernel(remainder, pick, spread, r2, r3, half, *tiles):
    tile = r2.shape[0]
    half[...] = (remainder[...] - product(spread[:, 2 * tile :], stacked(r2, r3))).astype(HALF)
    picked(pick, half, tiles)


def partner(place, exchange):
    odd = place % 2 if isinstance(place, int) else lax.rem(place, 2)
    return place + 1 - 2 * odd if exchange == 0 else place - 1 + 2 * odd


def swapped(shard, axis, exchange):
    rows, columns = lax.axis_size("row"), lax.axis_size("col")

    def other(row, col):
        if axis == "row":
            there = partner(row, exchange), col
            beside = row, partner(col, 0)
        else:
            there = row, partner(col, exchange)
            beside = partner(row, 0), col
        for at in (there, beside):
            if 0 <= at[0] < rows and 0 <= at[1] < columns:
                return at
        return row, col

    places = [(row, col) for row in range(rows) for col in range(columns)]
    ends = [(at, other(*at)) for at in places]
    pairs = [(i * columns + j, k * columns + l) for (i, j), (k, l) in ends]
    return lax.ppermute(shard, ("row", "col"), pairs)


def traded(tiles):
    return [swapped(tiles[i], "row" if i < 2 else "col", 1 - i % 2) for i in range(4)]


def per_device(
    right_side, local_operator, local_inverse, coarse_basis, coarse_inverse, send_rows, send_count
):
    target = right_side[0, 0]
    operator = local_operator[0, 0]
    inverse = local_inverse[0, 0]
    basis = jnp.swapaxes(coarse_basis[0, 0], 0, 1)
    rows_list = send_rows[0, 0]
    own, columns = target.shape
    local = operator.shape[0]
    tile = rows_list.shape[1]
    margin = 4 * tile
    coarse = basis.shape[0]
    groups = coarse_inverse.shape[0]
    across = lax.axis_size("col")

    four_tiles = [((tile, columns), HALF)] * 4
    owned_half = ((own, columns), HALF)
    owned_full = ((own, columns), FULL)
    local_full = ((local, columns), FULL)
    target, residual, pick, masked, basis, *tiles = call(
        select_kernel,
        "select",
        [
            owned_full,
            owned_half,
            ((margin, own), HALF),
            (rows_list.shape, jnp.int32),
            (basis.shape, HALF),
        ]
        + four_tiles,
        target,
        rows_list,
        send_count[0],
        basis,
        far=4,
        scratch=(
            pltpu.VMEM(rows_list.shape, jnp.int32),
            pltpu.SMEM((1, 4), jnp.int32),
            pltpu.SemaphoreType.DMA((8,)),
        ),
        flops=2 * margin * own * columns,
    )
    spread = solution = None
    for sweep in range(ITERS):
        first, last = sweep == 0, sweep == ITERS - 1
        if sweep:
            ghosts = traded(tiles)
            (partial,) = call(
                own_columns_kernel,
                "operator_own",
                [local_full],
                operator,
                solution_half,
                flops=2 * local * own * columns,
            )
            tiles = call(
                rim_kernel,
                "operator_rim",
                four_tiles,
                operator,
                partial,
                *ghosts,
                flops=2 * margin * margin * columns,
            )
            returned = traded(tiles)
            (remainder,) = call(
                remainder_kernel,
                "remainder",
                [owned_full],
                target,
                operator,
                partial,
                *ghosts,
                spread,
                *returned[:2],
                flops=2 * own * (margin + 2 * tile) * columns,
            )
            residual, *tiles = call(
                residual_kernel,
                "residual",
                [owned_half] + four_tiles,
                remainder,
                pick,
                spread,
                *returned[2:],
                flops=2 * (margin + 2 * tile) * own * columns,
            )
        ghosts = traded(tiles)
        if first:
            inverse, partial = call(
                load_kernel,
                "inverse_own",
                [(inverse.shape, HALF), local_full],
                inverse,
                residual,
                far=1,
                scratch=(pltpu.SemaphoreType.DMA((MATRIX_PIECES,)),),
                flops=2 * local * own * columns,
            )
        else:
            (partial,) = call(
                own_columns_kernel,
                "inverse_own",
                [local_full],
                inverse,
                residual,
                flops=2 * local * own * columns,
            )
        (restricted,) = call(
            restrict_kernel,
            "restrict",
            [((coarse, columns), HALF)],
            basis,
            residual,
            *ghosts,
            flops=2 * local * coarse * columns,
        )
        restricted = [meeting(restricted, "col", turn) for turn in reversed(range(across))][::-1]
        rim, inner = call(
            solve_kernel,
            "inverse_margin",
            [((margin, columns), FULL), owned_full],
            inverse,
            partial,
            *ghosts,
            flops=2 * local * margin * columns,
        )
        parts = call(
            parts_kernel(groups, across),
            "coarse_part",
            [((2 * coarse, columns), HALF)] * (groups // 2),
            coarse_inverse,
            *restricted,
            scratch=(pltpu.VMEM((across * coarse, columns), HALF),),
            flops=2 * coarse_inverse.size * columns,
        )
        parts = [meeting(parts[turn], "row", turn, 2) for turn in reversed(range(groups // 2))]
        mine, others = call(
            pair_kernel,
            "coarse_pair",
            [((coarse, columns), FULL), ((coarse, columns), HALF)],
            *parts,
        )
        level, *tiles = call(
            coarse_kernel,
            "coarse",
            [((coarse, columns), HALF)] + four_tiles,
            mine,
            swapped(others, "row", 0),
            basis,
            rim,
            flops=2 * coarse * margin * columns,
        )
        if first:
            masked, tiles = lax.optimization_barrier((masked, tuple(tiles)))
            spread, operator = call(
                spread_kernel,
                "spread",
                [((own, margin), HALF), (operator.shape, HALF)],
                operator,
                masked,
                far=1,
                scratch=(pltpu.SemaphoreType.DMA((MATRIX_PIECES,)),),
            )
        returned = traded(tiles)
        (base,) = call(
            base_kernel(first),
            "base",
            [owned_full],
            *([] if first else [solution]),
            inner,
            level,
            basis,
            spread,
            *returned[:2],
            flops=2 * (coarse + 2 * tile) * own * columns,
        )
        if last:
            break
        solution, solution_half, *tiles = call(
            update_kernel,
            "update",
            [owned_full, owned_half] + four_tiles,
            base,
            pick,
            spread,
            *returned[2:],
            flops=2 * (margin + 2 * tile) * own * columns,
        )
    (solution,) = call(
        last_update_kernel,
        "last_update",
        [owned_full],
        base,
        spread,
        *returned[2:],
        away=True,
        scratch=(pltpu.VMEM((own, columns), FULL), pltpu.SemaphoreType.DMA((4,))),
        flops=2 * margin * own * columns,
    )
    return solution[None, None]


def solution(mesh):
    return jax.shard_map(
        per_device,
        mesh=mesh,
        in_specs=(
            P("row", "col", None, None),
            P("row", "col", None, None),
            P("row", "col", None, None),
            P("row", "col", None, None),
            P(None, "col", "row"),
            P("row", "col", None, None),
            P("row", "col", None),
        ),
        out_specs=P("row", "col", None, None),
        check_vma=False,
    )
```

```python
import jax
import jax.numpy as jnp
from jax import lax
from jax.experimental import pallas as pl
from jax.experimental.pallas import tpu as pltpu
from jax.sharding import PartitionSpec as P

ITERS = 3
DAMPING = 0.5
HALF = jnp.bfloat16
FULL = jnp.float32


def product(left, right):
    return jnp.dot(left, right, preferred_element_type=FULL)


def turned_product(left, right):
    return lax.dot_general(left, right, (((0,), (0,)), ((), ())), preferred_element_type=FULL)


def call(body, name, outs, *args, far=0, away=False, scratch=(), flops=0):
    here = pl.BlockSpec(memory_space=pltpu.VMEM)
    there = pl.BlockSpec(memory_space=pltpu.HBM)
    size = sum(a.size * a.dtype.itemsize for a in args)
    distant = [pltpu.with_memory_space_constraint(a, pltpu.HBM) for a in args[:far]]
    near = [pltpu.with_memory_space_constraint(a, pltpu.VMEM) for a in args[far:]]
    return pl.pallas_call(
        body,
        out_shape=tuple((pltpu.HBM if away else pltpu.VMEM)(*out) for out in outs),
        in_specs=[there] * far + [here] * len(near),
        out_specs=tuple(there if away else here for _ in outs),
        scratch_shapes=list(scratch),
        compiler_params=pltpu.CompilerParams(vmem_limit_bytes=24 * 1024 * 1024),
        cost_estimate=pl.CostEstimate(flops=flops, bytes_accessed=size, transcendentals=0),
        name=name,
    )(*distant, *near)


def parities():
    return lax.rem(lax.axis_index("row"), 2), lax.rem(lax.axis_index("col"), 2)


def directions():
    row, col = parities()
    return 1 - row, row, 2 + col, 3 - col


def margin_spans(own, tile):
    return [
        (pl.ds(pl.multiple_of(own + d * tile, tile), tile), slice(own + i * tile, own + (i + 1) * tile))
        for i, d in enumerate(directions())
    ]


def matrix_pieces(far, near, own, tile):
    margins = margin_spans(own, tile)
    half = own // 2
    rows = [(slice(0, half), slice(0, half)), (slice(half, own), slice(half, own))] + margins
    columns = [(slice(0, own), slice(0, own))] + margins
    return [(far.at[fr, fc], near.at[nr, nc]) for fr, nr in rows for fc, nc in columns]


MATRIX_PIECES = 30


def started(pairs, sems):
    loads = [pltpu.make_async_copy(far, near, sems.at[i]) for i, (far, near) in enumerate(pairs)]
    for load in loads:
        load.start()
    return loads


def select_kernel(
    far_target, far_rows, far_counts, far_basis, target, half, pick, masked, basis, *rest
):
    *tiles, rows, counts, sems = rest
    own = target.shape[0]
    tile = rows.shape[1]
    pairs = [(far_rows, rows), (far_counts, counts), (far_target, target)]
    pairs += [
        (far_basis.at[:, far], basis.at[:, near])
        for far, near in [(slice(0, own), slice(0, own))] + margin_spans(own, tile)
    ]
    loads = started(pairs, sems)
    loads[0].wait()
    loads[1].wait()
    listed = [
        jnp.where(
            lax.broadcasted_iota(jnp.int32, (1, tile), 1) < counts[0, d], rows[d : d + 1, :], -1
        )
        for d in range(4)
    ]
    row, col = parities()
    ordered = (
        jnp.where(row == 0, listed[1], listed[0]),
        jnp.where(row == 0, listed[0], listed[1]),
        jnp.where(col == 0, listed[2], listed[3]),
        jnp.where(col == 0, listed[3], listed[2]),
    )
    for i, here in enumerate(ordered):
        masked[i : i + 1, :] = here
        down = jnp.transpose(jnp.broadcast_to(here, (tile, tile)))[:, :1]
        pick[i * tile : (i + 1) * tile, :] = (
            lax.broadcasted_iota(jnp.int32, (tile, own), 1) == down
        ).astype(FULL).astype(HALF)
    loads[2].wait()
    half[...] = target[...].astype(HALF)
    picked(pick, half, tiles)
    for load in loads[3:]:
        load.wait()


def picked(pick, half, tiles):
    tile = tiles[0].shape[0]
    for d in range(4):
        tiles[d][...] = product(pick[d * tile : (d + 1) * tile, :], half[...]).astype(HALF)


def spread_kernel(far, masked, spread, matrix, sems):
    own = spread.shape[0]
    tile = masked.shape[1]
    loads = started(matrix_pieces(far, matrix, own, tile), sems)
    for d in range(4):
        wide = jnp.broadcast_to(masked[d : d + 1, :], (own, tile))
        spread[:, d * tile : (d + 1) * tile] = (
            lax.broadcasted_iota(jnp.int32, (own, tile), 0) == wide
        ).astype(FULL).astype(HALF)
    for load in loads:
        load.wait()


def stacked(*parts):
    return jnp.concatenate([part[...] for part in parts], axis=0)


def load_kernel(far, own_like, matrix, sems):
    own = own_like.shape[0]
    tile = (matrix.shape[0] - own) // 4
    for load in started(matrix_pieces(far, matrix, own, tile), sems):
        load.wait()


def own_columns_kernel(matrix, owned, out):
    own = owned.shape[0]
    out[...] = product(matrix[:, :own], owned[...])


def restrict_kernel(basis, owned, g0, g1, g2, g3, *rest):
    out = rest[-1]
    own = owned.shape[0]
    out[...] = (
        product(basis[:, :own], owned[...]) + product(basis[:, own:], stacked(g0, g1, g2, g3))
    ).astype(HALF)


def solve_kernel(matrix, partial, g0, g1, g2, g3, rim, inner):
    own = inner.shape[0]
    ghosts = stacked(g0, g1, g2, g3)
    rim[...] = partial[own:, :] + product(matrix[own:, own:], ghosts)
    inner[...] = partial[:own, :] + product(matrix[:own, own:], ghosts)


def met(place, turn, devices):
    if devices & (devices - 1) == 0:
        return place ^ turn
    return (turn + devices - place) % devices


def meeting(shard, axis, turn, block=1):
    devices = lax.axis_size(axis)
    pairs = [
        (i, met(i // block, turn, devices // block) * block + i % block) for i in range(devices)
    ]
    return shard if all(i == j for i, j in pairs) else lax.ppermute(shard, axis, pairs)


def parts_kernel(groups, across):
    def body(inverse, *refs):
        restricted, parts, gathered = refs[:across], refs[across:-1], refs[-1]
        coarse = inverse.shape[1]
        for turn, piece in enumerate(restricted):
            at = pl.multiple_of(met(lax.axis_index("col"), turn, across) * coarse, coarse)
            gathered[pl.ds(at, coarse), :] = piece[...]
        pair = lax.axis_index("row") // 2
        for turn, part in enumerate(parts):
            other = 2 * met(pair, turn, groups // 2)
            for i in range(2):
                part[i * coarse : (i + 1) * coarse, :] = product(
                    inverse[other + i], gathered[...]
                ).astype(HALF)

    return body


def pair_kernel(*refs):
    *parts, mine, others = refs
    coarse = mine.shape[0]
    total = parts[0][...].astype(FULL)
    for part in parts[1:]:
        total += part[...].astype(FULL)
    odd = lax.rem(lax.axis_index("row"), 2) == 1
    low, high = total[:coarse, :], total[coarse:, :]
    mine[...] = jnp.where(odd, high, low)
    others[...] = jnp.where(odd, low, high).astype(HALF)


def coarse_kernel(mine, theirs, basis, rim, level, *tiles):
    tile = tiles[0].shape[0]
    own = basis.shape[1] - 4 * tile
    level[...] = (mine[...] + theirs[...].astype(FULL)).astype(HALF)
    for d in range(4):
        here = slice(d * tile, (d + 1) * tile)
        there = slice(own + d * tile, own + (d + 1) * tile)
        tiles[d][...] = (rim[here, :] + turned_product(basis[:, there], level[...])).astype(HALF)


def base_kernel(first):
    def body(*refs):
        refs = list(refs)
        before = None if first else refs.pop(0)
        inner, level, basis, spread, r0, r1, out = refs
        own, tile = out.shape[0], r0.shape[0]
        update = (
            inner[...]
            + turned_product(basis[:, :own], level[...])
            + product(spread[:, : 2 * tile], stacked(r0, r1))
        )
        out[...] = DAMPING * update if first else before[...] + DAMPING * update

    return body


def update_kernel(base, pick, spread, r2, r3, after, half, *tiles):
    tile = r2.shape[0]
    after[...] = base[...] + DAMPING * product(spread[:, 2 * tile :], stacked(r2, r3))
    half[...] = after[...].astype(HALF)
    picked(pick, half, tiles)


def last_update_kernel(base, spread, r2, r3, far, after, sems):
    tile = r2.shape[0]
    pieces = sems.shape[0]
    height = after.shape[0] // pieces
    returned = stacked(r2, r3)
    stores = []
    for i in range(pieces):
        at = slice(i * height, (i + 1) * height)
        after[at, :] = base[at, :] + DAMPING * product(spread[at, 2 * tile :], returned)
        stores.append(pltpu.make_async_copy(after.at[at], far.at[at], sems.at[i]))
        stores[-1].start()
    for store in stores:
        store.wait()


def rim_kernel(matrix, partial, g0, g1, g2, g3, *tiles):
    tile = g0.shape[0]
    own = matrix.shape[1] - 4 * tile
    ghosts = stacked(g0, g1, g2, g3)
    for d in range(4):
        at = slice(own + d * tile, own + (d + 1) * tile)
        tiles[d][...] = (partial[at, :] + product(matrix[at, own:], ghosts)).astype(HALF)


def remainder_kernel(target, matrix, partial, g0, g1, g2, g3, spread, r0, r1, out):
    own, tile = target.shape[0], r0.shape[0]
    image = (
        partial[:own, :]
        + product(matrix[:own, own:], stacked(g0, g1, g2, g3))
        + product(spread[:, : 2 * tile], stacked(r0, r1))
    )
    out[...] = target[...] - image


def residual_kernel(remainder, pick, spread, r2, r3, half, *tiles):
    tile = r2.shape[0]
    half[...] = (remainder[...] - product(spread[:, 2 * tile :], stacked(r2, r3))).astype(HALF)
    picked(pick, half, tiles)


def partner(place, exchange):
    odd = place % 2 if isinstance(place, int) else lax.rem(place, 2)
    return place + 1 - 2 * odd if exchange == 0 else place - 1 + 2 * odd


def swapped(shard, axis, exchange):
    rows, columns = lax.axis_size("row"), lax.axis_size("col")

    def other(row, col):
        if axis == "row":
            there = partner(row, exchange), col
            beside = row, partner(col, 0)
        else:
            there = row, partner(col, exchange)
            beside = partner(row, 0), col
        for at in (there, beside):
            if 0 <= at[0] < rows and 0 <= at[1] < columns:
                return at
        return row, col

    places = [(row, col) for row in range(rows) for col in range(columns)]
    ends = [(at, other(*at)) for at in places]
    pairs = [(i * columns + j, k * columns + l) for (i, j), (k, l) in ends]
    return lax.ppermute(shard, ("row", "col"), pairs)


def traded(tiles):
    ways = (("row", 0), ("row", 1), ("col", 1), ("col", 0))
    return [swapped(tile, *way) for tile, way in zip(tiles, ways)]


def per_device(
    right_side, local_operator, local_inverse, coarse_basis, coarse_inverse, send_rows, send_count
):
    target = right_side[0, 0]
    operator = local_operator[0, 0]
    inverse = local_inverse[0, 0]
    basis = jnp.swapaxes(coarse_basis[0, 0], 0, 1)
    rows_list = send_rows[0, 0]
    own, columns = target.shape
    local = operator.shape[0]
    tile = rows_list.shape[1]
    margin = 4 * tile
    coarse = basis.shape[0]
    groups = coarse_inverse.shape[0]
    across = lax.axis_size("col")

    four_tiles = [((tile, columns), HALF)] * 4
    owned_half = ((own, columns), HALF)
    owned_full = ((own, columns), FULL)
    local_full = ((local, columns), FULL)
    target, residual, pick, masked, basis, *tiles = call(
        select_kernel,
        "select",
        [
            owned_full,
            owned_half,
            ((margin, own), HALF),
            (rows_list.shape, jnp.int32),
            (basis.shape, HALF),
        ]
        + four_tiles,
        target,
        rows_list,
        send_count[0],
        basis,
        far=4,
        scratch=(
            pltpu.VMEM(rows_list.shape, jnp.int32),
            pltpu.SMEM((1, 4), jnp.int32),
            pltpu.SemaphoreType.DMA((8,)),
        ),
        flops=2 * margin * own * columns,
    )
    spread = solution = None
    for sweep in range(ITERS):
        first, last = sweep == 0, sweep == ITERS - 1
        if sweep:
            ghosts = traded(tiles)
            (partial,) = call(
                own_columns_kernel,
                "operator_own",
                [local_full],
                operator,
                solution_half,
                flops=2 * local * own * columns,
            )
            tiles = call(
                rim_kernel,
                "operator_rim",
                four_tiles,
                operator,
                partial,
                *ghosts,
                flops=2 * margin * margin * columns,
            )
            returned = traded(tiles)
            (remainder,) = call(
                remainder_kernel,
                "remainder",
                [owned_full],
                target,
                operator,
                partial,
                *ghosts,
                spread,
                *returned[:2],
                flops=2 * own * (margin + 2 * tile) * columns,
            )
            residual, *tiles = call(
                residual_kernel,
                "residual",
                [owned_half] + four_tiles,
                remainder,
                pick,
                spread,
                *returned[2:],
                flops=2 * (margin + 2 * tile) * own * columns,
            )
        ghosts = traded(tiles)
        if first:
            (inverse,) = call(
                load_kernel,
                "inverse_load",
                [(inverse.shape, HALF)],
                inverse,
                residual,
                far=1,
                scratch=(pltpu.SemaphoreType.DMA((MATRIX_PIECES,)),),
            )
        (partial,) = call(
            own_columns_kernel,
            "inverse_own",
            [local_full],
            inverse,
            residual,
            flops=2 * local * own * columns,
        )
        (restricted,) = call(
            restrict_kernel,
            "restrict",
            [((coarse, columns), HALF)],
            basis,
            residual,
            *ghosts,
            *([inverse] if first else []),
            flops=2 * local * coarse * columns,
        )
        restricted = [meeting(restricted, "col", turn) for turn in reversed(range(across))][::-1]
        rim, inner = call(
            solve_kernel,
            "inverse_margin",
            [((margin, columns), FULL), owned_full],
            inverse,
            partial,
            *ghosts,
            flops=2 * local * margin * columns,
        )
        parts = call(
            parts_kernel(groups, across),
            "coarse_part",
            [((2 * coarse, columns), HALF)] * (groups // 2),
            coarse_inverse,
            *restricted,
            scratch=(pltpu.VMEM((across * coarse, columns), HALF),),
            flops=2 * coarse_inverse.size * columns,
        )
        parts = [meeting(parts[turn], "row", turn, 2) for turn in reversed(range(groups // 2))]
        mine, others = call(
            pair_kernel,
            "coarse_pair",
            [((coarse, columns), FULL), ((coarse, columns), HALF)],
            *parts,
        )
        level, *tiles = call(
            coarse_kernel,
            "coarse",
            [((coarse, columns), HALF)] + four_tiles,
            mine,
            swapped(others, "row", 0),
            basis,
            rim,
            flops=2 * coarse * margin * columns,
        )
        if first:
            masked, tiles = lax.optimization_barrier((masked, tuple(tiles)))
            spread, operator = call(
                spread_kernel,
                "spread",
                [((own, margin), HALF), (operator.shape, HALF)],
                operator,
                masked,
                far=1,
                scratch=(pltpu.SemaphoreType.DMA((MATRIX_PIECES,)),),
            )
        returned = traded(tiles)
        (base,) = call(
            base_kernel(first),
            "base",
            [owned_full],
            *([] if first else [solution]),
            inner,
            level,
            basis,
            spread,
            *returned[:2],
            flops=2 * (coarse + 2 * tile) * own * columns,
        )
        if last:
            break
        solution, solution_half, *tiles = call(
            update_kernel,
            "update",
            [owned_full, owned_half] + four_tiles,
            base,
            pick,
            spread,
            *returned[2:],
            flops=2 * (margin + 2 * tile) * own * columns,
        )
    (solution,) = call(
        last_update_kernel,
        "last_update",
        [owned_full],
        base,
        spread,
        *returned[2:],
        away=True,
        scratch=(pltpu.VMEM((own, columns), FULL), pltpu.SemaphoreType.DMA((4,))),
        flops=2 * margin * own * columns,
    )
    return solution[None, None]


def solution(mesh):
    return jax.shard_map(
        per_device,
        mesh=mesh,
        in_specs=(
            P("row", "col", None, None),
            P("row", "col", None, None),
            P("row", "col", None, None),
            P("row", "col", None, None),
            P(None, "col", "row"),
            P("row", "col", None, None),
            P("row", "col", None),
        ),
        out_specs=P("row", "col", None, None),
        check_vma=False,
    )
```

```python
import jax
import jax.numpy as jnp
from jax import lax
from jax.experimental import pallas as pl
from jax.experimental.pallas import tpu as pltpu
from jax.sharding import PartitionSpec as P

ITERS = 3
DAMPING = 0.5
HALF = jnp.bfloat16
FULL = jnp.float32


def product(left, right):
    return jnp.dot(left, right, preferred_element_type=FULL)


def turned_product(left, right):
    return lax.dot_general(left, right, (((0,), (0,)), ((), ())), preferred_element_type=FULL)


def call(body, name, outs, *args, far=0, away=False, scratch=(), flops=0):
    here = pl.BlockSpec(memory_space=pltpu.VMEM)
    there = pl.BlockSpec(memory_space=pltpu.HBM)
    size = sum(a.size * a.dtype.itemsize for a in args)
    distant = [pltpu.with_memory_space_constraint(a, pltpu.HBM) for a in args[:far]]
    near = [pltpu.with_memory_space_constraint(a, pltpu.VMEM) for a in args[far:]]
    return pl.pallas_call(
        body,
        out_shape=tuple((pltpu.HBM if away else pltpu.VMEM)(*out) for out in outs),
        in_specs=[there] * far + [here] * len(near),
        out_specs=tuple(there if away else here for _ in outs),
        scratch_shapes=list(scratch),
        compiler_params=pltpu.CompilerParams(vmem_limit_bytes=24 * 1024 * 1024),
        cost_estimate=pl.CostEstimate(flops=flops, bytes_accessed=size, transcendentals=0),
        name=name,
    )(*distant, *near)


def parities():
    return lax.rem(lax.axis_index("row"), 2), lax.rem(lax.axis_index("col"), 2)


def directions():
    row, col = parities()
    return 1 - row, row, 2 + col, 3 - col


def margin_spans(own, tile):
    return [
        (pl.ds(pl.multiple_of(own + d * tile, tile), tile), slice(own + i * tile, own + (i + 1) * tile))
        for i, d in enumerate(directions())
    ]


def matrix_pieces(far, near, own, tile):
    margins = margin_spans(own, tile)
    half = own // 2
    rows = [(slice(0, half), slice(0, half)), (slice(half, own), slice(half, own))] + margins
    columns = [(slice(0, own), slice(0, own))] + margins
    return [(far.at[fr, fc], near.at[nr, nc]) for fr, nr in rows for fc, nc in columns]


MATRIX_PIECES = 30


def started(pairs, sems):
    loads = [pltpu.make_async_copy(far, near, sems.at[i]) for i, (far, near) in enumerate(pairs)]
    for load in loads:
        load.start()
    return loads


def select_kernel(
    far_target, far_rows, far_counts, far_basis, target, half, pick, masked, basis, *rest
):
    *tiles, rows, counts, sems = rest
    own = target.shape[0]
    tile = rows.shape[1]
    pairs = [(far_rows, rows), (far_counts, counts), (far_target, target)]
    pairs += [
        (far_basis.at[:, far], basis.at[:, near])
        for far, near in [(slice(0, own), slice(0, own))] + margin_spans(own, tile)
    ]
    loads = started(pairs, sems)
    loads[0].wait()
    loads[1].wait()
    listed = [
        jnp.where(
            lax.broadcasted_iota(jnp.int32, (1, tile), 1) < counts[0, d], rows[d : d + 1, :], -1
        )
        for d in range(4)
    ]
    row, col = parities()
    ordered = (
        jnp.where(row == 0, listed[1], listed[0]),
        jnp.where(row == 0, listed[0], listed[1]),
        jnp.where(col == 0, listed[2], listed[3]),
        jnp.where(col == 0, listed[3], listed[2]),
    )
    for i, here in enumerate(ordered):
        masked[i : i + 1, :] = here
        down = jnp.transpose(jnp.broadcast_to(here, (tile, tile)))[:, :1]
        pick[i * tile : (i + 1) * tile, :] = (
            lax.broadcasted_iota(jnp.int32, (tile, own), 1) == down
        ).astype(FULL).astype(HALF)
    loads[2].wait()
    half[...] = target[...].astype(HALF)
    picked(pick, half, tiles)
    for load in loads[3:]:
        load.wait()


def picked(pick, half, tiles):
    tile = tiles[0].shape[0]
    for d in range(4):
        tiles[d][...] = product(pick[d * tile : (d + 1) * tile, :], half[...]).astype(HALF)


def spread_kernel(far, masked, spread, matrix, sems):
    own = spread.shape[0]
    tile = masked.shape[1]
    loads = started(matrix_pieces(far, matrix, own, tile), sems)
    for d in range(4):
        wide = jnp.broadcast_to(masked[d : d + 1, :], (own, tile))
        spread[:, d * tile : (d + 1) * tile] = (
            lax.broadcasted_iota(jnp.int32, (own, tile), 0) == wide
        ).astype(FULL).astype(HALF)
    for load in loads:
        load.wait()


def stacked(*parts):
    return jnp.concatenate([part[...] for part in parts], axis=0)


def load_kernel(far, own_like, matrix, sems):
    own = own_like.shape[0]
    tile = (matrix.shape[0] - own) // 4
    for load in started(matrix_pieces(far, matrix, own, tile), sems):
        load.wait()


def own_columns_kernel(matrix, owned, out):
    own = owned.shape[0]
    out[...] = product(matrix[:, :own], owned[...])


def restrict_kernel(basis, owned, g0, g1, g2, g3, *rest):
    out = rest[-1]
    own = owned.shape[0]
    out[...] = (
        product(basis[:, :own], owned[...]) + product(basis[:, own:], stacked(g0, g1, g2, g3))
    ).astype(HALF)


def solve_kernel(matrix, partial, g0, g1, g2, g3, rim, inner):
    own = inner.shape[0]
    ghosts = stacked(g0, g1, g2, g3)
    rim[...] = partial[own:, :] + product(matrix[own:, own:], ghosts)
    inner[...] = partial[:own, :] + product(matrix[:own, own:], ghosts)


def met(place, turn, devices):
    if devices & (devices - 1) == 0:
        return place ^ turn
    return (turn + devices - place) % devices


def meeting(shard, axis, turn, block=1):
    devices = lax.axis_size(axis)
    pairs = [
        (i, met(i // block, turn, devices // block) * block + i % block) for i in range(devices)
    ]
    return shard if all(i == j for i, j in pairs) else lax.ppermute(shard, axis, pairs)


def parts_kernel(groups, across):
    def body(inverse, *refs):
        restricted, parts, gathered = refs[:across], refs[across:-1], refs[-1]
        coarse = inverse.shape[1]
        for turn, piece in enumerate(restricted):
            at = pl.multiple_of(met(lax.axis_index("col"), turn, across) * coarse, coarse)
            gathered[pl.ds(at, coarse), :] = piece[...]
        pair = lax.axis_index("row") // 2
        for turn, part in enumerate(parts):
            other = 2 * met(pair, turn, groups // 2)
            for i in range(2):
                part[i * coarse : (i + 1) * coarse, :] = product(
                    inverse[other + i], gathered[...]
                ).astype(HALF)

    return body


def pair_kernel(*refs):
    *parts, mine, others = refs
    coarse = mine.shape[0]
    total = parts[0][...].astype(FULL)
    for part in parts[1:]:
        total += part[...].astype(FULL)
    odd = lax.rem(lax.axis_index("row"), 2) == 1
    low, high = total[:coarse, :], total[coarse:, :]
    mine[...] = jnp.where(odd, high, low)
    others[...] = jnp.where(odd, low, high).astype(HALF)


def coarse_kernel(mine, theirs, basis, rim, level, *tiles):
    tile = tiles[0].shape[0]
    own = basis.shape[1] - 4 * tile
    level[...] = (mine[...] + theirs[...].astype(FULL)).astype(HALF)
    for d in range(4):
        here = slice(d * tile, (d + 1) * tile)
        there = slice(own + d * tile, own + (d + 1) * tile)
        tiles[d][...] = (rim[here, :] + turned_product(basis[:, there], level[...])).astype(HALF)


def base_kernel(first):
    def body(*refs):
        refs = list(refs)
        before = None if first else refs.pop(0)
        inner, level, basis, spread, r0, r1, out = refs
        own, tile = out.shape[0], r0.shape[0]
        update = (
            inner[...]
            + turned_product(basis[:, :own], level[...])
            + product(spread[:, : 2 * tile], stacked(r0, r1))
        )
        out[...] = DAMPING * update if first else before[...] + DAMPING * update

    return body


def update_kernel(base, pick, spread, r2, r3, after, half, *tiles):
    tile = r2.shape[0]
    after[...] = base[...] + DAMPING * product(spread[:, 2 * tile :], stacked(r2, r3))
    half[...] = after[...].astype(HALF)
    picked(pick, half, tiles)


def last_update_kernel(base, spread, r2, r3, far, after, sems):
    tile = r2.shape[0]
    pieces = sems.shape[0]
    height = after.shape[0] // pieces
    returned = stacked(r2, r3)
    stores = []
    for i in range(pieces):
        at = slice(i * height, (i + 1) * height)
        after[at, :] = base[at, :] + DAMPING * product(spread[at, 2 * tile :], returned)
        stores.append(pltpu.make_async_copy(after.at[at], far.at[at], sems.at[i]))
        stores[-1].start()
    for store in stores:
        store.wait()


def rim_kernel(matrix, partial, g0, g1, g2, g3, *tiles):
    tile = g0.shape[0]
    own = matrix.shape[1] - 4 * tile
    ghosts = stacked(g0, g1, g2, g3)
    for d in range(4):
        at = slice(own + d * tile, own + (d + 1) * tile)
        tiles[d][...] = (partial[at, :] + product(matrix[at, own:], ghosts)).astype(HALF)


def remainder_kernel(target, matrix, partial, g0, g1, g2, g3, spread, r0, r1, out):
    own, tile = target.shape[0], r0.shape[0]
    image = (
        partial[:own, :]
        + product(matrix[:own, own:], stacked(g0, g1, g2, g3))
        + product(spread[:, : 2 * tile], stacked(r0, r1))
    )
    out[...] = target[...] - image


def residual_kernel(remainder, pick, spread, r2, r3, half, *tiles):
    tile = r2.shape[0]
    half[...] = (remainder[...] - product(spread[:, 2 * tile :], stacked(r2, r3))).astype(HALF)
    picked(pick, half, tiles)


def partner(place, exchange):
    odd = place % 2 if isinstance(place, int) else lax.rem(place, 2)
    return place + 1 - 2 * odd if exchange == 0 else place - 1 + 2 * odd


def swapped(shard, axis, exchange):
    rows, columns = lax.axis_size("row"), lax.axis_size("col")

    def other(row, col):
        if axis == "row":
            there = partner(row, exchange), col
            beside = row, partner(col, 0)
        else:
            there = row, partner(col, exchange)
            beside = (row, there[1] % columns) if columns % 2 == 0 else (partner(row, 0), col)
        for at in (there, beside):
            if 0 <= at[0] < rows and 0 <= at[1] < columns:
                return at
        return row, col

    places = [(row, col) for row in range(rows) for col in range(columns)]
    ends = [(at, other(*at)) for at in places]
    pairs = [(i * columns + j, k * columns + l) for (i, j), (k, l) in ends]
    return lax.ppermute(shard, ("row", "col"), pairs)


def traded(tiles):
    ways = (("row", 0), ("row", 1), ("col", 1), ("col", 0))
    return [swapped(tile, *way) for tile, way in zip(tiles, ways)]


def per_device(
    right_side, local_operator, local_inverse, coarse_basis, coarse_inverse, send_rows, send_count
):
    target = right_side[0, 0]
    operator = local_operator[0, 0]
    inverse = local_inverse[0, 0]
    basis = jnp.swapaxes(coarse_basis[0, 0], 0, 1)
    rows_list = send_rows[0, 0]
    own, columns = target.shape
    local = operator.shape[0]
    tile = rows_list.shape[1]
    margin = 4 * tile
    coarse = basis.shape[0]
    groups = coarse_inverse.shape[0]
    across = lax.axis_size("col")

    four_tiles = [((tile, columns), HALF)] * 4
    owned_half = ((own, columns), HALF)
    owned_full = ((own, columns), FULL)
    local_full = ((local, columns), FULL)
    target, residual, pick, masked, basis, *tiles = call(
        select_kernel,
        "select",
        [
            owned_full,
            owned_half,
            ((margin, own), HALF),
            (rows_list.shape, jnp.int32),
            (basis.shape, HALF),
        ]
        + four_tiles,
        target,
        rows_list,
        send_count[0],
        basis,
        far=4,
        scratch=(
            pltpu.VMEM(rows_list.shape, jnp.int32),
            pltpu.SMEM((1, 4), jnp.int32),
            pltpu.SemaphoreType.DMA((8,)),
        ),
        flops=2 * margin * own * columns,
    )
    spread = solution = None
    for sweep in range(ITERS):
        first, last = sweep == 0, sweep == ITERS - 1
        if sweep:
            ghosts = traded(tiles)
            (partial,) = call(
                own_columns_kernel,
                "operator_own",
                [local_full],
                operator,
                solution_half,
                flops=2 * local * own * columns,
            )
            tiles = call(
                rim_kernel,
                "operator_rim",
                four_tiles,
                operator,
                partial,
                *ghosts,
                flops=2 * margin * margin * columns,
            )
            returned = traded(tiles)
            (remainder,) = call(
                remainder_kernel,
                "remainder",
                [owned_full],
                target,
                operator,
                partial,
                *ghosts,
                spread,
                *returned[:2],
                flops=2 * own * (margin + 2 * tile) * columns,
            )
            residual, *tiles = call(
                residual_kernel,
                "residual",
                [owned_half] + four_tiles,
                remainder,
                pick,
                spread,
                *returned[2:],
                flops=2 * (margin + 2 * tile) * own * columns,
            )
        ghosts = traded(tiles)
        if first:
            (inverse,) = call(
                load_kernel,
                "inverse_load",
                [(inverse.shape, HALF)],
                inverse,
                residual,
                far=1,
                scratch=(pltpu.SemaphoreType.DMA((MATRIX_PIECES,)),),
            )
        (partial,) = call(
            own_columns_kernel,
            "inverse_own",
            [local_full],
            inverse,
            residual,
            flops=2 * local * own * columns,
        )
        (restricted,) = call(
            restrict_kernel,
            "restrict",
            [((coarse, columns), HALF)],
            basis,
            residual,
            *ghosts,
            *([inverse] if first else []),
            flops=2 * local * coarse * columns,
        )
        restricted = [meeting(restricted, "col", turn) for turn in reversed(range(across))][::-1]
        rim, inner = call(
            solve_kernel,
            "inverse_margin",
            [((margin, columns), FULL), owned_full],
            inverse,
            partial,
            *ghosts,
            flops=2 * local * margin * columns,
        )
        parts = call(
            parts_kernel(groups, across),
            "coarse_part",
            [((2 * coarse, columns), HALF)] * (groups // 2),
            coarse_inverse,
            *restricted,
            scratch=(pltpu.VMEM((across * coarse, columns), HALF),),
            flops=2 * coarse_inverse.size * columns,
        )
        parts = [meeting(parts[turn], "row", turn, 2) for turn in reversed(range(groups // 2))]
        mine, others = call(
            pair_kernel,
            "coarse_pair",
            [((coarse, columns), FULL), ((coarse, columns), HALF)],
            *parts,
        )
        level, *tiles = call(
            coarse_kernel,
            "coarse",
            [((coarse, columns), HALF)] + four_tiles,
            mine,
            swapped(others, "row", 0),
            basis,
            rim,
            flops=2 * coarse * margin * columns,
        )
        if first:
            masked, tiles = lax.optimization_barrier((masked, tuple(tiles)))
            spread, operator = call(
                spread_kernel,
                "spread",
                [((own, margin), HALF), (operator.shape, HALF)],
                operator,
                masked,
                far=1,
                scratch=(pltpu.SemaphoreType.DMA((MATRIX_PIECES,)),),
            )
        returned = traded(tiles)
        (base,) = call(
            base_kernel(first),
            "base",
            [owned_full],
            *([] if first else [solution]),
            inner,
            level,
            basis,
            spread,
            *returned[:2],
            flops=2 * (coarse + 2 * tile) * own * columns,
        )
        if last:
            break
        solution, solution_half, *tiles = call(
            update_kernel,
            "update",
            [owned_full, owned_half] + four_tiles,
            base,
            pick,
            spread,
            *returned[2:],
            flops=2 * (margin + 2 * tile) * own * columns,
        )
    (solution,) = call(
        last_update_kernel,
        "last_update",
        [owned_full],
        base,
        spread,
        *returned[2:],
        away=True,
        scratch=(pltpu.VMEM((own, columns), FULL), pltpu.SemaphoreType.DMA((4,))),
        flops=2 * margin * own * columns,
    )
    return solution[None, None]


def solution(mesh):
    return jax.shard_map(
        per_device,
        mesh=mesh,
        in_specs=(
            P("row", "col", None, None),
            P("row", "col", None, None),
            P("row", "col", None, None),
            P("row", "col", None, None),
            P(None, "col", "row"),
            P("row", "col", None, None),
            P("row", "col", None),
        ),
        out_specs=P("row", "col", None, None),
        check_vma=False,
    )
```

```python
import jax
import jax.numpy as jnp
from jax import lax
from jax.experimental import pallas as pl
from jax.experimental.pallas import tpu as pltpu
from jax.sharding import PartitionSpec as P

ITERS = 3
DAMPING = 0.5
HALF = jnp.bfloat16
FULL = jnp.float32


def product(left, right):
    return jnp.dot(left, right, preferred_element_type=FULL)


def turned_product(left, right):
    return lax.dot_general(left, right, (((0,), (0,)), ((), ())), preferred_element_type=FULL)


def call(body, name, outs, *args, far=0, away=False, scratch=(), flops=0):
    here = pl.BlockSpec(memory_space=pltpu.VMEM)
    there = pl.BlockSpec(memory_space=pltpu.HBM)
    size = sum(a.size * a.dtype.itemsize for a in args)
    distant = [pltpu.with_memory_space_constraint(a, pltpu.HBM) for a in args[:far]]
    near = [pltpu.with_memory_space_constraint(a, pltpu.VMEM) for a in args[far:]]
    return pl.pallas_call(
        body,
        out_shape=tuple((pltpu.HBM if away else pltpu.VMEM)(*out) for out in outs),
        in_specs=[there] * far + [here] * len(near),
        out_specs=tuple(there if away else here for _ in outs),
        scratch_shapes=list(scratch),
        compiler_params=pltpu.CompilerParams(vmem_limit_bytes=24 * 1024 * 1024),
        cost_estimate=pl.CostEstimate(flops=flops, bytes_accessed=size, transcendentals=0),
        name=name,
    )(*distant, *near)


def parities():
    return lax.rem(lax.axis_index("row"), 2), lax.rem(lax.axis_index("col"), 2)


def directions():
    row, col = parities()
    return 1 - row, row, 2 + col, 3 - col


def margin_spans(own, tile):
    return [
        (pl.ds(pl.multiple_of(own + d * tile, tile), tile), slice(own + i * tile, own + (i + 1) * tile))
        for i, d in enumerate(directions())
    ]


def matrix_pieces(far, near, own, tile):
    margins = margin_spans(own, tile)
    half = own // 2
    rows = [(slice(0, half), slice(0, half)), (slice(half, own), slice(half, own))] + margins
    columns = [(slice(0, own), slice(0, own))] + margins
    return [(far.at[fr, fc], near.at[nr, nc]) for fr, nr in rows for fc, nc in columns]


MATRIX_PIECES = 30


def started(pairs, sems):
    loads = [pltpu.make_async_copy(far, near, sems.at[i]) for i, (far, near) in enumerate(pairs)]
    for load in loads:
        load.start()
    return loads


def select_kernel(
    far_target, far_rows, far_counts, far_basis, target, half, pick, masked, basis, *rest
):
    *tiles, rows, counts, sems = rest
    own = target.shape[0]
    tile = rows.shape[1]
    pairs = [(far_rows, rows), (far_counts, counts), (far_target, target)]
    pairs += [
        (far_basis.at[:, far], basis.at[:, near])
        for far, near in [(slice(0, own), slice(0, own))] + margin_spans(own, tile)
    ]
    loads = started(pairs, sems)
    loads[0].wait()
    loads[1].wait()
    listed = [
        jnp.where(
            lax.broadcasted_iota(jnp.int32, (1, tile), 1) < counts[0, d], rows[d : d + 1, :], -1
        )
        for d in range(4)
    ]
    row, col = parities()
    ordered = (
        jnp.where(row == 0, listed[1], listed[0]),
        jnp.where(row == 0, listed[0], listed[1]),
        jnp.where(col == 0, listed[2], listed[3]),
        jnp.where(col == 0, listed[3], listed[2]),
    )
    for i, here in enumerate(ordered):
        masked[i : i + 1, :] = here
        down = jnp.transpose(jnp.broadcast_to(here, (tile, tile)))[:, :1]
        pick[i * tile : (i + 1) * tile, :] = (
            lax.broadcasted_iota(jnp.int32, (tile, own), 1) == down
        ).astype(FULL).astype(HALF)
    loads[2].wait()
    half[...] = target[...].astype(HALF)
    picked(pick, half, tiles)
    for load in loads[3:]:
        load.wait()


def picked(pick, half, tiles):
    tile = tiles[0].shape[0]
    for d in range(4):
        tiles[d][...] = product(pick[d * tile : (d + 1) * tile, :], half[...]).astype(HALF)


def spread_kernel(far, masked, spread, matrix, sems):
    own = spread.shape[0]
    tile = masked.shape[1]
    loads = started(matrix_pieces(far, matrix, own, tile), sems)
    for d in range(4):
        wide = jnp.broadcast_to(masked[d : d + 1, :], (own, tile))
        spread[:, d * tile : (d + 1) * tile] = (
            lax.broadcasted_iota(jnp.int32, (own, tile), 0) == wide
        ).astype(FULL).astype(HALF)
    for load in loads:
        load.wait()


def stacked(*parts):
    return jnp.concatenate([part[...] for part in parts], axis=0)


def load_kernel(far, own_like, matrix, sems):
    own = own_like.shape[0]
    tile = (matrix.shape[0] - own) // 4
    for load in started(matrix_pieces(far, matrix, own, tile), sems):
        load.wait()


def own_columns_kernel(matrix, owned, out):
    own = owned.shape[0]
    out[...] = product(matrix[:, :own], owned[...])


def restrict_kernel(basis, owned, g0, g1, g2, g3, *rest):
    out = rest[-1]
    own = owned.shape[0]
    out[...] = (
        product(basis[:, :own], owned[...]) + product(basis[:, own:], stacked(g0, g1, g2, g3))
    ).astype(HALF)


def solve_kernel(matrix, partial, g0, g1, g2, g3, rim, inner):
    own = inner.shape[0]
    ghosts = stacked(g0, g1, g2, g3)
    rim[...] = partial[own:, :] + product(matrix[own:, own:], ghosts)
    inner[...] = partial[:own, :] + product(matrix[:own, own:], ghosts)


def met(place, turn, devices):
    if devices & (devices - 1) == 0:
        return place ^ turn
    return (turn + devices - place) % devices


def meeting(shard, axis, turn, block=1):
    devices = lax.axis_size(axis)
    pairs = [
        (i, met(i // block, turn, devices // block) * block + i % block) for i in range(devices)
    ]
    return shard if all(i == j for i, j in pairs) else lax.ppermute(shard, axis, pairs)


def parts_kernel(groups, across):
    def body(inverse, *refs):
        restricted, (mine, others, gathered) = refs[:across], refs[across:]
        coarse = inverse.shape[1]
        for turn, piece in enumerate(restricted):
            at = pl.multiple_of(met(lax.axis_index("col"), turn, across) * coarse, coarse)
            gathered[pl.ds(at, coarse), :] = piece[...]
        pair, odd = lax.axis_index("row") // 2, lax.rem(lax.axis_index("row"), 2)
        for turn in range(groups // 2):
            low = 2 * met(pair, turn, groups // 2)
            at = slice(turn * coarse, (turn + 1) * coarse)
            mine[at, :] = product(inverse[low + odd], gathered[...])
            others[at, :] = product(inverse[low + 1 - odd], gathered[...]).astype(HALF)

    return body


def pair_kernel(mine, theirs, *parts):
    coarse = parts[0].shape[0]
    for turn, part in enumerate(parts):
        at = slice(turn * coarse, (turn + 1) * coarse)
        part[...] = (mine[at, :] + theirs[at, :].astype(FULL)).astype(part.dtype)


def coarse_kernel(turns):
    def body(*refs):
        parts, (basis, rim, level, *tiles) = refs[:turns], refs[turns:]
        tile = tiles[0].shape[0]
        own = basis.shape[1] - 4 * tile
        total = parts[0][...].astype(FULL)
        for part in parts[1:]:
            total += part[...].astype(FULL)
        level[...] = total.astype(HALF)
        for d in range(4):
            here = slice(d * tile, (d + 1) * tile)
            there = slice(own + d * tile, own + (d + 1) * tile)
            tiles[d][...] = (
                rim[here, :] + turned_product(basis[:, there], level[...])
            ).astype(HALF)

    return body


def base_kernel(first):
    def body(*refs):
        refs = list(refs)
        before = None if first else refs.pop(0)
        inner, level, basis, spread, r0, r1, out = refs
        own, tile = out.shape[0], r0.shape[0]
        update = (
            inner[...]
            + turned_product(basis[:, :own], level[...])
            + product(spread[:, : 2 * tile], stacked(r0, r1))
        )
        out[...] = DAMPING * update if first else before[...] + DAMPING * update

    return body


def update_kernel(base, pick, spread, r2, r3, after, half, *tiles):
    tile = r2.shape[0]
    after[...] = base[...] + DAMPING * product(spread[:, 2 * tile :], stacked(r2, r3))
    half[...] = after[...].astype(HALF)
    picked(pick, half, tiles)


def last_update_kernel(base, spread, r2, r3, far, after, sems):
    tile = r2.shape[0]
    pieces = sems.shape[0]
    height = after.shape[0] // pieces
    returned = stacked(r2, r3)
    stores = []
    for i in range(pieces):
        at = slice(i * height, (i + 1) * height)
        after[at, :] = base[at, :] + DAMPING * product(spread[at, 2 * tile :], returned)
        stores.append(pltpu.make_async_copy(after.at[at], far.at[at], sems.at[i]))
        stores[-1].start()
    for store in stores:
        store.wait()


def rim_kernel(matrix, partial, g0, g1, g2, g3, *tiles):
    tile = g0.shape[0]
    own = matrix.shape[1] - 4 * tile
    ghosts = stacked(g0, g1, g2, g3)
    for d in range(4):
        at = slice(own + d * tile, own + (d + 1) * tile)
        tiles[d][...] = (partial[at, :] + product(matrix[at, own:], ghosts)).astype(HALF)


def remainder_kernel(target, matrix, partial, g0, g1, g2, g3, spread, r0, r1, out):
    own, tile = target.shape[0], r0.shape[0]
    image = (
        partial[:own, :]
        + product(matrix[:own, own:], stacked(g0, g1, g2, g3))
        + product(spread[:, : 2 * tile], stacked(r0, r1))
    )
    out[...] = target[...] - image


def residual_kernel(remainder, pick, spread, r2, r3, half, *tiles):
    tile = r2.shape[0]
    half[...] = (remainder[...] - product(spread[:, 2 * tile :], stacked(r2, r3))).astype(HALF)
    picked(pick, half, tiles)


def partner(place, exchange):
    odd = place % 2 if isinstance(place, int) else lax.rem(place, 2)
    return place + 1 - 2 * odd if exchange == 0 else place - 1 + 2 * odd


def swapped(shard, axis, exchange):
    rows, columns = lax.axis_size("row"), lax.axis_size("col")

    def other(row, col):
        if axis == "row":
            there = partner(row, exchange), col
            beside = row, partner(col, 0)
        else:
            there = row, partner(col, exchange)
            beside = (row, there[1] % columns) if columns % 2 == 0 else (partner(row, 0), col)
        for at in (there, beside):
            if 0 <= at[0] < rows and 0 <= at[1] < columns:
                return at
        return row, col

    places = [(row, col) for row in range(rows) for col in range(columns)]
    ends = [(at, other(*at)) for at in places]
    pairs = [(i * columns + j, k * columns + l) for (i, j), (k, l) in ends]
    return lax.ppermute(shard, ("row", "col"), pairs)


def traded(tiles):
    ways = (("row", 0), ("row", 1), ("col", 1), ("col", 0))
    return [swapped(tile, *way) for tile, way in zip(tiles, ways)]


def per_device(
    right_side, local_operator, local_inverse, coarse_basis, coarse_inverse, send_rows, send_count
):
    target = right_side[0, 0]
    operator = local_operator[0, 0]
    inverse = local_inverse[0, 0]
    basis = jnp.swapaxes(coarse_basis[0, 0], 0, 1)
    rows_list = send_rows[0, 0]
    own, columns = target.shape
    local = operator.shape[0]
    tile = rows_list.shape[1]
    margin = 4 * tile
    coarse = basis.shape[0]
    groups = coarse_inverse.shape[0]
    across = lax.axis_size("col")

    four_tiles = [((tile, columns), HALF)] * 4
    owned_half = ((own, columns), HALF)
    owned_full = ((own, columns), FULL)
    local_full = ((local, columns), FULL)
    target, residual, pick, masked, basis, *tiles = call(
        select_kernel,
        "select",
        [
            owned_full,
            owned_half,
            ((margin, own), HALF),
            (rows_list.shape, jnp.int32),
            (basis.shape, HALF),
        ]
        + four_tiles,
        target,
        rows_list,
        send_count[0],
        basis,
        far=4,
        scratch=(
            pltpu.VMEM(rows_list.shape, jnp.int32),
            pltpu.SMEM((1, 4), jnp.int32),
            pltpu.SemaphoreType.DMA((8,)),
        ),
        flops=2 * margin * own * columns,
    )
    spread = solution = None
    for sweep in range(ITERS):
        first, last = sweep == 0, sweep == ITERS - 1
        if sweep:
            ghosts = traded(tiles)
            (partial,) = call(
                own_columns_kernel,
                "operator_own",
                [local_full],
                operator,
                solution_half,
                flops=2 * local * own * columns,
            )
            tiles = call(
                rim_kernel,
                "operator_rim",
                four_tiles,
                operator,
                partial,
                *ghosts,
                flops=2 * margin * margin * columns,
            )
            returned = traded(tiles)
            (remainder,) = call(
                remainder_kernel,
                "remainder",
                [owned_full],
                target,
                operator,
                partial,
                *ghosts,
                spread,
                *returned[:2],
                flops=2 * own * (margin + 2 * tile) * columns,
            )
            residual, *tiles = call(
                residual_kernel,
                "residual",
                [owned_half] + four_tiles,
                remainder,
                pick,
                spread,
                *returned[2:],
                flops=2 * (margin + 2 * tile) * own * columns,
            )
        ghosts = traded(tiles)
        if first:
            (inverse,) = call(
                load_kernel,
                "inverse_load",
                [(inverse.shape, HALF)],
                inverse,
                residual,
                far=1,
                scratch=(pltpu.SemaphoreType.DMA((MATRIX_PIECES,)),),
            )
        (partial,) = call(
            own_columns_kernel,
            "inverse_own",
            [local_full],
            inverse,
            residual,
            flops=2 * local * own * columns,
        )
        (restricted,) = call(
            restrict_kernel,
            "restrict",
            [((coarse, columns), HALF)],
            basis,
            residual,
            *ghosts,
            *([inverse] if first else []),
            flops=2 * local * coarse * columns,
        )
        restricted = [meeting(restricted, "col", turn) for turn in reversed(range(across))][::-1]
        rim, inner = call(
            solve_kernel,
            "inverse_margin",
            [((margin, columns), FULL), owned_full],
            inverse,
            partial,
            *ghosts,
            flops=2 * local * margin * columns,
        )
        turns = groups // 2
        stack = (turns * coarse, columns)
        mine, others = call(
            parts_kernel(groups, across),
            "coarse_part",
            [(stack, FULL), (stack, HALF)],
            coarse_inverse,
            *restricted,
            scratch=(pltpu.VMEM((across * coarse, columns), HALF),),
            flops=2 * coarse_inverse.size * columns,
        )
        parts = call(
            pair_kernel,
            "coarse_pair",
            [((coarse, columns), FULL)] + [((coarse, columns), HALF)] * (turns - 1),
            mine,
            swapped(others, "row", 0),
        )
        parts = [meeting(parts[turn], "row", turn, 2) for turn in reversed(range(turns))]
        level, *tiles = call(
            coarse_kernel(turns),
            "coarse",
            [((coarse, columns), HALF)] + four_tiles,
            *parts,
            basis,
            rim,
            flops=2 * coarse * margin * columns,
        )
        if first:
            masked, tiles = lax.optimization_barrier((masked, tuple(tiles)))
            spread, operator = call(
                spread_kernel,
                "spread",
                [((own, margin), HALF), (operator.shape, HALF)],
                operator,
                masked,
                far=1,
                scratch=(pltpu.SemaphoreType.DMA((MATRIX_PIECES,)),),
            )
        returned = traded(tiles)
        (base,) = call(
            base_kernel(first),
            "base",
            [owned_full],
            *([] if first else [solution]),
            inner,
            level,
            basis,
            spread,
            *returned[:2],
            flops=2 * (coarse + 2 * tile) * own * columns,
        )
        if last:
            break
        solution, solution_half, *tiles = call(
            update_kernel,
            "update",
            [owned_full, owned_half] + four_tiles,
            base,
            pick,
            spread,
            *returned[2:],
            flops=2 * (margin + 2 * tile) * own * columns,
        )
    (solution,) = call(
        last_update_kernel,
        "last_update",
        [owned_full],
        base,
        spread,
        *returned[2:],
        away=True,
        scratch=(pltpu.VMEM((own, columns), FULL), pltpu.SemaphoreType.DMA((4,))),
        flops=2 * margin * own * columns,
    )
    return solution[None, None]


def solution(mesh):
    return jax.shard_map(
        per_device,
        mesh=mesh,
        in_specs=(
            P("row", "col", None, None),
            P("row", "col", None, None),
            P("row", "col", None, None),
            P("row", "col", None, None),
            P(None, "col", "row"),
            P("row", "col", None, None),
            P("row", "col", None),
        ),
        out_specs=P("row", "col", None, None),
        check_vma=False,
    )
```
